32 devices in a mesh: ta: 4 (over z), gx: 2 (over core), gy: 4 (over y, x).
Axes of the slice: x: 2, y: 2, z: 4, core: 2. Of those that a mesh axis runs over, the one named last changes fastest.
Arguments:
- initial_state: float32 [2, 64, 4096], P(None, 'gx', 'gy'), may hold values from 0 to 1
- feed_rate: float32 [64, 4096], P('gx', 'gy'), may hold values from 0.02 to 0.1
- kill_rate: float32 [64, 4096], P('gx', 'gy'), may hold values from 0.03 to 0.09
Outputs:
- final_state: float32 [4, 2, 64, 4096], P('ta', None, 'gx', 'gy')
The draws below stay inside these ranges and needn't reach their ends.
All inputs are finite; a program needn't handle non-finite values.
Results may differ from the reference program's by a relative error of at most 0.00002.
Values sent between devices are 32-bit elements; how exact they have to be, the bound alone decides.
No kernel may reach another device: no remote copies, remote signals or barrier semaphores. Data moves between devices by JAX's collectives and lax.ppermute only.
A program may use at most 64 MiB of HBM per device.

```python
import math
import jax
import jax.numpy as jnp

TURNS = 2
SLICES = 4
NX = 64
NY = 4096


def level_of(own_key, shape, cuts, low, largest):
    level = 1.0
    for axis_at, shards_of in cuts:
        draws = jax.random.uniform(jax.random.fold_in(jax.random.fold_in(own_key, 6), axis_at), (shards_of,), jnp.float32, low / len(cuts), largest / len(cuts))
        level = level * jnp.repeat(jnp.exp(draws), shape[axis_at] // shards_of).reshape((-1,) + (1,) * (len(shape) - 1 - axis_at))
    return level


def setup_inputs(seed: int = 0) -> dict:
    key_of = jax.random.split(jax.random.key(seed), 4)
    initial_state = jnp.clip(1.0 * jax.random.uniform(key_of[0], (2, NX, NY), jnp.float32) ** level_of(key_of[0], (2, NX, NY), ((1, 2), (2, 4)), -0.2, 0.2), 0.0, 1.0)
    feed_rate = jnp.clip(jnp.exp(math.log(0.1) - 1.609438 * jax.random.uniform(key_of[1], (NX, NY), jnp.float32) ** level_of(key_of[1], (NX, NY), ((0, 2), (1, 4)), -0.2, 0.2)), 0.02, 0.1)
    kill_rate = jnp.clip(jnp.exp(math.log(0.09) - 1.09861235 * jax.random.uniform(key_of[2], (NX, NY), jnp.float32) ** level_of(key_of[2], (NX, NY), ((0, 2), (1, 4)), -0.2, 0.2)), 0.03, 0.09)
    return dict(initial_state=initial_state, feed_rate=feed_rate, kill_rate=kill_rate)


DIFF_U = 0.2
DIFF_V = 0.1
HALF_STEP = 0.5
NODE_WEIGHTS = ((5.0 / 24.0, 1.0 / 3.0, -1.0 / 24.0), (-1.0 / 24.0, 1.0 / 3.0, 5.0 / 24.0))


def neighbours(padded, values_in):
    total = padded[..., 2:, 1:-1] + padded[..., :-2, 1:-1] + padded[..., 1:-1, 2:] + padded[..., 1:-1, :-2]
    return total - 4.0 * values_in


def react_rates(state, laplace_val, feed_rate, kill_rate, lap_scale):
    conc_u = state[:, 0]
    conc_v = state[:, 1]
    lap_u = lap_scale * laplace_val[:, 0]
    lap_v = lap_scale * laplace_val[:, 1]
    react_term = conc_u * conc_v * conc_v
    rate_u = DIFF_U * lap_u - react_term + feed_rate * (1.0 - conc_u)
    rate_v = DIFF_V * lap_v + react_term - (feed_rate + kill_rate) * conc_v
    return jnp.stack([rate_u, rate_v], axis=1)


def restrict(values_in):
    total = values_in[..., 0::2, 0::2] + values_in[..., 1::2, 0::2] + values_in[..., 0::2, 1::2] + values_in[..., 1::2, 1::2]
    return total * 0.25


def prolong(values_in):
    return jnp.repeat(jnp.repeat(values_in, 2, axis=-2), 2, axis=-1)


def integrals(rates_old):
    rows = []
    for weights in NODE_WEIGHTS:
        rows.append(weights[0] * rates_old[0] + weights[1] * rates_old[1] + weights[2] * rates_old[2])
    return jnp.stack(rows)


def fine_sweep(node_vals, slice_start, rhs_fn):
    old_vals = jnp.concatenate([slice_start[None], node_vals[1:]], axis=0)
    rates_old = rhs_fn(old_vals)
    integ = integrals(rates_old)
    second = slice_start + integ[0]
    rates_new = rhs_fn(second[None])[0]
    third = second + HALF_STEP * (rates_new - rates_old[1]) + integ[1]
    return jnp.stack([slice_start, second, third]), integ


def coarse_sweep(start_value, rates_coarse, coarse_integ, rhs_fn):
    rate_first = rhs_fn(start_value[None])[0]
    second = start_value + HALF_STEP * (rate_first - rates_coarse[0]) + coarse_integ[0]
    rate_second = rhs_fn(second[None])[0]
    third = second + HALF_STEP * (rate_second - rates_coarse[1]) + coarse_integ[1]
    return jnp.stack([start_value, second, third])


def padding(state):
    return jnp.pad(state, ((0, 0), (0, 0), (1, 1), (1, 1)))


def reference(initial_state, feed_rate, kill_rate):
    coarse_feed = restrict(feed_rate)
    coarse_kill = restrict(kill_rate)

    def fine_rhs(state):
        return react_rates(state, neighbours(padding(state), state), feed_rate, kill_rate, 1.0)

    def coarse_rhs(state):
        return react_rates(state, neighbours(padding(state), state), coarse_feed, coarse_kill, 0.25)

    coarse_start = restrict(initial_state)
    node_list = [jnp.stack([initial_state, initial_state, initial_state])] * SLICES
    starts = [initial_state] * SLICES
    ends = []
    for sweep_turn in range(TURNS):
        chain_value = coarse_start
        ends = []
        new_nodes = []
        for slice_pos in range(SLICES):
            node_vals, integ = fine_sweep(node_list[slice_pos], starts[slice_pos], fine_rhs)
            coarse_old = restrict(node_vals)
            rates_coarse = coarse_rhs(coarse_old)
            coarse_integ = restrict(integ)
            coarse_vals = coarse_sweep(chain_value, rates_coarse, coarse_integ, coarse_rhs)
            chain_value = coarse_vals[2]
            node_vals = node_vals + prolong(coarse_vals - coarse_old)
            new_nodes.append(node_vals)
            ends.append(node_vals[2])
        node_list = new_nodes
        starts = [initial_state] + ends[:-1]
    return jnp.stack(ends)
```

```python
import functools

import jax
import jax.numpy as jnp
from jax import lax
from jax.experimental import pallas as pl
from jax.experimental.pallas import tpu as pltpu
from jax.sharding import PartitionSpec as P

TURNS = 2

DIFF_U = 0.2
DIFF_V = 0.1
HALF_STEP = 0.5
W0 = (5.0 / 24.0, 1.0 / 3.0, -1.0 / 24.0)
W1 = (-1.0 / 24.0, 1.0 / 3.0, 5.0 / 24.0)
GUARD = 8
F32 = jnp.float32
BF16 = jnp.bfloat16
PHASES = ((0, 0), (0, 1), (1, 0), (1, 1))


def round_up(value, step):
    return -(-value // step) * step


def thirds(value):
    high = value.astype(BF16)
    rest = value - high.astype(F32)
    middle = rest.astype(BF16)
    low = (rest - middle.astype(F32)).astype(BF16)
    return high, middle, low


def permuted(value, matrix):
    rows = value.shape[0]
    parts = jnp.concatenate(thirds(value), axis=0)
    moved = jnp.dot(parts, matrix, preferred_element_type=F32)
    return (moved[2 * rows :] + moved[rows : 2 * rows]) + moved[:rows]


def split_matrix():
    source = lax.broadcasted_iota(jnp.int32, (256, 256), 0)
    target = lax.broadcasted_iota(jnp.int32, (256, 256), 1)
    wanted = jnp.where(target < 128, 2 * target, 2 * target - 255)
    return jnp.where(source == wanted, 1.0, 0.0).astype(BF16)


def merge_matrix():
    source = lax.broadcasted_iota(jnp.int32, (256, 256), 0)
    target = lax.broadcasted_iota(jnp.int32, (256, 256), 1)
    wanted = jnp.where(source < 128, 2 * source, 2 * source - 255)
    return jnp.where(target == wanted, 1.0, 0.0).astype(BF16)


C_X0, C_X1, C_X2, C_END, C_C1, C_Y1, C_NEW, C_NEW1, C_D1, C_D2 = (2 * i for i in range(10))
COARSE_STENCIL = 20 + 2
N_C1B, N_K0, N_K1, N_G0, N_RA, N_RB, N_RE, N_J0, N_J1, N_RF2 = (2 * i for i in range(10))
COARSE_PLAIN = 20
N_FEED, N_KILL = 0, 1


def scratch(rows, lanes):
    guarded = rows + 2 * GUARD
    return [
        pltpu.VMEM((4 * 8, guarded, lanes), F32),
        pltpu.VMEM((3 * 8, rows, lanes), F32),
        pltpu.VMEM((8, rows, lanes), F32),
        pltpu.VMEM((8, rows, lanes), F32),
        pltpu.VMEM((COARSE_STENCIL, guarded, lanes), F32),
        pltpu.VMEM((COARSE_PLAIN, rows, lanes), F32),
        pltpu.VMEM((2, rows, lanes), F32),
        pltpu.VMEM((8, rows, lanes), F32),
        pltpu.VMEM((24, rows, lanes), F32),
    ]


class Level:
    def __init__(self, refs, rows, lanes, mask):
        (self.fine, self.lin, self.coef, self.rest, self.cs, self.cp, self.cc, self.mom, self.tl) = refs
        self.rows, self.lanes, self.mask = rows, lanes, mask
        self.chunks = rows // 8

    def each(self, body):
        if self.chunks <= 4:
            for i in range(self.chunks):
                body(8 * i)
        else:
            pl.loop(0, self.chunks)(lambda i: body(pl.multiple_of(8 * i, 8)))

    def left(self, value):
        return pltpu.roll(value, 1, 1)

    def right(self, value):
        return pltpu.roll(value, self.lanes - 1, 1)

    def scaled(self, value, factor):
        if self.mask is None:
            return factor * value
        return (factor * self.mask) * value

    def at(self, ref, plane, row, shift=0):
        if shift and not isinstance(row, int):
            both = ref[plane, pl.ds(GUARD + row + 4 * (shift - 1), 16), :]
            return both[7:15] if shift < 0 else both[1:9]
        return ref[plane, pl.ds(GUARD + row + shift, 8), :]

    def put(self, ref, plane, row, value):
        ref[plane, pl.ds(GUARD + row, 8), :] = value

    def get(self, ref, plane, row):
        return ref[plane, pl.ds(row, 8), :]

    def set(self, ref, plane, row, value):
        ref[plane, pl.ds(row, 8), :] = value

    def clear_guards(self):
        for ref in (self.fine, self.cs):
            zeros = jnp.zeros((GUARD, self.lanes), F32)
            for plane in range(ref.shape[0]):
                ref[plane, pl.ds(0, GUARD), :] = zeros
                ref[plane, pl.ds(GUARD + self.rows, GUARD), :] = zeros

    def fine_rates(self, base, row):
        state = [[self.at(self.fine, base * 8 + s * 4 + p, row) for p in range(4)] for s in range(2)]
        linear, rates = [], []
        for p, (a, b) in enumerate(PHASES):
            laps = []
            for s in range(2):
                across = state[s][2 * a + 1 - b]
                along = state[s][2 * (1 - a) + b]
                moved = self.at(self.fine, base * 8 + s * 4 + 2 * (1 - a) + b, row, 1 if a else -1)
                side = self.right(across) if b else self.left(across)
                laps.append((along + moved) + (across + side) - 4.0 * state[s][p])
            u, v = state[0][p], state[1][p]
            feed = self.get(self.coef, p, row)
            both = self.get(self.coef, 4 + p, row)
            lin_u = self.scaled(laps[0], DIFF_U) + feed
            lin_v = self.scaled(laps[1], DIFF_V)
            linear.append((lin_u, lin_v))
            rates.append(self.reacted(u, v, lin_u, lin_v, feed, both))
        return state, linear, rates

    def reacted(self, u, v, lin_u, lin_v, feed, both):
        return lin_u - u * (feed + v * v), lin_v + v * (u * v - both)

    def neighbours(self, plane, row, value):
        rows = self.at(self.cs, plane, row, -1) + self.at(self.cs, plane, row, 1)
        return rows + (self.left(value) + self.right(value))

    def coarse_rates(self, first, row):
        u = self.at(self.cs, first, row)
        v = self.at(self.cs, first + 1, row)
        feed = self.get(self.cc, 0, row)
        both = self.get(self.cc, 1, row)
        lap_u = self.neighbours(first, row, u) - 4.0 * u
        lap_v = self.neighbours(first + 1, row, v) - 4.0 * v
        lin_u = self.scaled(lap_u, 0.25 * DIFF_U) + feed
        lin_v = self.scaled(lap_v, 0.25 * DIFF_V)
        return (u, v), self.reacted(u, v, lin_u, lin_v, feed, both)

    def moved_rates(self, first, row, which, base):
        a = self.at(self.cs, first, row)
        b = self.at(self.cs, first + 1, row)
        m_vv, m_uv = self.get(self.mom, 4 * which, row), self.get(self.mom, 4 * which + 1, row)
        m_u, m_v = self.get(self.mom, 4 * which + 2, row), self.get(self.mom, 4 * which + 3, row)
        react = a * (m_vv + b * (2.0 * m_v + b)) + b * (2.0 * m_uv + b * m_u)
        lap_a = self.neighbours(first, row, a) - 4.0 * a
        lap_b = self.neighbours(first + 1, row, b) - 4.0 * b
        feed = self.get(self.cc, 0, row)
        both = self.get(self.cc, 1, row)
        rate_u = self.get(self.cp, base, row) + (self.scaled(lap_a, 0.5 * DIFF_U) - (feed * a + react))
        rate_v = self.get(self.cp, base + 1, row) + (self.scaled(lap_b, 0.5 * DIFF_V) + (react - both * b))
        return rate_u, rate_v

    def block_mean(self, values):
        return 0.25 * ((values[0] + values[1]) + (values[2] + values[3]))

    def run(self, own):
        lv = self
        cs, cp = self.cs, self.cp

        def coefficients(row):
            for k in range(2):
                self.set(self.cc, k, row, self.block_mean([self.get(self.coef, 4 * k + p, row) for p in range(4)]))

        def first_sweep(row):
            state, linear, rates = lv.fine_rates(0, row)
            for s in range(2):
                for p in range(4):
                    lv.set(lv.lin, s * 4 + p, row, linear[p][s])
                    lv.put(lv.fine, 8 + s * 4 + p, row, state[s][p] + HALF_STEP * rates[p][s])
                mean = lv.block_mean([r[s] for r in rates])
                start = lv.block_mean(state[s])
                lv.set(cp, N_RA + s, row, mean)
                lv.put(cs, C_X0 + s, row, start)
                lv.put(cs, C_X1 + s, row, start + HALF_STEP * mean)
                lv.put(cs, C_END + s, row, start + mean)
                lv.put(cs, C_D1 + s, row, jnp.zeros_like(mean))
                lv.put(cs, C_D2 + s, row, jnp.zeros_like(mean))

        def moments(which, state, row):
            u, v = state
            lv.set(lv.mom, 4 * which, row, lv.block_mean([v[p] * v[p] for p in range(4)]))
            lv.set(lv.mom, 4 * which + 1, row, lv.block_mean([u[p] * v[p] for p in range(4)]))
            lv.set(lv.mom, 4 * which + 2, row, lv.block_mean(u))
            lv.set(lv.mom, 4 * which + 3, row, lv.block_mean(v))

        def second_sweep(row):
            state, linear, rates = lv.fine_rates(1, row)
            for s in range(2):
                for p in range(4):
                    lv.set(lv.lin, 8 + s * 4 + p, row, linear[p][s])
                    lv.put(lv.fine, 16 + s * 4 + p, row, state[s][p] + HALF_STEP * rates[p][s])
                mean = lv.block_mean([r[s] for r in rates])
                lv.set(cp, N_RB + s, row, mean)
                lv.put(cs, C_X2 + s, row, lv.at(cs, C_X1 + s, row) + HALF_STEP * mean)
            moments(0, state, row)
            _, g0 = lv.coarse_rates(C_X0, row)
            _, g1 = lv.coarse_rates(C_X1, row)
            for s in range(2):
                integral = HALF_STEP * lv.get(cp, N_RA + s, row)
                lv.set(cp, N_K0 + s, row, integral - HALF_STEP * g0[s])
                lv.set(cp, N_K1 + s, row, integral - HALF_STEP * g1[s])

        def third_sweep(row):
            state, linear, rates = lv.fine_rates(2, row)
            for s in range(2):
                for p in range(4):
                    lv.set(lv.lin, 16 + s * 4 + p, row, linear[p][s])
                mean = lv.block_mean([r[s] for r in rates])
                lv.set(cp, N_RE + s, row, mean)
                lv.put(cs, C_D2 + s, row, lv.at(cs, C_END + s, row) - lv.at(cs, C_X2 + s, row))
            moments(1, state, row)

        def first_slice(row):
            last = lv.moved_rates(C_D2, row, 1, N_RE)
            for s in range(2):
                f0, f1 = lv.get(cp, N_RA + s, row), lv.get(cp, N_RB + s, row)
                total = (W0[0] + W1[0]) * f0 + (W0[1] + W1[1]) * f1 + (W0[2] + W1[2]) * last[s]
                lv.put(cs, C_NEW + s, row, lv.at(cs, C_X0 + s, row) + total)
                lv.set(cp, N_RF2 + s, row, last[s])

        def chain(now, before):
            def stage_1(row):
                value, rate = lv.coarse_rates(C_END, row)
                for s in range(2):
                    half = HALF_STEP * rate[s]
                    lv.set(cp, N_G0 + s, row, half)
                    mid = value[s] + half + lv.get(cp, N_K0 + s, row)
                    lv.put(cs, C_C1 + s, row, mid)
                    lv.put(cs, C_D1 + s, row, mid - lv.at(cs, C_X1 + s, row))

            def stage_2(row):
                value, rate = lv.coarse_rates(C_C1, row)
                for s in range(2):
                    end = value[s] + HALF_STEP * rate[s] + lv.get(cp, N_K1 + s, row)
                    lv.set(cp, N_C1B + s, row, lv.at(cs, C_END + s, row))
                    lv.put(cs, C_END + s, row, end)
                    lv.put(cs, now + s, row, end - lv.at(cs, C_X2 + s, row))

            def stage_3(row):
                mid = lv.moved_rates(C_D1, row, 0, N_RB)
                last = lv.moved_rates(now, row, 1, N_RE)
                value, rate = lv.coarse_rates(C_NEW, row)
                for s in range(2):
                    f0 = lv.get(cp, N_RF2 + s, row)
                    j0 = W0[0] * f0 + W0[1] * mid[s] + W0[2] * last[s]
                    j1 = W1[0] * f0 + W1[1] * mid[s] + W1[2] * last[s]
                    lv.set(cp, N_RF2 + s, row, last[s])
                    lv.set(cp, N_J1 + s, row, j1)
                    lv.put(cs, C_Y1 + s, row, lv.get(cp, N_C1B + s, row) + j0)
                    lv.put(cs, C_NEW1 + s, row, value[s] + HALF_STEP * rate[s] - lv.get(cp, N_G0 + s, row) + j0)

            def stage_4(row):
                _, old = lv.coarse_rates(C_Y1, row)
                value, rate = lv.coarse_rates(C_NEW1, row)
                for s in range(2):
                    change = HALF_STEP * (rate[s] - old[s])
                    lv.put(cs, C_NEW + s, row, value[s] + change + lv.get(cp, N_J1 + s, row))

            for stage in (stage_1, stage_2, stage_3, stage_4):
                lv.each(stage)

        def corrections(starts):
            def body(row):
                for k, first in enumerate(starts):
                    for s in range(2):
                        d = lv.at(cs, first + s, row)
                        ring = [lv.at(cs, first + s, row, -1), lv.at(cs, first + s, row, 1), lv.left(d), lv.right(d)]
                        north, south, west, east = (lv.scaled(x - d, (DIFF_U, DIFF_V)[s]) for x in ring)
                        for p, (a, b) in enumerate(PHASES):
                            lv.set(lv.tl, k * 8 + s * 4 + p, row, (south if a else north) + (east if b else west))

            return body

        lv.clear_guards()
        lv.each(coefficients)
        lv.each(first_sweep)
        lv.each(second_sweep)
        lv.each(third_sweep)
        lv.each(first_slice)

        def one_slice(n, carry):
            even = lax.rem(n, 2) == 0
            pl.when(even)(lambda: chain(C_D2, C_D2 + 2))
            pl.when(jnp.logical_not(even))(lambda: chain(C_D2 + 2, C_D2))
            return carry

        lax.fori_loop(1, own + 1, one_slice, 0)

        first = own == 0
        even = lax.rem(own, 2) == 0
        now = jnp.where(even, C_D2, C_D2 + 2)
        before = jnp.where(first, C_D1, jnp.where(even, C_D2 + 2, C_D2))
        origin = jnp.where(first, 0, 2)
        lv.each(corrections((before, C_D1, now)))

        def own_nodes(row):
            for p in range(4):
                for t in range(0, lv.lanes, 128):
                    lane = pl.ds(t, 128)
                    high = pl.ds(GUARD + row, 8)
                    low = pl.ds(row, 8)
                    feed, both = lv.coef[p, low, lane], lv.coef[4 + p, low, lane]
                    rates, start = [], None
                    for k, (base, d) in enumerate(((origin, before), (1, C_D1), (2, now))):
                        pair = [lv.fine[base * 8 + s * 4 + p, high, lane] + cs[d + s, high, lane] for s in range(2)]
                        lin = [lv.lin[base * 8 + s * 4 + p, low, lane] + lv.tl[k * 8 + s * 4 + p, low, lane] for s in range(2)]
                        rates.append(lv.reacted(pair[0], pair[1], lin[0], lin[1], feed, both))
                        start = pair if k == 0 else start
                    for s in range(2):
                        f0, f1, f2 = (r[s] for r in rates)
                        second = start[s] + (W0[0] * f0 + W0[1] * f1 + W0[2] * f2)
                        lv.fine[24 + s * 4 + p, high, lane] = second
                        lv.rest[s * 4 + p, low, lane] = second + (W1[0] * f0 + (W1[1] - HALF_STEP) * f1 + W1[2] * f2)

        lv.each(own_nodes)

        def last_node(row):
            _, _, rates = lv.fine_rates(3, row)
            for s in range(2):
                ends = [lv.get(lv.rest, s * 4 + p, row) + HALF_STEP * rates[p][s] for p in range(4)]
                fix = lv.at(cs, C_NEW + s, row) - lv.block_mean(ends)
                for p in range(4):
                    lv.set(lv.rest, s * 4 + p, row, ends[p] + fix)

        lv.each(last_node)


def load_planes(level, sources, blocks, columns):
    matrix = split_matrix()
    for block in range(blocks):
        lane = pl.ds(128 * block, 128)
        for read, first in sources:
            values = [read(plane, block) for plane in range(4)]
            rows = values[0].shape[0]
            moved = permuted(jnp.concatenate(values, axis=0), matrix)
            columns[0], columns[1] = moved[:, :128], moved[:, 128:]
            half = rows // 2
            for plane in range(4):
                for a in range(2):
                    for b in range(2):
                        value = columns[b, pl.ds(plane * rows + a, half, stride=2), :]
                        p = 2 * a + b
                        if plane < 2:
                            level.fine[plane * 4 + p, pl.ds(GUARD + first, half), lane] = value
                        elif plane == 2:
                            level.coef[p, pl.ds(first, half), lane] = value
                        else:
                            level.coef[4 + p, pl.ds(first, half), lane] = value + level.coef[p, pl.ds(first, half), lane]


def merged(level, first, rows, block, matrix, columns):
    half = rows // 2
    groups = []
    lane = pl.ds(128 * block, 128)
    for s in range(2):
        for a in range(2):
            pair = [level.rest[s * 4 + 2 * a + b, pl.ds(first, half), lane] for b in range(2)]
            groups.append(jnp.concatenate(pair, axis=1))
    natural = permuted(jnp.concatenate(groups, axis=0), matrix)
    for s in range(2):
        for a in range(2):
            at = (2 * s + a) * half
            for b in range(2):
                columns[b, pl.ds(s * rows + a, half, stride=2), :] = natural[at : at + half, 128 * b : 128 * b + 128]
    return [[columns[b, pl.ds(s * rows, rows), :] for b in range(2)] for s in range(2)]


def own_first(rows):
    return pl.multiple_of(lax.axis_index("gx") * (rows // 2), rows // 2)


def source_list(refs, rows, parts):
    half = rows // 2
    if parts == 2:
        mine = own_first(rows)
        count = len(refs) // 2
        return [(refs[:count], mine), (refs[count:], pl.multiple_of(half - mine, half))]
    return [(tuple(ref.at[g] for ref in refs), g * half) for g in range(parts)]


def interior_kernel(parts, rows, columns_in, *refs):
    count = 6 if parts == 2 else 3
    ins, out, work = refs[:count], refs[count], refs[count + 1 :]
    level = Level(work[:-1], parts * rows // 2, columns_in // 2, None)

    def reader(three):
        state, feed, kill = three

        def read(plane, block):
            lane = pl.ds(256 * block, 256)
            return state[plane, :, lane] if plane < 2 else (feed, kill)[plane - 2][:, lane]

        return read

    sources = [(reader(three), first) for three, first in source_list(ins, rows, parts)]
    load_planes(level, sources, columns_in // 256, work[-1])
    level.run(lax.axis_index("ta"))
    matrix = merge_matrix()
    for block in range(columns_in // 256):
        natural = merged(level, own_first(rows), rows, block, matrix, work[-1])
        for s in range(2):
            for b in range(2):
                out[s, :, pl.ds(256 * block + 128 * b, 128)] = natural[s][b]


def border_kernel(parts, rows, halo, depth, width, *refs):
    count = 16 if parts == 2 else 8
    ins, done, out, work = refs[:count], refs[count], refs[count + 1], refs[count + 2 :]
    own_cols = width // 2 - halo
    lanes = width // 2
    index, size = lax.axis_index("gy"), lax.axis_size("gy")
    even = lax.rem(index, 2) == 0
    at = lax.broadcasted_iota(jnp.int32, (1, lanes), 1)
    outside = ((at < halo // 2) & (index == 0)) | ((at >= lanes - halo // 2) & (index == size - 1))
    level = Level(work[:-1], parts * rows // 2, lanes, jnp.where(outside, 0.0, 1.0))

    def reader(eight):
        state_l, feed_l, kill_l, state_r, feed_r, kill_r, from_a, from_b = eight

        def read(plane, block):
            pick = (lambda s, f, k: s[plane] if plane < 2 else (f, k)[plane - 2][...])
            low = jnp.where(even, from_b[:, halo * plane : halo * plane + halo], from_a[:, halo * plane : halo * plane + halo])
            high = jnp.where(even, from_a[:, halo * plane : halo * plane + halo], from_b[:, halo * plane : halo * plane + halo])
            left = pick(state_l, feed_l, kill_l)[:, :own_cols]
            right = pick(state_r, feed_r, kill_r)
            right = right[:, right.shape[1] - own_cols :]
            whole = jnp.concatenate([low, left, right, high], axis=1)
            return whole[:, 256 * block : 256 * block + 256]

        return read

    sources = [(reader(eight), first) for eight, first in source_list(ins, rows, parts)]
    load_planes(level, sources, width // 256, work[-1])
    level.run(lax.axis_index("ta"))
    matrix = merge_matrix()
    total = out.shape[-1]
    patch = 2 * depth
    out[0] = done[...]
    pieces = [merged(level, own_first(rows), rows, block, matrix, work[-1]) for block in range(width // 256)]
    tile = round_up(patch, 128)
    for s in range(2):
        whole = jnp.concatenate([part for piece in pieces for part in piece[s]], axis=1)
        low = whole[:, halo : halo + patch]
        high = whole[:, width - halo - patch : width - halo]
        old = out[0, s, :, pl.ds(0, tile)]
        out[0, s, :, pl.ds(0, tile)] = jnp.concatenate([low, old[:, patch:]], axis=1)
        old = out[0, s, :, pl.ds(total - tile, tile)]
        out[0, s, :, pl.ds(total - tile, tile)] = jnp.concatenate([old[:, : tile - patch], high], axis=1)


def pack_kernel(halo, state, feed, kill, to_a, to_b):
    planes = [state[0], state[1], feed[...], kill[...]]
    total = feed.shape[1]
    left = jnp.concatenate([x[:, :halo] for x in planes], axis=1)
    right = jnp.concatenate([x[:, total - halo :] for x in planes], axis=1)
    even = lax.rem(lax.axis_index("gy"), 2) == 0
    to_a[...] = jnp.where(even, right, left)
    to_b[...] = jnp.where(even, left, right)


def both_ways(pairs):
    return [pair for low, high in pairs for pair in ((low, high), (high, low))]


VMEM = pl.BlockSpec(memory_space=pltpu.VMEM)
PARAMS = pltpu.CompilerParams(vmem_limit_bytes=56 * 2**20)


def per_device(initial_state, feed_rate, kill_rate):
    slices, parts, blocks = (lax.axis_size(axis) for axis in ("ta", "gx", "gy"))
    _, rows, columns = initial_state.shape
    depth = 2 * (2 * slices + 2)
    halo = round_up(depth, 32)
    width = round_up(2 * halo + 4 * depth, 256)
    edge = round_up(width // 2 - halo, 128)

    def across(value):
        if parts == 2:
            return [value, lax.ppermute(value, "gx", [(0, 1), (1, 0)])]
        return [lax.all_gather(value, "gx")]

    def joined(groups):
        return [value for part in zip(*groups) for value in part]

    to_a, to_b = pl.pallas_call(
        functools.partial(pack_kernel, halo),
        out_shape=[jax.ShapeDtypeStruct((rows, 4 * halo), F32)] * 2,
        in_specs=[VMEM] * 3,
        out_specs=[VMEM] * 2,
        name="pack",
    )(initial_state, feed_rate, kill_rate)
    fields = [across(value) for value in (initial_state, feed_rate, kill_rate)]
    from_b = lax.ppermute(to_b, "gy", both_ways([(i, i + 1) for i in range(1, blocks - 1, 2)]))
    from_a = lax.ppermute(to_a, "gy", both_ways([(i, i + 1) for i in range(0, blocks - 1, 2)]))
    whole_rows = parts * rows // 2
    inner = pl.pallas_call(
        functools.partial(interior_kernel, parts, rows, columns),
        out_shape=jax.ShapeDtypeStruct((2, rows, columns), F32),
        in_specs=[VMEM] * (3 * len(fields[0])),
        out_specs=VMEM,
        scratch_shapes=scratch(whole_rows, columns // 2) + [pltpu.VMEM((2, 4 * rows, 128), F32)],
        compiler_params=PARAMS,
        name="interior",
    )(*joined(fields))
    strips = [across(value) for value in (from_a, from_b)]
    edges = [[value[..., :edge] for value in field] for field in fields]
    edges += [[value[..., columns - edge :] for value in field] for field in fields]
    return pl.pallas_call(
        functools.partial(border_kernel, parts, rows, halo, depth, width),
        out_shape=jax.ShapeDtypeStruct((1, 2, rows, columns), F32),
        in_specs=[VMEM] * (8 * len(fields[0]) + 1),
        out_specs=VMEM,
        scratch_shapes=scratch(whole_rows, width // 2) + [pltpu.VMEM((2, 4 * rows, 128), F32)],
        compiler_params=PARAMS,
        name="border",
    )(*joined(edges + strips), inner)


def solution(mesh):
    placed = (P(None, "gx", "gy"), P("gx", "gy"), P("gx", "gy"))
    return jax.shard_map(
        per_device, mesh=mesh, in_specs=placed, out_specs=P("ta", None, "gx", "gy"), check_vma=False
    )
```

```python
import functools
import math

import jax
import jax.numpy as jnp
from jax import lax
from jax.experimental import pallas as pl
from jax.experimental.pallas import tpu as pltpu
from jax.sharding import PartitionSpec as P

TURNS = 2

DIFF_U = 0.2
DIFF_V = 0.1
HALF_STEP = 0.5
W0 = (5.0 / 24.0, 1.0 / 3.0, -1.0 / 24.0)
W1 = (-1.0 / 24.0, 1.0 / 3.0, 5.0 / 24.0)
GUARD = 8
F32 = jnp.float32
BF16 = jnp.bfloat16
PHASES = ((0, 0), (0, 1), (1, 0), (1, 1))


def round_up(value, step):
    return -(-value // step) * step


def thirds(value):
    high = value.astype(BF16)
    rest = value - high.astype(F32)
    middle = rest.astype(BF16)
    low = (rest - middle.astype(F32)).astype(BF16)
    return high, middle, low


def permuted(value, matrix):
    rows = value.shape[0]
    parts = jnp.concatenate(thirds(value), axis=0)
    moved = jnp.dot(parts, matrix, preferred_element_type=F32)
    return (moved[2 * rows :] + moved[rows : 2 * rows]) + moved[:rows]


def group_matrix(tiles, inverse):
    group = 128 // tiles
    natural = lax.broadcasted_iota(jnp.int32, (256, 256), 1 if inverse else 0)
    grouped = lax.broadcasted_iota(jnp.int32, (256, 256), 0 if inverse else 1)
    wanted = 2 * tiles * (grouped % group) + 2 * ((grouped % 128) // group) + grouped // 128
    return jnp.where(natural == wanted, 1.0, 0.0).astype(BF16)


def exchanged(tiles, slot):
    count = len(tiles)
    if count == 1:
        return tiles
    group = 128 // count
    turned = [pltpu.roll(tile, k * group, 1) if k else tile for k, tile in enumerate(tiles)]
    results = []
    for q in range(count):
        value = turned[(count - q) % count]
        for at in range(1, count):
            value = jnp.where(slot == at, turned[(at - q) % count], value)
        results.append(pltpu.roll(value, (count - q) * group, 1) if q else value)
    return results


def slots(tiles):
    return lax.broadcasted_iota(jnp.int32, (1, 128), 1) // (128 // tiles)


C_X0, C_X1, C_X2, C_END, C_C1, C_NEW, C_E1, C_D1, C_D2 = (2 * i for i in range(9))
COARSE_STENCIL = 20
N_LAST, N_K0, N_K1, N_G0, N_RA, N_RB, N_RE, N_F1, N_RF2 = (2 * i for i in range(9))
COARSE_PLAIN = 18


def scratch(rows, lanes):
    guarded = rows + 2 * GUARD
    return [
        pltpu.VMEM((4 * 8, guarded, lanes), F32),
        pltpu.VMEM((3 * 8, rows, lanes), F32),
        pltpu.VMEM((8, rows, lanes), F32),
        pltpu.VMEM((8, rows, lanes), F32),
        pltpu.VMEM((COARSE_STENCIL, guarded, lanes), F32),
        pltpu.VMEM((COARSE_PLAIN, rows, lanes), F32),
        pltpu.VMEM((2, rows, lanes), F32),
        pltpu.VMEM((8, rows, lanes), F32),
        pltpu.VMEM((24, rows, lanes), F32),
    ]


class Level:
    def __init__(self, refs, rows, lanes, mask):
        (self.fine, self.lin, self.coef, self.rest, self.cs, self.cp, self.cc, self.mom, self.tl) = refs
        self.rows, self.lanes, self.mask = rows, lanes, mask
        self.chunks = rows // 8

    def each(self, body):
        if self.chunks <= 4:
            for i in range(self.chunks):
                body(8 * i)
        else:
            pl.loop(0, self.chunks)(lambda i: body(pl.multiple_of(8 * i, 8)))

    def left(self, value):
        if self.lanes == 128:
            return pltpu.roll(value, 1, 1)
        return jnp.concatenate([pltpu.roll(value[:, -128:], 1, 1), value[:, :-128]], axis=1)

    def right(self, value):
        if self.lanes == 128:
            return pltpu.roll(value, 127, 1)
        return jnp.concatenate([value[:, 128:], pltpu.roll(value[:, :128], 127, 1)], axis=1)

    def scaled(self, value, factor):
        if self.mask is None:
            return factor * value
        return (factor * self.mask) * value

    def at(self, ref, plane, row, shift=0):
        return ref[plane, pl.ds(GUARD + row + 8 * shift, 8), :]

    def put(self, ref, plane, row, value, lane=slice(None)):
        ref[plane, pl.ds(GUARD + row, 8), lane] = value
        sublane = lax.broadcasted_iota(jnp.int32, (8, 1), 0)
        last = self.rows - 8

        def top():
            ref[plane, pl.ds(0, 8), lane] = jnp.where(sublane == 0, 0.0, pltpu.roll(value, 1, 0))

        def bottom():
            ref[plane, pl.ds(GUARD + self.rows, 8), lane] = jnp.where(sublane == 7, 0.0, pltpu.roll(value, 7, 0))

        for edge, fill in ((last, top), (0, bottom)):
            if not isinstance(row, int):
                pl.when(row == edge)(fill)
            elif row == edge:
                fill()

    def get(self, ref, plane, row):
        return ref[plane, pl.ds(row, 8), :]

    def set(self, ref, plane, row, value):
        ref[plane, pl.ds(row, 8), :] = value

    def fine_rates(self, base, row):
        state = [[self.at(self.fine, base * 8 + s * 4 + p, row) for p in range(4)] for s in range(2)]
        linear, rates = [], []
        for p, (a, b) in enumerate(PHASES):
            laps = []
            for s in range(2):
                across = state[s][2 * a + 1 - b]
                along = state[s][2 * (1 - a) + b]
                moved = self.at(self.fine, base * 8 + s * 4 + 2 * (1 - a) + b, row, 1 if a else -1)
                side = self.right(across) if b else self.left(across)
                laps.append((along + moved) + (across + side) - 4.0 * state[s][p])
            u, v = state[0][p], state[1][p]
            feed = self.get(self.coef, p, row)
            both = self.get(self.coef, 4 + p, row)
            lin_u = self.scaled(laps[0], DIFF_U) + feed
            lin_v = self.scaled(laps[1], DIFF_V)
            linear.append((lin_u, lin_v))
            rates.append(self.reacted(u, v, lin_u, lin_v, feed, both))
        return state, linear, rates

    def reacted(self, u, v, lin_u, lin_v, feed, both):
        return lin_u - u * (feed + v * v), lin_v + v * (u * v - both)

    def neighbours(self, plane, row, value):
        rows = self.at(self.cs, plane, row, -1) + self.at(self.cs, plane, row, 1)
        return rows + (self.left(value) + self.right(value))

    def laplacians(self, first, row):
        pair = [self.at(self.cs, first + s, row) for s in range(2)]
        return pair, [self.neighbours(first + s, row, pair[s]) - 4.0 * pair[s] for s in range(2)]

    def coarse_rates(self, first, row):
        (u, v), laps = self.laplacians(first, row)
        scaled = [self.scaled(laps[s], 0.25 * (DIFF_U, DIFF_V)[s]) for s in range(2)]
        feed, both = self.get(self.cc, 0, row), self.get(self.cc, 1, row)
        return (u, v), scaled, self.reacted(u, v, scaled[0] + feed, scaled[1], feed, both)

    def moved_rates(self, shift, scaled, which, base, row):
        a, b = shift
        m_vv, m_uv, m_u, m_v = (self.get(self.mom, 4 * which + k, row) for k in range(4))
        react = a * (m_vv + b * (2.0 * m_v + b)) + b * (2.0 * m_uv + b * m_u)
        feed, both = self.get(self.cc, 0, row), self.get(self.cc, 1, row)
        rate_u = (self.get(self.cp, base, row) + 2.0 * scaled[0]) - (feed * a + react)
        rate_v = (self.get(self.cp, base + 1, row) + 2.0 * scaled[1]) + (react - both * b)
        return rate_u, rate_v

    def block_mean(self, values):
        return 0.25 * ((values[0] + values[1]) + (values[2] + values[3]))

    def run(self, own):
        lv = self
        cs, cp = self.cs, self.cp

        def first_sweep(row):
            for k in range(2):
                lv.set(lv.cc, k, row, lv.block_mean([lv.get(lv.coef, 4 * k + p, row) for p in range(4)]))
            state, linear, rates = lv.fine_rates(0, row)
            for s in range(2):
                for p in range(4):
                    lv.set(lv.lin, s * 4 + p, row, linear[p][s])
                    lv.put(lv.fine, 8 + s * 4 + p, row, state[s][p] + HALF_STEP * rates[p][s])
                mean = lv.block_mean([r[s] for r in rates])
                start = lv.block_mean(state[s])
                lv.set(cp, N_RA + s, row, mean)
                lv.put(cs, C_X0 + s, row, start)
                lv.put(cs, C_X1 + s, row, start + HALF_STEP * mean)
                lv.put(cs, C_END + s, row, start + mean)
                lv.put(cs, C_D1 + s, row, jnp.zeros_like(mean))

        def moments(which, state, row):
            u, v = state
            lv.set(lv.mom, 4 * which, row, lv.block_mean([v[p] * v[p] for p in range(4)]))
            lv.set(lv.mom, 4 * which + 1, row, lv.block_mean([u[p] * v[p] for p in range(4)]))
            lv.set(lv.mom, 4 * which + 2, row, lv.block_mean(u))
            lv.set(lv.mom, 4 * which + 3, row, lv.block_mean(v))

        def second_sweep(row):
            state, linear, rates = lv.fine_rates(1, row)
            _, _, g0 = lv.coarse_rates(C_X0, row)
            first, scaled, g1 = lv.coarse_rates(C_X1, row)
            for s in range(2):
                for p in range(4):
                    lv.set(lv.lin, 8 + s * 4 + p, row, linear[p][s])
                    lv.put(lv.fine, 16 + s * 4 + p, row, state[s][p] + HALF_STEP * rates[p][s])
                mean = lv.block_mean([r[s] for r in rates])
                lv.set(cp, N_F1 + s, row, mean)
                lv.set(cp, N_RB + s, row, mean - 2.0 * scaled[s])
                lv.put(cs, C_X2 + s, row, first[s] + HALF_STEP * mean)
                integral = HALF_STEP * lv.get(cp, N_RA + s, row)
                lv.set(cp, N_K0 + s, row, integral - HALF_STEP * g0[s])
                lv.set(cp, N_K1 + s, row, integral - HALF_STEP * g1[s])
            moments(0, state, row)

        def third_sweep(row):
            state, linear, rates = lv.fine_rates(2, row)
            for s in range(2):
                for p in range(4):
                    lv.set(lv.lin, 16 + s * 4 + p, row, linear[p][s])
            moments(1, state, row)
            second, laps = lv.laplacians(C_X2, row)
            for s in range(2):
                mean = lv.block_mean([r[s] for r in rates])
                lv.set(cp, N_RE + s, row, mean - lv.scaled(laps[s], 0.5 * (DIFF_U, DIFF_V)[s]))
            end, last = slice_end(C_D2, row)
            for s in range(2):
                j0, j1 = integrals(lv.get(cp, N_RA + s, row), lv.get(cp, N_F1 + s, row), last[s])
                lv.put(cs, C_NEW + s, row, lv.at(cs, C_X0 + s, row) + (j0 + j1))

        def integrals(f0, f1, f2):
            middle = W0[1] * f1
            return middle + (W0[0] * f0 + W0[2] * f2), middle + (W1[0] * f0 + W1[2] * f2)

        def slice_end(now, row):
            end, scaled, rate = lv.coarse_rates(C_END, row)
            shift = [end[s] - lv.at(cs, C_X2 + s, row) for s in range(2)]
            last = lv.moved_rates(shift, scaled, 1, N_RE, row)
            for s in range(2):
                half = HALF_STEP * rate[s]
                lv.set(cp, N_G0 + s, row, half)
                lv.put(cs, C_C1 + s, row, end[s] + half + lv.get(cp, N_K0 + s, row))
                lv.put(cs, now + s, row, shift[s])
                lv.set(cp, N_RF2 + s, row, last[s])
            return end, last

        def middle_nodes(row):
            mid, scaled, rate = lv.coarse_rates(C_C1, row)
            new, _, new_rate = lv.coarse_rates(C_NEW, row)
            shift = [mid[s] - lv.at(cs, C_X1 + s, row) for s in range(2)]
            f1 = lv.moved_rates(shift, scaled, 0, N_RB, row)
            for s in range(2):
                old = lv.at(cs, C_END + s, row)
                lv.set(cp, N_LAST + s, row, old)
                lv.set(cp, N_F1 + s, row, f1[s])
                lv.put(cs, C_D1 + s, row, shift[s])
                lv.put(cs, C_END + s, row, mid[s] + HALF_STEP * rate[s] + lv.get(cp, N_K1 + s, row))
                change = HALF_STEP * new_rate[s] - lv.get(cp, N_G0 + s, row)
                lv.put(cs, C_E1 + s, row, (new[s] - old) + change)

        def end_nodes(now):
            def body(row):
                before = [lv.get(cp, N_RF2 + s, row) for s in range(2)]
                _, last = slice_end(now, row)
                change, laps = lv.laplacians(C_E1, row)
                old, new, j1s = [], [], []
                for s in range(2):
                    j0, j1 = integrals(before[s], lv.get(cp, N_F1 + s, row), last[s])
                    old.append(lv.get(cp, N_LAST + s, row) + j0)
                    new.append(old[s] + change[s])
                    j1s.append(j1)
                feed, both = lv.get(lv.cc, 0, row), lv.get(lv.cc, 1, row)
                lin = [lv.scaled(laps[s], 0.25 * (DIFF_U, DIFF_V)[s]) for s in range(2)]
                rate_new = lv.reacted(new[0], new[1], lin[0], lin[1], feed, both)
                rate_old = lv.reacted(old[0], old[1], 0.0, 0.0, feed, both)
                for s in range(2):
                    total = new[s] + j1s[s] + HALF_STEP * (rate_new[s] - rate_old[s])
                    lv.put(cs, C_NEW + s, row, total)

            return body

        def corrections(starts):
            def body(row):
                for k, first in enumerate(starts):
                    for s in range(2):
                        d = lv.at(cs, first + s, row)
                        ring = [lv.at(cs, first + s, row, -1), lv.at(cs, first + s, row, 1), lv.left(d), lv.right(d)]
                        north, south, west, east = (lv.scaled(x - d, (DIFF_U, DIFF_V)[s]) for x in ring)
                        for p, (a, b) in enumerate(PHASES):
                            lv.set(lv.tl, k * 8 + s * 4 + p, row, (south if a else north) + (east if b else west))

            return body

        lv.each(first_sweep)
        lv.each(second_sweep)
        lv.each(third_sweep)

        def one_slice(n, carry):
            lv.each(middle_nodes)
            lv.each(end_nodes(C_D2 + 2 * lax.rem(n, 2)))
            return carry

        lax.fori_loop(1, own + 1, one_slice, 0)

        first = own == 0
        now = C_D2 + 2 * lax.rem(own, 2)
        before = jnp.where(first, C_D1, 2 * C_D2 + 2 - now)
        origin = jnp.where(first, 0, 2)
        lv.each(corrections((before, C_D1, now)))

        def own_nodes(row):
            for p in range(4):
                for t in range(0, lv.lanes, 128):
                    lane = pl.ds(t, 128)
                    high = pl.ds(GUARD + row, 8)
                    low = pl.ds(row, 8)
                    feed, both = lv.coef[p, low, lane], lv.coef[4 + p, low, lane]
                    rates, start = [], None
                    for k, (base, d) in enumerate(((origin, before), (1, C_D1), (2, now))):
                        pair = [lv.fine[base * 8 + s * 4 + p, high, lane] + cs[d + s, high, lane] for s in range(2)]
                        lin = [lv.lin[base * 8 + s * 4 + p, low, lane] + lv.tl[k * 8 + s * 4 + p, low, lane] for s in range(2)]
                        rates.append(lv.reacted(pair[0], pair[1], lin[0], lin[1], feed, both))
                        start = pair if k == 0 else start
                    for s in range(2):
                        f0, f1, f2 = (r[s] for r in rates)
                        second = start[s] + (W0[0] * f0 + W0[1] * f1 + W0[2] * f2)
                        lv.put(lv.fine, 24 + s * 4 + p, row, second, lane)
                        lv.rest[s * 4 + p, low, lane] = second + (W1[0] * f0 + (W1[1] - HALF_STEP) * f1 + W1[2] * f2)

        lv.each(own_nodes)

        def last_node(row):
            _, _, rates = lv.fine_rates(3, row)
            for s in range(2):
                ends = [lv.get(lv.rest, s * 4 + p, row) + HALF_STEP * rates[p][s] for p in range(4)]
                fix = lv.at(cs, C_NEW + s, row) - lv.block_mean(ends)
                for p in range(4):
                    lv.set(lv.rest, s * 4 + p, row, ends[p] + fix)

        lv.each(last_node)


def load_planes(level, sources, columns, natural):
    count = level.lanes // 128
    matrix = group_matrix(count, False)
    slot = slots(count)
    for read, first in sources:
        blocks = []
        for k in range(count):
            values = [read(plane, k) for plane in range(4)]
            blocks.append(permuted(jnp.concatenate(values, axis=0), matrix))
        rows = blocks[0].shape[0] // 4
        for b in range(2):
            tiles = exchanged([block[:, 128 * b : 128 * b + 128] for block in blocks], slot)
            for q, tile in enumerate(tiles):
                for plane in range(4):
                    natural[plane, 2 * q + b, pl.ds(first, rows), :] = tile[plane * rows : (plane + 1) * rows]
    chunks = level.chunks
    for q in range(count):
        for p, (a, b) in enumerate(PHASES):
            for t in range(chunks):
                picked = [natural[plane, 2 * q + b, pl.ds(2 * t + a, 8, stride=2 * chunks), :] for plane in range(4)]
                lane, row = pl.ds(128 * q, 128), 8 * t
                for s in range(2):
                    level.fine[s * 4 + p, pl.ds(GUARD + row, 8), lane] = picked[s]
                level.coef[p, pl.ds(row, 8), lane] = picked[2]
                level.coef[4 + p, pl.ds(row, 8), lane] = picked[2] + picked[3]
    for plane in range(8):
        for row in {0, level.rows - 8}:
            level.put(level.fine, plane, row, level.at(level.fine, plane, row))


def spread(level, natural):
    count, chunks = level.lanes // 128, level.chunks
    for s in range(2):
        for q in range(count):
            for p, (a, b) in enumerate(PHASES):
                for t in range(chunks):
                    value = level.rest[s * 4 + p, pl.ds(8 * t, 8), pl.ds(128 * q, 128)]
                    natural[s, 2 * q + b, pl.ds(2 * t + a, 8, stride=2 * chunks), :] = value


def merged(level, first, rows, natural):
    count = level.lanes // 128
    matrix = group_matrix(count, True)
    slot = slots(count)
    halves = []
    for b in range(2):
        tiles = []
        for q in range(count):
            tiles.append(jnp.concatenate([natural[s, 2 * q + b, pl.ds(first, rows), :] for s in range(2)], axis=0))
        halves.append(exchanged(tiles, slot))
    blocks = [permuted(jnp.concatenate([halves[0][k], halves[1][k]], axis=1), matrix) for k in range(count)]
    return [[block[s * rows : (s + 1) * rows] for block in blocks] for s in range(2)]


def own_first(rows):
    return pl.multiple_of(lax.axis_index("gx") * rows, rows)


def source_list(refs, rows, parts):
    if parts == 2:
        mine = own_first(rows)
        return [(refs[0::2], mine), (refs[1::2], pl.multiple_of(rows - mine, rows))]
    return [(tuple(ref.at[g] for ref in refs), g * rows) for g in range(parts)]


def interior_kernel(parts, rows, columns, halo, depth, width, *refs):
    count, outs = (6, 3) if parts == 2 else (3, 2)
    ins, window, keep, give = refs[:count], refs[count], refs[count + 1], refs[count + 2]
    work = refs[count + outs :]
    here = columns // 2 if parts == 2 else columns
    origin = pl.multiple_of(lax.axis_index("gx") * here, here) if parts == 2 else 0
    level = Level(work[:-1], parts * rows // 2, here // 2, None)
    seam = 4 * depth if parts == 2 else 0
    side = (width - seam) // 2 - halo

    def reader(state, feed, kill):
        def read(plane, block):
            lane = pl.ds(origin + 256 * block, 256)
            return state[plane, :, lane] if plane < 2 else (feed, kill)[plane - 2][:, lane]

        return read

    sources = []
    for (state, feed, kill), first in source_list(ins, rows, parts):
        sources.append((reader(state, feed, kill), first))
        for plane in range(4):
            value = state[plane] if plane < 2 else (feed, kill)[plane - 2][...]
            cuts = [value[:, :halo], value[:, :side], value[:, (columns - seam) // 2 : (columns + seam) // 2]]
            cuts += [value[:, columns - side :], value[:, columns - halo :]]
            window[plane, pl.ds(first, rows), :] = jnp.concatenate([cut for cut in cuts if cut.shape[1]], axis=1)
    load_planes(level, sources, here, work[-1])
    level.run(lax.axis_index("ta"))
    spread(level, work[-1])
    mine = own_first(rows)
    targets = [(keep, mine), (give, pl.multiple_of(rows - mine, rows))] if parts == 2 else [(keep, mine)]
    for target, first in targets:
        natural = merged(level, first, rows, work[-1])
        for s in range(2):
            for k, block in enumerate(natural[s]):
                target[s, :, pl.ds(256 * k, 256)] = block


def border_kernel(parts, rows, halo, depth, width, *refs):
    count, inners = (4, 2) if parts == 2 else (2, 1)
    strips, window, inner = refs[:count], refs[count], refs[count + 1 : count + 1 + inners]
    out, work = refs[count + 1 + inners], refs[count + 2 + inners :]
    lanes = width // 2
    seam = 4 * depth if parts == 2 else 0
    index, size = lax.axis_index("gy"), lax.axis_size("gy")
    even = lax.rem(index, 2) == 0
    tiles = lanes // 128
    at = lax.broadcasted_iota(jnp.int32, (1, lanes), 1)
    at = tiles * (at % 128) + at // 128
    outside = ((at < halo // 2) & (index == 0)) | ((at >= lanes - halo // 2) & (index == size - 1))
    level = Level(work[:-1], parts * rows // 2, lanes, jnp.where(outside, 0.0, 1.0))

    def reader(from_a, from_b, first):
        def read(plane, block):
            part = slice(halo * plane, halo * plane + halo)
            a, b = from_a[:, part], from_b[:, part]
            low, high = jnp.where(even, b, a), jnp.where(even, a, b)
            own = window[plane, pl.ds(first, rows), :]
            whole = jnp.concatenate([low, own[:, halo : width - halo], high], axis=1)
            return whole[:, 256 * block : 256 * block + 256]

        return read

    sources = [(reader(a, b, first), first) for (a, b), first in source_list(strips, rows, parts)]
    load_planes(level, sources, width, work[-1])
    total = out.shape[-1]
    share = total // inners
    for k, value in enumerate(inner):
        origin = lax.axis_index("gx") * share
        origin = 0 if inners == 1 else pl.multiple_of(origin if k == 0 else share - origin, share)
        out[0, :, :, pl.ds(origin, share)] = value[...]
    level.run(lax.axis_index("ta"))
    spread(level, work[-1])
    natural = merged(level, own_first(rows), rows, work[-1])
    pieces = [(0, halo, depth), (total - depth, width - halo - depth, depth)]
    if seam:
        pieces.append((total // 2 - depth, width // 2 - depth, depth))
        pieces.append((total // 2, width // 2, depth))
    for s in range(2):
        whole = jnp.concatenate(natural[s], axis=1) if len(natural[s]) > 1 else natural[s][0]
        for column, source, size in pieces:
            low = column // 128 * 128
            high = round_up(column + size, 128)
            old = out[0, s, :, pl.ds(low, high - low)]
            parts_of = [old[:, : column - low], whole[:, source : source + size], old[:, column + size - low :]]
            out[0, s, :, pl.ds(low, high - low)] = jnp.concatenate([x for x in parts_of if x.shape[1]], axis=1)


def pack_kernel(halo, state, feed, kill, to_a, to_b, left, right, sems):
    width, total = left.shape[-1], feed.shape[1]
    copies = []
    for side, (target, lane) in enumerate(((left, pl.ds(0, width)), (right, pl.ds(total - width, width)))):
        copies.append(pltpu.make_async_copy(state.at[:, :, lane], target.at[pl.ds(0, 2)], sems.at[side, 0]))
        copies.append(pltpu.make_async_copy(feed.at[:, lane], target.at[2], sems.at[side, 1]))
        copies.append(pltpu.make_async_copy(kill.at[:, lane], target.at[3], sems.at[side, 2]))
    for copy in copies:
        copy.start()
    for copy in copies:
        copy.wait()
    low = jnp.concatenate([left[plane, :, :halo] for plane in range(4)], axis=1)
    high = jnp.concatenate([right[plane, :, width - halo :] for plane in range(4)], axis=1)
    even = lax.rem(lax.axis_index("gy"), 2) == 0
    to_a[...] = jnp.where(even, high, low)
    to_b[...] = jnp.where(even, low, high)


def both_ways(pairs):
    return [pair for low, high in pairs for pair in ((low, high), (high, low))]


VMEM = pl.BlockSpec(memory_space=pltpu.VMEM)
ANY = pl.BlockSpec(memory_space=pl.ANY)


def work_of(rows, lanes):
    shapes = scratch(rows, lanes) + [pltpu.VMEM((4, 2 * lanes // 128, 2 * rows, 128), F32)]
    size = sum(4 * math.prod(shape.shape) for shape in shapes)
    return shapes, size


def per_device(initial_state, feed_rate, kill_rate):
    slices, parts, blocks = (lax.axis_size(axis) for axis in ("ta", "gx", "gy"))
    _, rows, columns = initial_state.shape
    depth = 2 * (2 * slices + 2)
    halo = round_up(depth, 32)
    seam = 4 * depth if parts == 2 else 0
    width = round_up(2 * halo + 4 * depth + seam, 256)
    strip = round_up(halo, 128)
    every = parts * rows
    here = columns // 2 if parts == 2 else columns

    def across(value):
        if parts == 2:
            return [value, lax.ppermute(value, "gx", [(0, 1), (1, 0)])]
        return [lax.all_gather(value, "gx")]

    to_a, to_b = pl.pallas_call(
        functools.partial(pack_kernel, halo),
        out_shape=[jax.ShapeDtypeStruct((rows, 4 * halo), F32)] * 2,
        in_specs=[ANY] * 3,
        out_specs=[VMEM] * 2,
        scratch_shapes=[pltpu.VMEM((4, rows, strip), F32)] * 2 + [pltpu.SemaphoreType.DMA((2, 3))],
        name="pack",
    )(initial_state, feed_rate, kill_rate)
    fields = [value for field in (initial_state, feed_rate, kill_rate) for value in across(field)]
    from_b = lax.ppermute(to_b, "gy", both_ways([(i, i + 1) for i in range(1, blocks - 1, 2)]))
    from_a = lax.ppermute(to_a, "gy", both_ways([(i, i + 1) for i in range(0, blocks - 1, 2)]))
    work, size = work_of(every // 2, here // 2)
    window, *inner = pl.pallas_call(
        functools.partial(interior_kernel, parts, rows, columns, halo, depth, width),
        out_shape=[jax.ShapeDtypeStruct((4, every, width), F32)]
        + [jax.ShapeDtypeStruct((2, rows, here), F32)] * (2 if parts == 2 else 1),
        in_specs=[VMEM] * len(fields),
        out_specs=[VMEM] * (3 if parts == 2 else 2),
        scratch_shapes=work,
        compiler_params=pltpu.CompilerParams(vmem_limit_bytes=size + 32 * every * (columns + width) + 2**22),
        cost_estimate=pl.CostEstimate(flops=40 * 2**20, bytes_accessed=20 * 2**20, transcendentals=0),
        name="interior",
    )(*fields)
    from_a, from_b, window, *inner = lax.optimization_barrier((from_a, from_b, window, *inner))
    if parts == 2:
        inner[1] = lax.ppermute(inner[1], "gx", [(0, 1), (1, 0)])
    strips = [value for strip in (from_a, from_b) for value in across(strip)]
    work, size = work_of(every // 2, width // 2)
    return pl.pallas_call(
        functools.partial(border_kernel, parts, rows, halo, depth, width),
        out_shape=jax.ShapeDtypeStruct((1, 2, rows, columns), F32),
        in_specs=[VMEM] * (len(strips) + 1 + len(inner)),
        out_specs=VMEM,
        scratch_shapes=work,
        compiler_params=pltpu.CompilerParams(vmem_limit_bytes=size + 32 * rows * columns + 2**23),
        name="border",
    )(*strips, window, *inner)


def solution(mesh):
    placed = (P(None, "gx", "gy"), P("gx", "gy"), P("gx", "gy"))
    return jax.shard_map(
        per_device, mesh=mesh, in_specs=placed, out_specs=P("ta", None, "gx", "gy"), check_vma=False
    )
```

```python
import functools
import math

import jax
import jax.numpy as jnp
from jax import lax
from jax.experimental import pallas as pl
from jax.experimental.pallas import tpu as pltpu
from jax.sharding import PartitionSpec as P

TURNS = 2

DIFF_U = 0.2
DIFF_V = 0.1
HALF_STEP = 0.5
W0 = (5.0 / 24.0, 1.0 / 3.0, -1.0 / 24.0)
W1 = (-1.0 / 24.0, 1.0 / 3.0, 5.0 / 24.0)
GUARD = 8
F32 = jnp.float32
BF16 = jnp.bfloat16
PHASES = ((0, 0), (0, 1), (1, 0), (1, 1))


def round_up(value, step):
    return -(-value // step) * step


def thirds(value):
    high = value.astype(BF16)
    rest = value - high.astype(F32)
    middle = rest.astype(BF16)
    low = (rest - middle.astype(F32)).astype(BF16)
    return high, middle, low


def permuted(value, matrix):
    rows = value.shape[0]
    parts = jnp.concatenate(thirds(value), axis=0)
    moved = jnp.dot(parts, matrix, preferred_element_type=F32)
    return (moved[2 * rows :] + moved[rows : 2 * rows]) + moved[:rows]


def group_matrix(tiles, inverse):
    group = 128 // tiles
    natural = lax.broadcasted_iota(jnp.int32, (256, 256), 1 if inverse else 0)
    grouped = lax.broadcasted_iota(jnp.int32, (256, 256), 0 if inverse else 1)
    wanted = 2 * tiles * (grouped % group) + 2 * ((grouped % 128) // group) + grouped // 128
    return jnp.where(natural == wanted, 1.0, 0.0).astype(BF16)


def exchanged(tiles, slot):
    count = len(tiles)
    if count == 1:
        return tiles
    group = 128 // count
    turned = [pltpu.roll(tile, k * group, 1) if k else tile for k, tile in enumerate(tiles)]
    results = []
    for q in range(count):
        value = turned[(count - q) % count]
        for at in range(1, count):
            value = jnp.where(slot == at, turned[(at - q) % count], value)
        results.append(pltpu.roll(value, (count - q) * group, 1) if q else value)
    return results


def slots(tiles):
    return lax.broadcasted_iota(jnp.int32, (1, 128), 1) // (128 // tiles)


C_X0, C_X1, C_X2, C_END, C_C1, C_NEW, C_E1, C_D1, C_D2 = (2 * i for i in range(9))
COARSE_STENCIL = 20
N_LAST, N_K0, N_K1, N_G0, N_RA, N_RB, N_RE, N_F1, N_RF2 = (2 * i for i in range(9))
COARSE_PLAIN = 18


def scratch(rows, lanes):
    guarded = rows + 2 * GUARD
    return [
        pltpu.VMEM((4 * 8, guarded, lanes), F32),
        pltpu.VMEM((3 * 8, rows, lanes), F32),
        pltpu.VMEM((8, rows, lanes), F32),
        pltpu.VMEM((8, rows, lanes), F32),
        pltpu.VMEM((COARSE_STENCIL, guarded, lanes), F32),
        pltpu.VMEM((COARSE_PLAIN, rows, lanes), F32),
        pltpu.VMEM((2, rows, lanes), F32),
        pltpu.VMEM((8, rows, lanes), F32),
        pltpu.VMEM((24, rows, lanes), F32),
    ]


class Level:
    def __init__(self, refs, rows, lanes, mask):
        (self.fine, self.lin, self.coef, self.rest, self.cs, self.cp, self.cc, self.mom, self.tl) = refs
        self.rows, self.lanes, self.mask = rows, lanes, mask
        self.chunks = rows // 8

    def each(self, body):
        if self.chunks <= 4:
            for i in range(self.chunks):
                body(8 * i)
        else:
            pl.loop(0, self.chunks)(lambda i: body(pl.multiple_of(8 * i, 8)))

    def left(self, value):
        if self.lanes == 128:
            return pltpu.roll(value, 1, 1)
        return jnp.concatenate([pltpu.roll(value[:, -128:], 1, 1), value[:, :-128]], axis=1)

    def right(self, value):
        if self.lanes == 128:
            return pltpu.roll(value, 127, 1)
        return jnp.concatenate([value[:, 128:], pltpu.roll(value[:, :128], 127, 1)], axis=1)

    def scaled(self, value, factor):
        if self.mask is None:
            return factor * value
        return (factor * self.mask) * value

    def at(self, ref, plane, row, shift=0):
        return ref[plane, pl.ds(GUARD + row + 8 * shift, 8), :]

    def put(self, ref, plane, row, value, lane=slice(None)):
        ref[plane, pl.ds(GUARD + row, 8), lane] = value
        sublane = lax.broadcasted_iota(jnp.int32, (8, 1), 0)
        last = self.rows - 8

        def top():
            ref[plane, pl.ds(0, 8), lane] = jnp.where(sublane == 0, 0.0, pltpu.roll(value, 1, 0))

        def bottom():
            ref[plane, pl.ds(GUARD + self.rows, 8), lane] = jnp.where(sublane == 7, 0.0, pltpu.roll(value, 7, 0))

        for edge, fill in ((last, top), (0, bottom)):
            if not isinstance(row, int):
                pl.when(row == edge)(fill)
            elif row == edge:
                fill()

    def get(self, ref, plane, row):
        return ref[plane, pl.ds(row, 8), :]

    def set(self, ref, plane, row, value):
        ref[plane, pl.ds(row, 8), :] = value

    def fine_rates(self, base, row):
        state = [[self.at(self.fine, base * 8 + s * 4 + p, row) for p in range(4)] for s in range(2)]
        linear, rates = [], []
        for p, (a, b) in enumerate(PHASES):
            laps = []
            for s in range(2):
                across = state[s][2 * a + 1 - b]
                along = state[s][2 * (1 - a) + b]
                moved = self.at(self.fine, base * 8 + s * 4 + 2 * (1 - a) + b, row, 1 if a else -1)
                side = self.right(across) if b else self.left(across)
                laps.append((along + moved) + (across + side) - 4.0 * state[s][p])
            u, v = state[0][p], state[1][p]
            feed = self.get(self.coef, p, row)
            both = self.get(self.coef, 4 + p, row)
            lin_u = self.scaled(laps[0], DIFF_U) + feed
            lin_v = self.scaled(laps[1], DIFF_V)
            linear.append((lin_u, lin_v))
            rates.append(self.reacted(u, v, lin_u, lin_v, feed, both))
        return state, linear, rates

    def reacted(self, u, v, lin_u, lin_v, feed, both):
        return lin_u - u * (feed + v * v), lin_v + v * (u * v - both)

    def neighbours(self, plane, row, value):
        rows = self.at(self.cs, plane, row, -1) + self.at(self.cs, plane, row, 1)
        return rows + (self.left(value) + self.right(value))

    def laplacians(self, first, row):
        pair = [self.at(self.cs, first + s, row) for s in range(2)]
        return pair, [self.neighbours(first + s, row, pair[s]) - 4.0 * pair[s] for s in range(2)]

    def coarse_rates(self, first, row):
        (u, v), laps = self.laplacians(first, row)
        scaled = [self.scaled(laps[s], 0.25 * (DIFF_U, DIFF_V)[s]) for s in range(2)]
        feed, both = self.get(self.cc, 0, row), self.get(self.cc, 1, row)
        return (u, v), scaled, self.reacted(u, v, scaled[0] + feed, scaled[1], feed, both)

    def moved_rates(self, shift, scaled, which, base, row):
        a, b = shift
        m_vv, m_uv, m_u, m_v = (self.get(self.mom, 4 * which + k, row) for k in range(4))
        react = a * (m_vv + b * (2.0 * m_v + b)) + b * (2.0 * m_uv + b * m_u)
        feed, both = self.get(self.cc, 0, row), self.get(self.cc, 1, row)
        rate_u = (self.get(self.cp, base, row) + 2.0 * scaled[0]) - (feed * a + react)
        rate_v = (self.get(self.cp, base + 1, row) + 2.0 * scaled[1]) + (react - both * b)
        return rate_u, rate_v

    def block_mean(self, values):
        return 0.25 * ((values[0] + values[1]) + (values[2] + values[3]))

    def run(self, own):
        lv = self
        cs, cp = self.cs, self.cp

        def first_sweep(row):
            for k in range(2):
                lv.set(lv.cc, k, row, lv.block_mean([lv.get(lv.coef, 4 * k + p, row) for p in range(4)]))
            state, linear, rates = lv.fine_rates(0, row)
            for s in range(2):
                for p in range(4):
                    lv.set(lv.lin, s * 4 + p, row, linear[p][s])
                    lv.put(lv.fine, 8 + s * 4 + p, row, state[s][p] + HALF_STEP * rates[p][s])
                mean = lv.block_mean([r[s] for r in rates])
                start = lv.block_mean(state[s])
                lv.set(cp, N_RA + s, row, mean)
                lv.put(cs, C_X0 + s, row, start)
                lv.put(cs, C_X1 + s, row, start + HALF_STEP * mean)
                lv.put(cs, C_END + s, row, start + mean)
                lv.put(cs, C_D1 + s, row, jnp.zeros_like(mean))

        def moments(which, state, row):
            u, v = state
            lv.set(lv.mom, 4 * which, row, lv.block_mean([v[p] * v[p] for p in range(4)]))
            lv.set(lv.mom, 4 * which + 1, row, lv.block_mean([u[p] * v[p] for p in range(4)]))
            lv.set(lv.mom, 4 * which + 2, row, lv.block_mean(u))
            lv.set(lv.mom, 4 * which + 3, row, lv.block_mean(v))

        def second_sweep(row):
            state, linear, rates = lv.fine_rates(1, row)
            _, _, g0 = lv.coarse_rates(C_X0, row)
            first, scaled, g1 = lv.coarse_rates(C_X1, row)
            for s in range(2):
                for p in range(4):
                    lv.set(lv.lin, 8 + s * 4 + p, row, linear[p][s])
                    lv.put(lv.fine, 16 + s * 4 + p, row, state[s][p] + HALF_STEP * rates[p][s])
                mean = lv.block_mean([r[s] for r in rates])
                lv.set(cp, N_F1 + s, row, mean)
                lv.set(cp, N_RB + s, row, mean - 2.0 * scaled[s])
                lv.put(cs, C_X2 + s, row, first[s] + HALF_STEP * mean)
                integral = HALF_STEP * lv.get(cp, N_RA + s, row)
                lv.set(cp, N_K0 + s, row, integral - HALF_STEP * g0[s])
                lv.set(cp, N_K1 + s, row, integral - HALF_STEP * g1[s])
            moments(0, state, row)

        def third_sweep(row):
            state, linear, rates = lv.fine_rates(2, row)
            for s in range(2):
                for p in range(4):
                    lv.set(lv.lin, 16 + s * 4 + p, row, linear[p][s])
            moments(1, state, row)
            second, laps = lv.laplacians(C_X2, row)
            for s in range(2):
                mean = lv.block_mean([r[s] for r in rates])
                lv.set(cp, N_RE + s, row, mean - lv.scaled(laps[s], 0.5 * (DIFF_U, DIFF_V)[s]))
            end, last = slice_end(C_D2, row)
            for s in range(2):
                j0, j1 = integrals(lv.get(cp, N_RA + s, row), lv.get(cp, N_F1 + s, row), last[s])
                lv.put(cs, C_NEW + s, row, lv.at(cs, C_X0 + s, row) + (j0 + j1))

        def integrals(f0, f1, f2):
            middle = W0[1] * f1
            return middle + (W0[0] * f0 + W0[2] * f2), middle + (W1[0] * f0 + W1[2] * f2)

        def slice_end(now, row):
            end, scaled, rate = lv.coarse_rates(C_END, row)
            shift = [end[s] - lv.at(cs, C_X2 + s, row) for s in range(2)]
            last = lv.moved_rates(shift, scaled, 1, N_RE, row)
            for s in range(2):
                half = HALF_STEP * rate[s]
                lv.set(cp, N_G0 + s, row, half)
                lv.put(cs, C_C1 + s, row, end[s] + half + lv.get(cp, N_K0 + s, row))
                lv.put(cs, now + s, row, shift[s])
                lv.set(cp, N_RF2 + s, row, last[s])
            return end, last

        def middle_nodes(row):
            mid, scaled, rate = lv.coarse_rates(C_C1, row)
            new, _, new_rate = lv.coarse_rates(C_NEW, row)
            shift = [mid[s] - lv.at(cs, C_X1 + s, row) for s in range(2)]
            f1 = lv.moved_rates(shift, scaled, 0, N_RB, row)
            for s in range(2):
                old = lv.at(cs, C_END + s, row)
                lv.set(cp, N_LAST + s, row, old)
                lv.set(cp, N_F1 + s, row, f1[s])
                lv.put(cs, C_D1 + s, row, shift[s])
                lv.put(cs, C_END + s, row, mid[s] + HALF_STEP * rate[s] + lv.get(cp, N_K1 + s, row))
                change = HALF_STEP * new_rate[s] - lv.get(cp, N_G0 + s, row)
                lv.put(cs, C_E1 + s, row, (new[s] - old) + change)

        def end_nodes(now):
            def body(row):
                before = [lv.get(cp, N_RF2 + s, row) for s in range(2)]
                _, last = slice_end(now, row)
                change, laps = lv.laplacians(C_E1, row)
                old, new, j1s = [], [], []
                for s in range(2):
                    j0, j1 = integrals(before[s], lv.get(cp, N_F1 + s, row), last[s])
                    old.append(lv.get(cp, N_LAST + s, row) + j0)
                    new.append(old[s] + change[s])
                    j1s.append(j1)
                feed, both = lv.get(lv.cc, 0, row), lv.get(lv.cc, 1, row)
                lin = [lv.scaled(laps[s], 0.25 * (DIFF_U, DIFF_V)[s]) for s in range(2)]
                rate_new = lv.reacted(new[0], new[1], lin[0], lin[1], feed, both)
                rate_old = lv.reacted(old[0], old[1], 0.0, 0.0, feed, both)
                for s in range(2):
                    total = new[s] + j1s[s] + HALF_STEP * (rate_new[s] - rate_old[s])
                    lv.put(cs, C_NEW + s, row, total)

            return body

        def corrections(starts):
            def body(row):
                for k, first in enumerate(starts):
                    for s in range(2):
                        d = lv.at(cs, first + s, row)
                        ring = [lv.at(cs, first + s, row, -1), lv.at(cs, first + s, row, 1), lv.left(d), lv.right(d)]
                        north, south, west, east = (lv.scaled(x - d, (DIFF_U, DIFF_V)[s]) for x in ring)
                        for p, (a, b) in enumerate(PHASES):
                            lv.set(lv.tl, k * 8 + s * 4 + p, row, (south if a else north) + (east if b else west))

            return body

        lv.each(first_sweep)
        lv.each(second_sweep)
        lv.each(third_sweep)

        def one_slice(n, carry):
            lv.each(middle_nodes)
            lv.each(end_nodes(C_D2 + 2 * lax.rem(n, 2)))
            return carry

        lax.fori_loop(1, own + 1, one_slice, 0)

        first = own == 0
        now = C_D2 + 2 * lax.rem(own, 2)
        before = jnp.where(first, C_D1, 2 * C_D2 + 2 - now)
        origin = jnp.where(first, 0, 2)
        lv.each(corrections((before, C_D1, now)))

        def own_nodes(row):
            for p in range(4):
                for t in range(0, lv.lanes, 128):
                    lane = pl.ds(t, 128)
                    high = pl.ds(GUARD + row, 8)
                    low = pl.ds(row, 8)
                    feed, both = lv.coef[p, low, lane], lv.coef[4 + p, low, lane]
                    rates, start = [], None
                    for k, (base, d) in enumerate(((origin, before), (1, C_D1), (2, now))):
                        pair = [lv.fine[base * 8 + s * 4 + p, high, lane] + cs[d + s, high, lane] for s in range(2)]
                        lin = [lv.lin[base * 8 + s * 4 + p, low, lane] + lv.tl[k * 8 + s * 4 + p, low, lane] for s in range(2)]
                        rates.append(lv.reacted(pair[0], pair[1], lin[0], lin[1], feed, both))
                        start = pair if k == 0 else start
                    for s in range(2):
                        f0, f1, f2 = (r[s] for r in rates)
                        second = start[s] + (W0[0] * f0 + W0[1] * f1 + W0[2] * f2)
                        lv.put(lv.fine, 24 + s * 4 + p, row, second, lane)
                        lv.rest[s * 4 + p, low, lane] = second + (W1[0] * f0 + (W1[1] - HALF_STEP) * f1 + W1[2] * f2)

        lv.each(own_nodes)

        def last_node(row):
            _, _, rates = lv.fine_rates(3, row)
            for s in range(2):
                ends = [lv.get(lv.rest, s * 4 + p, row) + HALF_STEP * rates[p][s] for p in range(4)]
                fix = lv.at(cs, C_NEW + s, row) - lv.block_mean(ends)
                for p in range(4):
                    lv.set(lv.rest, s * 4 + p, row, ends[p] + fix)

        lv.each(last_node)


def load_planes(level, sources, columns, natural):
    count = level.lanes // 128
    matrix = group_matrix(count, False)
    slot = slots(count)
    for read, first in sources:
        blocks = []
        for k in range(count):
            values = [read(plane, k) for plane in range(4)]
            blocks.append(permuted(jnp.concatenate(values, axis=0), matrix))
        rows = blocks[0].shape[0] // 4
        for b in range(2):
            tiles = exchanged([block[:, 128 * b : 128 * b + 128] for block in blocks], slot)
            for q, tile in enumerate(tiles):
                for plane in range(4):
                    natural[plane, 2 * q + b, pl.ds(first, rows), :] = tile[plane * rows : (plane + 1) * rows]
    chunks = level.chunks
    for q in range(count):
        for p, (a, b) in enumerate(PHASES):
            for t in range(chunks):
                picked = [natural[plane, 2 * q + b, pl.ds(2 * t + a, 8, stride=2 * chunks), :] for plane in range(4)]
                lane, row = pl.ds(128 * q, 128), 8 * t
                for s in range(2):
                    level.fine[s * 4 + p, pl.ds(GUARD + row, 8), lane] = picked[s]
                level.coef[p, pl.ds(row, 8), lane] = picked[2]
                level.coef[4 + p, pl.ds(row, 8), lane] = picked[2] + picked[3]
    for plane in range(8):
        for row in {0, level.rows - 8}:
            level.put(level.fine, plane, row, level.at(level.fine, plane, row))


def spread(level, natural):
    count, chunks = level.lanes // 128, level.chunks
    for s in range(2):
        for q in range(count):
            for p, (a, b) in enumerate(PHASES):
                for t in range(chunks):
                    value = level.rest[s * 4 + p, pl.ds(8 * t, 8), pl.ds(128 * q, 128)]
                    natural[s, 2 * q + b, pl.ds(2 * t + a, 8, stride=2 * chunks), :] = value


def merged(level, first, rows, natural):
    count = level.lanes // 128
    matrix = group_matrix(count, True)
    slot = slots(count)
    halves = []
    for b in range(2):
        tiles = []
        for q in range(count):
            tiles.append(jnp.concatenate([natural[s, 2 * q + b, pl.ds(first, rows), :] for s in range(2)], axis=0))
        halves.append(exchanged(tiles, slot))
    blocks = [permuted(jnp.concatenate([halves[0][k], halves[1][k]], axis=1), matrix) for k in range(count)]
    return [[block[s * rows : (s + 1) * rows] for block in blocks] for s in range(2)]


def own_first(rows):
    return pl.multiple_of(lax.axis_index("gx") * rows, rows)


def source_list(refs, rows, parts):
    if parts == 2:
        mine = own_first(rows)
        return [(refs[0::2], mine), (refs[1::2], pl.multiple_of(rows - mine, rows))]
    return [(tuple(ref.at[g] for ref in refs), g * rows) for g in range(parts)]


def interior_kernel(parts, rows, columns, halo, depth, width, *refs):
    count, outs = (6, 3) if parts == 2 else (3, 2)
    ins, window, keep, give = refs[:count], refs[count], refs[count + 1], refs[count + 2]
    work = refs[count + outs :]
    here = columns // 2 if parts == 2 else columns
    origin = pl.multiple_of(lax.axis_index("gx") * here, here) if parts == 2 else 0
    level = Level(work[:-1], parts * rows // 2, here // 2, None)
    seam = 4 * depth if parts == 2 else 0
    side = (width - seam) // 2 - halo

    def reader(state, feed, kill):
        def read(plane, block):
            lane = pl.ds(origin + 256 * block, 256)
            return state[plane, :, lane] if plane < 2 else (feed, kill)[plane - 2][:, lane]

        return read

    sources = []
    for (state, feed, kill), first in source_list(ins, rows, parts):
        sources.append((reader(state, feed, kill), first))
        for plane in range(4):
            value = state[plane] if plane < 2 else (feed, kill)[plane - 2][...]
            cuts = [value[:, :halo], value[:, :side], value[:, (columns - seam) // 2 : (columns + seam) // 2]]
            cuts += [value[:, columns - side :], value[:, columns - halo :]]
            window[plane, pl.ds(first, rows), :] = jnp.concatenate([cut for cut in cuts if cut.shape[1]], axis=1)
    load_planes(level, sources, here, work[-1])
    level.run(lax.axis_index("ta"))
    spread(level, work[-1])
    mine = own_first(rows)
    targets = [(keep, mine), (give, pl.multiple_of(rows - mine, rows))] if parts == 2 else [(keep, mine)]
    for target, first in targets:
        natural = merged(level, first, rows, work[-1])
        for s in range(2):
            for k, block in enumerate(natural[s]):
                target[s, :, pl.ds(256 * k, 256)] = block


def border_kernel(parts, rows, halo, depth, width, *refs):
    count, inners = (4, 2) if parts == 2 else (2, 1)
    strips, window, inner = refs[:count], refs[count], refs[count + 1 : count + 1 + inners]
    out, work = refs[count + 1 + inners], refs[count + 2 + inners :]
    lanes = width // 2
    seam = 4 * depth if parts == 2 else 0
    index, size = lax.axis_index("gy"), lax.axis_size("gy")
    even = lax.rem(index, 2) == 0
    tiles = lanes // 128
    at = lax.broadcasted_iota(jnp.int32, (1, lanes), 1)
    at = tiles * (at % 128) + at // 128
    outside = ((at < halo // 2) & (index == 0)) | ((at >= lanes - halo // 2) & (index == size - 1))
    level = Level(work[:-1], parts * rows // 2, lanes, jnp.where(outside, 0.0, 1.0))

    def reader(from_a, from_b, first):
        def read(plane, block):
            part = slice(halo * plane, halo * plane + halo)
            a, b = from_a[:, part], from_b[:, part]
            low, high = jnp.where(even, b, a), jnp.where(even, a, b)
            low, high = jnp.where(index == 0, 0.0, low), jnp.where(index == size - 1, 0.0, high)
            own = window[plane, pl.ds(first, rows), :]
            whole = jnp.concatenate([low, own[:, halo : width - halo], high], axis=1)
            return whole[:, 256 * block : 256 * block + 256]

        return read

    sources = [(reader(a, b, first), first) for (a, b), first in source_list(strips, rows, parts)]
    load_planes(level, sources, width, work[-1])
    total = out.shape[-1]
    share = total // inners
    for k, value in enumerate(inner):
        origin = lax.axis_index("gx") * share
        origin = 0 if inners == 1 else pl.multiple_of(origin if k == 0 else share - origin, share)
        out[0, :, :, pl.ds(origin, share)] = value[...]
    level.run(lax.axis_index("ta"))
    spread(level, work[-1])
    natural = merged(level, own_first(rows), rows, work[-1])
    pieces = [(0, halo, depth), (total - depth, width - halo - depth, depth)]
    if seam:
        pieces.append((total // 2 - depth, width // 2 - depth, depth))
        pieces.append((total // 2, width // 2, depth))
    for s in range(2):
        whole = jnp.concatenate(natural[s], axis=1) if len(natural[s]) > 1 else natural[s][0]
        for column, source, size in pieces:
            low = column // 128 * 128
            high = round_up(column + size, 128)
            old = out[0, s, :, pl.ds(low, high - low)]
            parts_of = [old[:, : column - low], whole[:, source : source + size], old[:, column + size - low :]]
            out[0, s, :, pl.ds(low, high - low)] = jnp.concatenate([x for x in parts_of if x.shape[1]], axis=1)


def pack_kernel(halo, state, feed, kill, to_a, to_b, left, right, sems):
    width, total = left.shape[-1], feed.shape[1]
    copies = []
    for side, (target, lane) in enumerate(((left, pl.ds(0, width)), (right, pl.ds(total - width, width)))):
        copies.append(pltpu.make_async_copy(state.at[:, :, lane], target.at[pl.ds(0, 2)], sems.at[side, 0]))
        copies.append(pltpu.make_async_copy(feed.at[:, lane], target.at[2], sems.at[side, 1]))
        copies.append(pltpu.make_async_copy(kill.at[:, lane], target.at[3], sems.at[side, 2]))
    for copy in copies:
        copy.start()
    for copy in copies:
        copy.wait()
    low = jnp.concatenate([left[plane, :, :halo] for plane in range(4)], axis=1)
    high = jnp.concatenate([right[plane, :, width - halo :] for plane in range(4)], axis=1)
    even = lax.rem(lax.axis_index("gy"), 2) == 0
    to_a[...] = jnp.where(even, high, low)
    to_b[...] = jnp.where(even, low, high)


def both_ways(pairs):
    return [pair for low, high in pairs for pair in ((low, high), (high, low))]


VMEM = pl.BlockSpec(memory_space=pltpu.VMEM)
ANY = pl.BlockSpec(memory_space=pl.ANY)


def work_of(rows, lanes):
    shapes = scratch(rows, lanes) + [pltpu.VMEM((4, 2 * lanes // 128, 2 * rows, 128), F32)]
    size = sum(4 * math.prod(shape.shape) for shape in shapes)
    return shapes, size


def per_device(initial_state, feed_rate, kill_rate):
    slices, parts, blocks = (lax.axis_size(axis) for axis in ("ta", "gx", "gy"))
    _, rows, columns = initial_state.shape
    depth = 2 * (2 * slices + 2)
    halo = round_up(depth, 32)
    seam = 4 * depth if parts == 2 else 0
    width = round_up(2 * halo + 4 * depth + seam, 256)
    strip = round_up(halo, 128)
    every = parts * rows
    here = columns // 2 if parts == 2 else columns

    def across(value):
        if parts == 2:
            return [value, lax.ppermute(value, "gx", [(0, 1), (1, 0)])]
        return [lax.all_gather(value, "gx")]

    to_a, to_b = pl.pallas_call(
        functools.partial(pack_kernel, halo),
        out_shape=[jax.ShapeDtypeStruct((rows, 4 * halo), F32)] * 2,
        in_specs=[ANY] * 3,
        out_specs=[VMEM] * 2,
        scratch_shapes=[pltpu.VMEM((4, rows, strip), F32)] * 2 + [pltpu.SemaphoreType.DMA((2, 3))],
        compiler_params=pltpu.CompilerParams(vmem_limit_bytes=54 * 2**20 - 2**17),
        name="pack",
    )(initial_state, feed_rate, kill_rate)
    fields = [value for field in (initial_state, feed_rate, kill_rate) for value in across(field)]
    from_b = lax.ppermute(to_b, "gy", both_ways([(i, (i + 1) % blocks) for i in range(1, blocks - blocks % 2, 2)]))
    from_a = lax.ppermute(to_a, "gy", both_ways([(i, i + 1) for i in range(0, blocks - 1, 2)]))
    work, size = work_of(every // 2, here // 2)
    window, *inner = pl.pallas_call(
        functools.partial(interior_kernel, parts, rows, columns, halo, depth, width),
        out_shape=[jax.ShapeDtypeStruct((4, every, width), F32)]
        + [jax.ShapeDtypeStruct((2, rows, here), F32)] * (2 if parts == 2 else 1),
        in_specs=[VMEM] * len(fields),
        out_specs=[VMEM] * (3 if parts == 2 else 2),
        scratch_shapes=work,
        compiler_params=pltpu.CompilerParams(vmem_limit_bytes=size + 32 * every * (columns + width) + 2**22),
        cost_estimate=pl.CostEstimate(flops=40 * 2**20, bytes_accessed=20 * 2**20, transcendentals=0),
        name="interior",
    )(*fields)
    from_a, from_b, window, *inner = lax.optimization_barrier((from_a, from_b, window, *inner))
    if parts == 2:
        inner[1] = lax.ppermute(inner[1], "gx", [(0, 1), (1, 0)])
    strips = [value for strip in (from_a, from_b) for value in across(strip)]
    work, size = work_of(every // 2, width // 2)
    return pl.pallas_call(
        functools.partial(border_kernel, parts, rows, halo, depth, width),
        out_shape=jax.ShapeDtypeStruct((1, 2, rows, columns), F32),
        in_specs=[VMEM] * (len(strips) + 1 + len(inner)),
        out_specs=VMEM,
        scratch_shapes=work,
        compiler_params=pltpu.CompilerParams(vmem_limit_bytes=size + 32 * rows * columns + 2**23),
        name="border",
    )(*strips, window, *inner)


def solution(mesh):
    placed = (P(None, "gx", "gy"), P("gx", "gy"), P("gx", "gy"))
    return jax.shard_map(
        per_device, mesh=mesh, in_specs=placed, out_specs=P("ta", None, "gx", "gy"), check_vma=False
    )
```

```python
import functools
import math

import jax
import jax.numpy as jnp
from jax import lax
from jax.experimental import pallas as pl
from jax.experimental.pallas import tpu as pltpu
from jax.sharding import PartitionSpec as P

TURNS = 2

DIFF_U = 0.2
DIFF_V = 0.1
HALF_STEP = 0.5
W0 = (5.0 / 24.0, 1.0 / 3.0, -1.0 / 24.0)
W1 = (-1.0 / 24.0, 1.0 / 3.0, 5.0 / 24.0)
GUARD = 8
F32 = jnp.float32
BF16 = jnp.bfloat16
PHASES = ((0, 0), (0, 1), (1, 0), (1, 1))


def round_up(value, step):
    return -(-value // step) * step


def thirds(value):
    high = value.astype(BF16)
    rest = value - high.astype(F32)
    middle = rest.astype(BF16)
    low = (rest - middle.astype(F32)).astype(BF16)
    return high, middle, low


def permuted(value, matrix):
    rows = value.shape[0]
    parts = jnp.concatenate(thirds(value), axis=0)
    moved = jnp.dot(parts, matrix, preferred_element_type=F32)
    return (moved[2 * rows :] + moved[rows : 2 * rows]) + moved[:rows]


def group_matrix(tiles, inverse):
    group = 128 // tiles
    natural = lax.broadcasted_iota(jnp.int32, (256, 256), 1 if inverse else 0)
    grouped = lax.broadcasted_iota(jnp.int32, (256, 256), 0 if inverse else 1)
    wanted = 2 * tiles * (grouped % group) + 2 * ((grouped % 128) // group) + grouped // 128
    return jnp.where(natural == wanted, 1.0, 0.0).astype(BF16)


def exchanged(tiles, slot):
    count = len(tiles)
    if count == 1:
        return tiles
    group = 128 // count
    turned = [pltpu.roll(tile, k * group, 1) if k else tile for k, tile in enumerate(tiles)]
    results = []
    for q in range(count):
        value = turned[(count - q) % count]
        for at in range(1, count):
            value = jnp.where(slot == at, turned[(at - q) % count], value)
        results.append(pltpu.roll(value, (count - q) * group, 1) if q else value)
    return results


def slots(tiles):
    return lax.broadcasted_iota(jnp.int32, (1, 128), 1) // (128 // tiles)


C_X0, C_X1, C_X2, C_END, C_C1, C_NEW, C_E1, C_D1, C_D2 = (2 * i for i in range(9))
COARSE_STENCIL = 20
N_LAST, N_K0, N_K1, N_G0, N_RA, N_RB, N_RE, N_F1, N_RF2 = (2 * i for i in range(9))
COARSE_PLAIN = 18


def scratch(rows, lanes):
    guarded = rows + 2 * GUARD
    return [
        pltpu.VMEM((4 * 8, guarded, lanes), F32),
        pltpu.VMEM((3 * 8, rows, lanes), F32),
        pltpu.VMEM((8, rows, lanes), F32),
        pltpu.VMEM((8, rows, lanes), F32),
        pltpu.VMEM((COARSE_STENCIL, guarded, lanes), F32),
        pltpu.VMEM((COARSE_PLAIN, rows, lanes), F32),
        pltpu.VMEM((2, rows, lanes), F32),
        pltpu.VMEM((8, rows, lanes), F32),
        pltpu.VMEM((24, rows, lanes), F32),
    ]


class Level:
    def __init__(self, refs, rows, lanes, mask):
        (self.fine, self.lin, self.coef, self.rest, self.cs, self.cp, self.cc, self.mom, self.tl) = refs
        self.rows, self.lanes, self.mask = rows, lanes, mask
        self.chunks = rows // 8

    def each(self, body):
        if self.chunks <= 4:
            for i in range(self.chunks):
                body(8 * i)
        else:
            pl.loop(0, self.chunks)(lambda i: body(pl.multiple_of(8 * i, 8)))

    def left(self, value):
        if self.lanes == 128:
            return pltpu.roll(value, 1, 1)
        return jnp.concatenate([pltpu.roll(value[:, -128:], 1, 1), value[:, :-128]], axis=1)

    def right(self, value):
        if self.lanes == 128:
            return pltpu.roll(value, 127, 1)
        return jnp.concatenate([value[:, 128:], pltpu.roll(value[:, :128], 127, 1)], axis=1)

    def scaled(self, value, factor):
        if self.mask is None:
            return factor * value
        return (factor * self.mask) * value

    def at(self, ref, plane, row, shift=0):
        return ref[plane, pl.ds(GUARD + row + 8 * shift, 8), :]

    def put(self, ref, plane, row, value, lane=slice(None)):
        ref[plane, pl.ds(GUARD + row, 8), lane] = value
        sublane = lax.broadcasted_iota(jnp.int32, (8, 1), 0)
        last = self.rows - 8

        def top():
            ref[plane, pl.ds(0, 8), lane] = jnp.where(sublane == 0, 0.0, pltpu.roll(value, 1, 0))

        def bottom():
            ref[plane, pl.ds(GUARD + self.rows, 8), lane] = jnp.where(sublane == 7, 0.0, pltpu.roll(value, 7, 0))

        for edge, fill in ((last, top), (0, bottom)):
            if not isinstance(row, int):
                pl.when(row == edge)(fill)
            elif row == edge:
                fill()

    def get(self, ref, plane, row):
        return ref[plane, pl.ds(row, 8), :]

    def set(self, ref, plane, row, value):
        ref[plane, pl.ds(row, 8), :] = value

    def fine_rates(self, base, row):
        state = [[self.at(self.fine, base * 8 + s * 4 + p, row) for p in range(4)] for s in range(2)]
        linear, rates = [], []
        for p, (a, b) in enumerate(PHASES):
            laps = []
            for s in range(2):
                across = state[s][2 * a + 1 - b]
                along = state[s][2 * (1 - a) + b]
                moved = self.at(self.fine, base * 8 + s * 4 + 2 * (1 - a) + b, row, 1 if a else -1)
                side = self.right(across) if b else self.left(across)
                laps.append((along + moved) + (across + side) - 4.0 * state[s][p])
            u, v = state[0][p], state[1][p]
            feed = self.get(self.coef, p, row)
            both = self.get(self.coef, 4 + p, row)
            lin_u = self.scaled(laps[0], DIFF_U) + feed
            lin_v = self.scaled(laps[1], DIFF_V)
            linear.append((lin_u, lin_v))
            rates.append(self.reacted(u, v, lin_u, lin_v, feed, both))
        return state, linear, rates

    def reacted(self, u, v, lin_u, lin_v, feed, both):
        return lin_u - u * (feed + v * v), lin_v + v * (u * v - both)

    def neighbours(self, plane, row, value):
        rows = self.at(self.cs, plane, row, -1) + self.at(self.cs, plane, row, 1)
        return rows + (self.left(value) + self.right(value))

    def laplacians(self, first, row):
        pair = [self.at(self.cs, first + s, row) for s in range(2)]
        return pair, [self.neighbours(first + s, row, pair[s]) - 4.0 * pair[s] for s in range(2)]

    def coarse_rates(self, first, row):
        (u, v), laps = self.laplacians(first, row)
        scaled = [self.scaled(laps[s], 0.25 * (DIFF_U, DIFF_V)[s]) for s in range(2)]
        feed, both = self.get(self.cc, 0, row), self.get(self.cc, 1, row)
        return (u, v), scaled, self.reacted(u, v, scaled[0] + feed, scaled[1], feed, both)

    def moved_rates(self, shift, scaled, which, base, row):
        a, b = shift
        m_vv, m_uv, m_u, m_v = (self.get(self.mom, 4 * which + k, row) for k in range(4))
        react = a * (m_vv + b * (2.0 * m_v + b)) + b * (2.0 * m_uv + b * m_u)
        feed, both = self.get(self.cc, 0, row), self.get(self.cc, 1, row)
        rate_u = (self.get(self.cp, base, row) + 2.0 * scaled[0]) - (feed * a + react)
        rate_v = (self.get(self.cp, base + 1, row) + 2.0 * scaled[1]) + (react - both * b)
        return rate_u, rate_v

    def block_mean(self, values):
        return 0.25 * ((values[0] + values[1]) + (values[2] + values[3]))

    def run(self, own):
        lv = self
        cs, cp = self.cs, self.cp

        def first_sweep(row):
            for k in range(2):
                lv.set(lv.cc, k, row, lv.block_mean([lv.get(lv.coef, 4 * k + p, row) for p in range(4)]))
            state, linear, rates = lv.fine_rates(0, row)
            for s in range(2):
                for p in range(4):
                    lv.set(lv.lin, s * 4 + p, row, linear[p][s])
                    lv.put(lv.fine, 8 + s * 4 + p, row, state[s][p] + HALF_STEP * rates[p][s])
                mean = lv.block_mean([r[s] for r in rates])
                start = lv.block_mean(state[s])
                lv.set(cp, N_RA + s, row, mean)
                lv.put(cs, C_X0 + s, row, start)
                lv.put(cs, C_X1 + s, row, start + HALF_STEP * mean)
                lv.put(cs, C_END + s, row, start + mean)
                lv.put(cs, C_D1 + s, row, jnp.zeros_like(mean))

        def moments(which, state, row):
            u, v = state
            lv.set(lv.mom, 4 * which, row, lv.block_mean([v[p] * v[p] for p in range(4)]))
            lv.set(lv.mom, 4 * which + 1, row, lv.block_mean([u[p] * v[p] for p in range(4)]))
            lv.set(lv.mom, 4 * which + 2, row, lv.block_mean(u))
            lv.set(lv.mom, 4 * which + 3, row, lv.block_mean(v))

        def second_sweep(row):
            state, linear, rates = lv.fine_rates(1, row)
            _, _, g0 = lv.coarse_rates(C_X0, row)
            first, scaled, g1 = lv.coarse_rates(C_X1, row)
            for s in range(2):
                for p in range(4):
                    lv.set(lv.lin, 8 + s * 4 + p, row, linear[p][s])
                    lv.put(lv.fine, 16 + s * 4 + p, row, state[s][p] + HALF_STEP * rates[p][s])
                mean = lv.block_mean([r[s] for r in rates])
                lv.set(cp, N_F1 + s, row, mean)
                lv.set(cp, N_RB + s, row, mean - 2.0 * scaled[s])
                lv.put(cs, C_X2 + s, row, first[s] + HALF_STEP * mean)
                integral = HALF_STEP * lv.get(cp, N_RA + s, row)
                lv.set(cp, N_K0 + s, row, integral - HALF_STEP * g0[s])
                lv.set(cp, N_K1 + s, row, integral - HALF_STEP * g1[s])
            moments(0, state, row)

        def third_sweep(row):
            state, linear, rates = lv.fine_rates(2, row)
            for s in range(2):
                for p in range(4):
                    lv.set(lv.lin, 16 + s * 4 + p, row, linear[p][s])
            moments(1, state, row)
            second, laps = lv.laplacians(C_X2, row)
            for s in range(2):
                mean = lv.block_mean([r[s] for r in rates])
                lv.set(cp, N_RE + s, row, mean - lv.scaled(laps[s], 0.5 * (DIFF_U, DIFF_V)[s]))
            end, last = slice_end(C_D2, row)
            for s in range(2):
                j0, j1 = integrals(lv.get(cp, N_RA + s, row), lv.get(cp, N_F1 + s, row), last[s])
                lv.put(cs, C_NEW + s, row, lv.at(cs, C_X0 + s, row) + (j0 + j1))

        def integrals(f0, f1, f2):
            middle = W0[1] * f1
            return middle + (W0[0] * f0 + W0[2] * f2), middle + (W1[0] * f0 + W1[2] * f2)

        def slice_end(now, row):
            end, scaled, rate = lv.coarse_rates(C_END, row)
            shift = [end[s] - lv.at(cs, C_X2 + s, row) for s in range(2)]
            last = lv.moved_rates(shift, scaled, 1, N_RE, row)
            for s in range(2):
                half = HALF_STEP * rate[s]
                lv.set(cp, N_G0 + s, row, half)
                lv.put(cs, C_C1 + s, row, end[s] + half + lv.get(cp, N_K0 + s, row))
                lv.put(cs, now + s, row, shift[s])
                lv.set(cp, N_RF2 + s, row, last[s])
            return end, last

        def middle_nodes(row):
            mid, scaled, rate = lv.coarse_rates(C_C1, row)
            new, _, new_rate = lv.coarse_rates(C_NEW, row)
            shift = [mid[s] - lv.at(cs, C_X1 + s, row) for s in range(2)]
            f1 = lv.moved_rates(shift, scaled, 0, N_RB, row)
            for s in range(2):
                old = lv.at(cs, C_END + s, row)
                lv.set(cp, N_LAST + s, row, old)
                lv.set(cp, N_F1 + s, row, f1[s])
                lv.put(cs, C_D1 + s, row, shift[s])
                lv.put(cs, C_END + s, row, mid[s] + HALF_STEP * rate[s] + lv.get(cp, N_K1 + s, row))
                change = HALF_STEP * new_rate[s] - lv.get(cp, N_G0 + s, row)
                lv.put(cs, C_E1 + s, row, (new[s] - old) + change)

        def end_nodes(now):
            def body(row):
                before = [lv.get(cp, N_RF2 + s, row) for s in range(2)]
                _, last = slice_end(now, row)
                change, laps = lv.laplacians(C_E1, row)
                old, new, j1s = [], [], []
                for s in range(2):
                    j0, j1 = integrals(before[s], lv.get(cp, N_F1 + s, row), last[s])
                    old.append(lv.get(cp, N_LAST + s, row) + j0)
                    new.append(old[s] + change[s])
                    j1s.append(j1)
                feed, both = lv.get(lv.cc, 0, row), lv.get(lv.cc, 1, row)
                lin = [lv.scaled(laps[s], 0.25 * (DIFF_U, DIFF_V)[s]) for s in range(2)]
                rate_new = lv.reacted(new[0], new[1], lin[0], lin[1], feed, both)
                rate_old = lv.reacted(old[0], old[1], 0.0, 0.0, feed, both)
                for s in range(2):
                    total = new[s] + j1s[s] + HALF_STEP * (rate_new[s] - rate_old[s])
                    lv.put(cs, C_NEW + s, row, total)

            return body

        def corrections(starts):
            def body(row):
                for k, first in enumerate(starts):
                    for s in range(2):
                        d = lv.at(cs, first + s, row)
                        ring = [lv.at(cs, first + s, row, -1), lv.at(cs, first + s, row, 1), lv.left(d), lv.right(d)]
                        north, south, west, east = (lv.scaled(x - d, (DIFF_U, DIFF_V)[s]) for x in ring)
                        for p, (a, b) in enumerate(PHASES):
                            lv.set(lv.tl, k * 8 + s * 4 + p, row, (south if a else north) + (east if b else west))

            return body

        lv.each(first_sweep)
        lv.each(second_sweep)
        lv.each(third_sweep)

        def one_slice(n, carry):
            lv.each(middle_nodes)
            lv.each(end_nodes(C_D2 + 2 * lax.rem(n, 2)))
            return carry

        lax.fori_loop(1, own + 1, one_slice, 0)

        first = own == 0
        now = C_D2 + 2 * lax.rem(own, 2)
        before = jnp.where(first, C_D1, 2 * C_D2 + 2 - now)
        origin = jnp.where(first, 0, 2)
        lv.each(corrections((before, C_D1, now)))

        def own_nodes(row):
            for p in range(4):
                for t in range(0, lv.lanes, 128):
                    lane = pl.ds(t, 128)
                    high = pl.ds(GUARD + row, 8)
                    low = pl.ds(row, 8)
                    feed, both = lv.coef[p, low, lane], lv.coef[4 + p, low, lane]
                    rates, start = [], None
                    for k, (base, d) in enumerate(((origin, before), (1, C_D1), (2, now))):
                        pair = [lv.fine[base * 8 + s * 4 + p, high, lane] + cs[d + s, high, lane] for s in range(2)]
                        lin = [lv.lin[base * 8 + s * 4 + p, low, lane] + lv.tl[k * 8 + s * 4 + p, low, lane] for s in range(2)]
                        rates.append(lv.reacted(pair[0], pair[1], lin[0], lin[1], feed, both))
                        start = pair if k == 0 else start
                    for s in range(2):
                        f0, f1, f2 = (r[s] for r in rates)
                        second = start[s] + (W0[0] * f0 + W0[1] * f1 + W0[2] * f2)
                        lv.put(lv.fine, 24 + s * 4 + p, row, second, lane)
                        lv.rest[s * 4 + p, low, lane] = second + (W1[0] * f0 + (W1[1] - HALF_STEP) * f1 + W1[2] * f2)

        lv.each(own_nodes)

        def last_node(row):
            _, _, rates = lv.fine_rates(3, row)
            for s in range(2):
                ends = [lv.get(lv.rest, s * 4 + p, row) + HALF_STEP * rates[p][s] for p in range(4)]
                fix = lv.at(cs, C_NEW + s, row) - lv.block_mean(ends)
                for p in range(4):
                    lv.set(lv.rest, s * 4 + p, row, ends[p] + fix)

        lv.each(last_node)


def load_planes(level, sources, columns, natural):
    count = level.lanes // 128
    matrix = group_matrix(count, False)
    slot = slots(count)
    for read, first in sources:
        blocks = []
        for k in range(count):
            values = [read(plane, k) for plane in range(4)]
            blocks.append(permuted(jnp.concatenate(values, axis=0), matrix))
        rows = blocks[0].shape[0] // 4
        for b in range(2):
            tiles = exchanged([block[:, 128 * b : 128 * b + 128] for block in blocks], slot)
            for q, tile in enumerate(tiles):
                for plane in range(4):
                    natural[plane, 2 * q + b, pl.ds(first, rows), :] = tile[plane * rows : (plane + 1) * rows]
    chunks = level.chunks
    for q in range(count):
        for p, (a, b) in enumerate(PHASES):
            for t in range(chunks):
                picked = [natural[plane, 2 * q + b, pl.ds(2 * t + a, 8, stride=2 * chunks), :] for plane in range(4)]
                lane, row = pl.ds(128 * q, 128), 8 * t
                for s in range(2):
                    level.fine[s * 4 + p, pl.ds(GUARD + row, 8), lane] = picked[s]
                level.coef[p, pl.ds(row, 8), lane] = picked[2]
                level.coef[4 + p, pl.ds(row, 8), lane] = picked[2] + picked[3]
    for plane in range(8):
        for row in {0, level.rows - 8}:
            level.put(level.fine, plane, row, level.at(level.fine, plane, row))


def spread(level, natural):
    count, chunks = level.lanes // 128, level.chunks
    for s in range(2):
        for q in range(count):
            for p, (a, b) in enumerate(PHASES):
                for t in range(chunks):
                    value = level.rest[s * 4 + p, pl.ds(8 * t, 8), pl.ds(128 * q, 128)]
                    natural[s, 2 * q + b, pl.ds(2 * t + a, 8, stride=2 * chunks), :] = value


def merged(level, first, rows, natural):
    count = level.lanes // 128
    matrix = group_matrix(count, True)
    slot = slots(count)
    halves = []
    for b in range(2):
        tiles = []
        for q in range(count):
            tiles.append(jnp.concatenate([natural[s, 2 * q + b, pl.ds(first, rows), :] for s in range(2)], axis=0))
        halves.append(exchanged(tiles, slot))
    blocks = [permuted(jnp.concatenate([halves[0][k], halves[1][k]], axis=1), matrix) for k in range(count)]
    return [[block[s * rows : (s + 1) * rows] for block in blocks] for s in range(2)]


def own_first(rows):
    return pl.multiple_of(lax.axis_index("gx") * rows, rows)


def source_list(refs, rows, parts):
    if parts == 2:
        mine = own_first(rows)
        state, feed, kill = refs[4:]
        other = [state.at[0], state.at[1], feed, kill]
        return [(refs[:4], mine), (other, pl.multiple_of(rows - mine, rows))]
    state, feed, kill = refs
    return [([state.at[g, 0], state.at[g, 1], feed.at[g], kill.at[g]], g * rows) for g in range(parts)]


def interior_kernel(parts, rows, columns, halo, depth, width, *refs):
    count, outs = (7, 3) if parts == 2 else (3, 2)
    ins, window, keep, give = refs[:count], refs[count], refs[count + 1], refs[count + 2]
    work = refs[count + outs :]
    here = columns // 2 if parts == 2 else columns
    origin = pl.multiple_of(lax.axis_index("gx") * here, here) if parts == 2 else 0
    level = Level(work[:-1], parts * rows // 2, here // 2, None)
    seam = 4 * depth if parts == 2 else 0
    side = (width - seam) // 2 - halo

    def reader(planes):
        return lambda plane, block: planes[plane][:, pl.ds(origin + 256 * block, 256)]

    sources = []
    for planes, first in source_list(ins, rows, parts):
        sources.append((reader(planes), first))
        for plane in range(4):
            value = planes[plane][...]
            cuts = [value[:, :halo], value[:, :side], value[:, (columns - seam) // 2 : (columns + seam) // 2]]
            cuts += [value[:, columns - side :], value[:, columns - halo :]]
            window[plane, pl.ds(first, rows), :] = jnp.concatenate([cut for cut in cuts if cut.shape[1]], axis=1)
    load_planes(level, sources, here, work[-1])
    level.run(lax.axis_index("ta"))
    spread(level, work[-1])
    mine = own_first(rows)
    targets = [(keep, mine), (give, pl.multiple_of(rows - mine, rows))] if parts == 2 else [(keep, mine)]
    for target, first in targets:
        natural = merged(level, first, rows, work[-1])
        for s in range(2):
            for k, block in enumerate(natural[s]):
                target[s, :, pl.ds(256 * k, 256)] = block


def border_kernel(parts, rows, halo, depth, width, window, from_a, from_b, out, *work):
    lanes = width // 2
    index, size = lax.axis_index("gy"), lax.axis_size("gy")
    even = lax.rem(index, 2) == 0
    tiles = lanes // 128
    at = lax.broadcasted_iota(jnp.int32, (1, lanes), 1)
    at = tiles * (at % 128) + at // 128
    outside = ((at < halo // 2) & (index == 0)) | ((at >= lanes - halo // 2) & (index == size - 1))
    level = Level(work[:-1], parts * rows // 2, lanes, jnp.where(outside, 0.0, 1.0))

    def reader(first):
        def read(plane, block):
            part = slice(halo * plane, halo * plane + halo)
            a, b = from_a[pl.ds(first, rows), :][:, part], from_b[pl.ds(first, rows), :][:, part]
            low, high = jnp.where(even, b, a), jnp.where(even, a, b)
            low, high = jnp.where(index == 0, 0.0, low), jnp.where(index == size - 1, 0.0, high)
            own = window[plane, pl.ds(first, rows), :]
            whole = jnp.concatenate([low, own[:, halo : width - halo], high], axis=1)
            return whole[:, 256 * block : 256 * block + 256]

        return read

    load_planes(level, [(reader(g * rows), g * rows) for g in range(parts)], width, work[-1])
    level.run(lax.axis_index("ta"))
    spread(level, work[-1])
    natural = merged(level, own_first(rows), rows, work[-1])
    for s in range(2):
        for k, block in enumerate(natural[s]):
            out[s, :, pl.ds(256 * k, 256)] = block


def final_kernel(halo, depth, width, *refs):
    inner, border, out = refs[:-2], refs[-2], refs[-1]
    total = out.shape[-1]
    share = total // len(inner)
    for k, value in enumerate(inner):
        origin = lax.axis_index("gx") * share
        origin = 0 if len(inner) == 1 else pl.multiple_of(origin if k == 0 else share - origin, share)
        out[0, :, :, pl.ds(origin, share)] = value[...]
    pieces = [(0, halo, depth), (total - depth, width - halo - depth, depth)]
    if len(inner) > 1:
        pieces.append((total // 2 - depth, width // 2 - depth, depth))
        pieces.append((total // 2, width // 2, depth))
    for s in range(2):
        whole = border[s]
        for column, source, size in pieces:
            low = column // 128 * 128
            high = round_up(column + size, 128)
            old = out[0, s, :, pl.ds(low, high - low)]
            parts_of = [old[:, : column - low], whole[:, source : source + size], old[:, column + size - low :]]
            out[0, s, :, pl.ds(low, high - low)] = jnp.concatenate([x for x in parts_of if x.shape[1]], axis=1)


def pack_kernel(parts, rows, halo, *refs):
    ins, to_a, to_b = refs[:-2], refs[-2], refs[-1]
    even = lax.rem(lax.axis_index("gy"), 2) == 0
    for planes, first in source_list(ins, rows, parts):
        total = planes[0].shape[-1]
        tile = round_up(halo, 128)
        low = jnp.concatenate([ref[:, pl.ds(0, tile)][:, :halo] for ref in planes], axis=1)
        high = jnp.concatenate([ref[:, pl.ds(total - tile, tile)][:, tile - halo :] for ref in planes], axis=1)
        to_a[pl.ds(first, rows), :] = jnp.where(even, high, low)
        to_b[pl.ds(first, rows), :] = jnp.where(even, low, high)


def fetch_kernel(state, feed, kill, *refs):
    planes, sems = refs[:4], refs[4]
    sources = (state.at[0], state.at[1], feed, kill)
    copies = [pltpu.make_async_copy(sources[i], planes[i], sems.at[i]) for i in range(4)]
    for copy in copies:
        copy.start()
    for copy in copies:
        copy.wait()


def both_ways(pairs):
    return [pair for low, high in pairs for pair in ((low, high), (high, low))]


VMEM = pl.BlockSpec(memory_space=pltpu.VMEM)
ANY = pl.BlockSpec(memory_space=pl.ANY)


def work_of(rows, lanes):
    shapes = scratch(rows, lanes) + [pltpu.VMEM((4, 2 * lanes // 128, 2 * rows, 128), F32)]
    size = sum(4 * math.prod(shape.shape) for shape in shapes)
    return shapes, size


def per_device(initial_state, feed_rate, kill_rate):
    slices, parts, blocks = (lax.axis_size(axis) for axis in ("ta", "gx", "gy"))
    _, rows, columns = initial_state.shape
    depth = 2 * (2 * slices + 2)
    halo = round_up(depth, 32)
    seam = 4 * depth if parts == 2 else 0
    width = round_up(2 * halo + 4 * depth + seam, 256)
    strip = round_up(halo, 128)
    every = parts * rows
    here = columns // 2 if parts == 2 else columns

    def across(value):
        if parts == 2:
            return [value, lax.ppermute(value, "gx", [(0, 1), (1, 0)])]
        return [lax.all_gather(value, "gx")]

    given = (initial_state, feed_rate, kill_rate)
    fields = [value for field in given for value in across(field)]
    if parts == 2:
        own = pl.pallas_call(
            fetch_kernel,
            out_shape=[jax.ShapeDtypeStruct((rows, columns), F32)] * 4,
            in_specs=[ANY] * 3,
            out_specs=[VMEM] * 4,
            scratch_shapes=[pltpu.SemaphoreType.DMA((4,))],
            compiler_params=pltpu.CompilerParams(vmem_limit_bytes=1709 * 2**15),
            name="fetch",
        )(*given)
        fields = [*own, *fields[1::2]]
    to_a, to_b = pl.pallas_call(
        functools.partial(pack_kernel, parts, rows, halo),
        out_shape=[jax.ShapeDtypeStruct((every, 4 * halo), F32)] * 2,
        in_specs=[VMEM] * len(fields),
        out_specs=[VMEM] * 2,
        compiler_params=pltpu.CompilerParams(vmem_limit_bytes=32 * every * columns + 2**22),
        name="pack",
    )(*fields)
    from_b = lax.ppermute(to_b, "gy", both_ways([(i, (i + 1) % blocks) for i in range(1, blocks - blocks % 2, 2)]))
    from_a = lax.ppermute(to_a, "gy", both_ways([(i, i + 1) for i in range(0, blocks - 1, 2)]))
    work, size = work_of(every // 2, here // 2)
    window, *inner = pl.pallas_call(
        functools.partial(interior_kernel, parts, rows, columns, halo, depth, width),
        out_shape=[jax.ShapeDtypeStruct((4, every, width), F32)]
        + [jax.ShapeDtypeStruct((2, rows, here), F32)] * (2 if parts == 2 else 1),
        in_specs=[VMEM] * len(fields),
        out_specs=[VMEM] * (3 if parts == 2 else 2),
        scratch_shapes=work,
        compiler_params=pltpu.CompilerParams(vmem_limit_bytes=size + 32 * every * (columns + width) + 2**22),
        cost_estimate=pl.CostEstimate(flops=40 * 2**20, bytes_accessed=20 * 2**20, transcendentals=0),
        name="interior",
    )(*fields)
    from_a, from_b, window, *inner = lax.optimization_barrier((from_a, from_b, window, *inner))
    if parts == 2:
        inner[1] = lax.ppermute(inner[1], "gx", [(0, 1), (1, 0)])
    work, size = work_of(every // 2, width // 2)
    border = pl.pallas_call(
        functools.partial(border_kernel, parts, rows, halo, depth, width),
        out_shape=jax.ShapeDtypeStruct((2, rows, width), F32),
        in_specs=[VMEM] * 3,
        out_specs=VMEM,
        scratch_shapes=work,
        compiler_params=pltpu.CompilerParams(vmem_limit_bytes=size + 32 * every * width + 2**23),
        cost_estimate=pl.CostEstimate(flops=10 * 2**20, bytes_accessed=10 * 2**20, transcendentals=0),
        name="border",
    )(window, from_a, from_b)
    return pl.pallas_call(
        functools.partial(final_kernel, halo, depth, width),
        out_shape=jax.ShapeDtypeStruct((1, 2, rows, columns), F32),
        in_specs=[VMEM] * (len(inner) + 1),
        out_specs=VMEM,
        compiler_params=pltpu.CompilerParams(vmem_limit_bytes=64 * rows * columns + 2**22),
        name="final",
    )(*inner, border)


def solution(mesh):
    placed = (P(None, "gx", "gy"), P("gx", "gy"), P("gx", "gy"))
    return jax.shard_map(
        per_device, mesh=mesh, in_specs=placed, out_specs=P("ta", None, "gx", "gy"), check_vma=False
    )
```

```python
import functools
import math

import jax
import jax.numpy as jnp
from jax import lax
from jax.experimental import pallas as pl
from jax.experimental.pallas import tpu as pltpu
from jax.sharding import PartitionSpec as P

TURNS = 2

DIFF_U = 0.2
DIFF_V = 0.1
HALF_STEP = 0.5
W0 = (5.0 / 24.0, 1.0 / 3.0, -1.0 / 24.0)
W1 = (-1.0 / 24.0, 1.0 / 3.0, 5.0 / 24.0)
GUARD = 8
F32 = jnp.float32
BF16 = jnp.bfloat16
PHASES = ((0, 0), (0, 1), (1, 0), (1, 1))


def round_up(value, step):
    return -(-value // step) * step


def thirds(value):
    high = value.astype(BF16)
    rest = value - high.astype(F32)
    middle = rest.astype(BF16)
    low = (rest - middle.astype(F32)).astype(BF16)
    return high, middle, low


def permuted(value, matrix):
    rows = value.shape[0]
    parts = jnp.concatenate(thirds(value), axis=0)
    moved = jnp.dot(parts, matrix, preferred_element_type=F32)
    return (moved[2 * rows :] + moved[rows : 2 * rows]) + moved[:rows]


def group_matrix(tiles, inverse):
    group = 128 // tiles
    natural = lax.broadcasted_iota(jnp.int32, (256, 256), 1 if inverse else 0)
    grouped = lax.broadcasted_iota(jnp.int32, (256, 256), 0 if inverse else 1)
    wanted = 2 * tiles * (grouped % group) + 2 * ((grouped % 128) // group) + grouped // 128
    return jnp.where(natural == wanted, 1.0, 0.0).astype(BF16)


def exchanged(tiles, slot):
    count = len(tiles)
    if count == 1:
        return tiles
    group = 128 // count
    turned = [pltpu.roll(tile, k * group, 1) if k else tile for k, tile in enumerate(tiles)]
    results = []
    for q in range(count):
        value = turned[(count - q) % count]
        for at in range(1, count):
            value = jnp.where(slot == at, turned[(at - q) % count], value)
        results.append(pltpu.roll(value, (count - q) * group, 1) if q else value)
    return results


def slots(tiles):
    return lax.broadcasted_iota(jnp.int32, (1, 128), 1) // (128 // tiles)


C_X0, C_X1, C_X2, C_END, C_C1, C_NEW, C_E1, C_D1, C_D2 = (2 * i for i in range(9))
COARSE_STENCIL = 20
N_LAST, N_K0, N_K1, N_G0, N_RA, N_RB, N_RE, N_F1, N_RF2 = (2 * i for i in range(9))
COARSE_PLAIN = 18


def state_shapes(rows, lanes):
    guarded = rows + 2 * GUARD
    return [
        (24, guarded, lanes),
        (24, rows, lanes),
        (8, rows, lanes),
        (COARSE_STENCIL, guarded, lanes),
        (COARSE_PLAIN, rows, lanes),
        (2, rows, lanes),
        (8, rows, lanes),
    ]


def late_shapes(rows, lanes):
    return [
        (8, rows + 2 * GUARD, lanes),
        (8, rows, lanes),
        (24, rows, lanes),
    ]


def natural_shape(rows, lanes):
    return (4, 2 * lanes // 128, 2 * rows, 128)


class Level:
    def __init__(self, refs, rows, lanes, mask):
        self.fine, self.lin, self.coef, self.cs, self.cp, self.cc, self.mom, *late = refs
        self.fresh, self.rest, self.tl = late or (None, None, None)
        self.rows, self.lanes, self.mask = rows, lanes, mask
        self.chunks = rows // 8

    def each(self, body):
        if self.chunks <= 4:
            for i in range(self.chunks):
                body(8 * i)
        else:
            pl.loop(0, self.chunks)(lambda i: body(pl.multiple_of(8 * i, 8)))

    def left(self, value):
        if self.lanes == 128:
            return pltpu.roll(value, 1, 1)
        return jnp.concatenate([pltpu.roll(value[:, -128:], 1, 1), value[:, :-128]], axis=1)

    def right(self, value):
        if self.lanes == 128:
            return pltpu.roll(value, 127, 1)
        return jnp.concatenate([value[:, 128:], pltpu.roll(value[:, :128], 127, 1)], axis=1)

    def scaled(self, value, factor):
        if self.mask is None:
            return factor * value
        return (factor * self.mask) * value

    def at(self, ref, plane, row, shift=0):
        return ref[plane, pl.ds(GUARD + row + 8 * shift, 8), :]

    def put(self, ref, plane, row, value, lane=slice(None)):
        ref[plane, pl.ds(GUARD + row, 8), lane] = value
        sublane = lax.broadcasted_iota(jnp.int32, (8, 1), 0)
        last = self.rows - 8

        def top():
            ref[plane, pl.ds(0, 8), lane] = jnp.where(sublane == 0, 0.0, pltpu.roll(value, 1, 0))

        def bottom():
            ref[plane, pl.ds(GUARD + self.rows, 8), lane] = jnp.where(sublane == 7, 0.0, pltpu.roll(value, 7, 0))

        for edge, fill in ((last, top), (0, bottom)):
            if not isinstance(row, int):
                pl.when(row == edge)(fill)
            elif row == edge:
                fill()

    def get(self, ref, plane, row):
        return ref[plane, pl.ds(row, 8), :]

    def set(self, ref, plane, row, value):
        ref[plane, pl.ds(row, 8), :] = value

    def fine_rates(self, base, row):
        ref, base = (self.fresh, 0) if base == 3 else (self.fine, base)
        state = [[self.at(ref, base * 8 + s * 4 + p, row) for p in range(4)] for s in range(2)]
        linear, rates = [], []
        for p, (a, b) in enumerate(PHASES):
            laps = []
            for s in range(2):
                across = state[s][2 * a + 1 - b]
                along = state[s][2 * (1 - a) + b]
                moved = self.at(ref, base * 8 + s * 4 + 2 * (1 - a) + b, row, 1 if a else -1)
                side = self.right(across) if b else self.left(across)
                laps.append((along + moved) + (across + side) - 4.0 * state[s][p])
            u, v = state[0][p], state[1][p]
            feed = self.get(self.coef, p, row)
            both = self.get(self.coef, 4 + p, row)
            lin_u = self.scaled(laps[0], DIFF_U) + feed
            lin_v = self.scaled(laps[1], DIFF_V)
            linear.append((lin_u, lin_v))
            rates.append(self.reacted(u, v, lin_u, lin_v, feed, both))
        return state, linear, rates

    def reacted(self, u, v, lin_u, lin_v, feed, both):
        return lin_u - u * (feed + v * v), lin_v + v * (u * v - both)

    def neighbours(self, plane, row, value):
        rows = self.at(self.cs, plane, row, -1) + self.at(self.cs, plane, row, 1)
        return rows + (self.left(value) + self.right(value))

    def laplacians(self, first, row):
        pair = [self.at(self.cs, first + s, row) for s in range(2)]
        return pair, [self.neighbours(first + s, row, pair[s]) - 4.0 * pair[s] for s in range(2)]

    def coarse_rates(self, first, row):
        (u, v), laps = self.laplacians(first, row)
        scaled = [self.scaled(laps[s], 0.25 * (DIFF_U, DIFF_V)[s]) for s in range(2)]
        feed, both = self.get(self.cc, 0, row), self.get(self.cc, 1, row)
        return (u, v), scaled, self.reacted(u, v, scaled[0] + feed, scaled[1], feed, both)

    def moved_rates(self, shift, scaled, which, base, row):
        a, b = shift
        m_vv, m_uv, m_u, m_v = (self.get(self.mom, 4 * which + k, row) for k in range(4))
        react = a * (m_vv + b * (2.0 * m_v + b)) + b * (2.0 * m_uv + b * m_u)
        feed, both = self.get(self.cc, 0, row), self.get(self.cc, 1, row)
        rate_u = (self.get(self.cp, base, row) + 2.0 * scaled[0]) - (feed * a + react)
        rate_v = (self.get(self.cp, base + 1, row) + 2.0 * scaled[1]) + (react - both * b)
        return rate_u, rate_v

    def block_mean(self, values):
        return 0.25 * ((values[0] + values[1]) + (values[2] + values[3]))

    def run(self, own, start=True, finish=True):
        lv = self
        cs, cp = self.cs, self.cp

        def first_sweep(row):
            for k in range(2):
                lv.set(lv.cc, k, row, lv.block_mean([lv.get(lv.coef, 4 * k + p, row) for p in range(4)]))
            state, linear, rates = lv.fine_rates(0, row)
            for s in range(2):
                for p in range(4):
                    lv.set(lv.lin, s * 4 + p, row, linear[p][s])
                    lv.put(lv.fine, 8 + s * 4 + p, row, state[s][p] + HALF_STEP * rates[p][s])
                mean = lv.block_mean([r[s] for r in rates])
                start = lv.block_mean(state[s])
                lv.set(cp, N_RA + s, row, mean)
                lv.put(cs, C_X0 + s, row, start)
                lv.put(cs, C_X1 + s, row, start + HALF_STEP * mean)
                lv.put(cs, C_END + s, row, start + mean)
                lv.put(cs, C_D1 + s, row, jnp.zeros_like(mean))

        def moments(which, state, row):
            u, v = state
            lv.set(lv.mom, 4 * which, row, lv.block_mean([v[p] * v[p] for p in range(4)]))
            lv.set(lv.mom, 4 * which + 1, row, lv.block_mean([u[p] * v[p] for p in range(4)]))
            lv.set(lv.mom, 4 * which + 2, row, lv.block_mean(u))
            lv.set(lv.mom, 4 * which + 3, row, lv.block_mean(v))

        def second_sweep(row):
            state, linear, rates = lv.fine_rates(1, row)
            _, _, g0 = lv.coarse_rates(C_X0, row)
            first, scaled, g1 = lv.coarse_rates(C_X1, row)
            for s in range(2):
                for p in range(4):
                    lv.set(lv.lin, 8 + s * 4 + p, row, linear[p][s])
                    lv.put(lv.fine, 16 + s * 4 + p, row, state[s][p] + HALF_STEP * rates[p][s])
                mean = lv.block_mean([r[s] for r in rates])
                lv.set(cp, N_F1 + s, row, mean)
                lv.set(cp, N_RB + s, row, mean - 2.0 * scaled[s])
                lv.put(cs, C_X2 + s, row, first[s] + HALF_STEP * mean)
                integral = HALF_STEP * lv.get(cp, N_RA + s, row)
                lv.set(cp, N_K0 + s, row, integral - HALF_STEP * g0[s])
                lv.set(cp, N_K1 + s, row, integral - HALF_STEP * g1[s])
            moments(0, state, row)

        def third_sweep(row):
            state, linear, rates = lv.fine_rates(2, row)
            for s in range(2):
                for p in range(4):
                    lv.set(lv.lin, 16 + s * 4 + p, row, linear[p][s])
            moments(1, state, row)
            second, laps = lv.laplacians(C_X2, row)
            for s in range(2):
                mean = lv.block_mean([r[s] for r in rates])
                lv.set(cp, N_RE + s, row, mean - lv.scaled(laps[s], 0.5 * (DIFF_U, DIFF_V)[s]))
            end, last = slice_end(C_D2, row)
            for s in range(2):
                j0, j1 = integrals(lv.get(cp, N_RA + s, row), lv.get(cp, N_F1 + s, row), last[s])
                lv.put(cs, C_NEW + s, row, lv.at(cs, C_X0 + s, row) + (j0 + j1))

        def integrals(f0, f1, f2):
            middle = W0[1] * f1
            return middle + (W0[0] * f0 + W0[2] * f2), middle + (W1[0] * f0 + W1[2] * f2)

        def slice_end(now, row):
            end, scaled, rate = lv.coarse_rates(C_END, row)
            shift = [end[s] - lv.at(cs, C_X2 + s, row) for s in range(2)]
            last = lv.moved_rates(shift, scaled, 1, N_RE, row)
            for s in range(2):
                half = HALF_STEP * rate[s]
                lv.set(cp, N_G0 + s, row, half)
                lv.put(cs, C_C1 + s, row, end[s] + half + lv.get(cp, N_K0 + s, row))
                lv.put(cs, now + s, row, shift[s])
                lv.set(cp, N_RF2 + s, row, last[s])
            return end, last

        def middle_nodes(row):
            mid, scaled, rate = lv.coarse_rates(C_C1, row)
            new, _, new_rate = lv.coarse_rates(C_NEW, row)
            shift = [mid[s] - lv.at(cs, C_X1 + s, row) for s in range(2)]
            f1 = lv.moved_rates(shift, scaled, 0, N_RB, row)
            for s in range(2):
                old = lv.at(cs, C_END + s, row)
                lv.set(cp, N_LAST + s, row, old)
                lv.set(cp, N_F1 + s, row, f1[s])
                lv.put(cs, C_D1 + s, row, shift[s])
                lv.put(cs, C_END + s, row, mid[s] + HALF_STEP * rate[s] + lv.get(cp, N_K1 + s, row))
                change = HALF_STEP * new_rate[s] - lv.get(cp, N_G0 + s, row)
                lv.put(cs, C_E1 + s, row, (new[s] - old) + change)

        def end_nodes(now):
            def body(row):
                before = [lv.get(cp, N_RF2 + s, row) for s in range(2)]
                _, last = slice_end(now, row)
                change, laps = lv.laplacians(C_E1, row)
                old, new, j1s = [], [], []
                for s in range(2):
                    j0, j1 = integrals(before[s], lv.get(cp, N_F1 + s, row), last[s])
                    old.append(lv.get(cp, N_LAST + s, row) + j0)
                    new.append(old[s] + change[s])
                    j1s.append(j1)
                feed, both = lv.get(lv.cc, 0, row), lv.get(lv.cc, 1, row)
                lin = [lv.scaled(laps[s], 0.25 * (DIFF_U, DIFF_V)[s]) for s in range(2)]
                rate_new = lv.reacted(new[0], new[1], lin[0], lin[1], feed, both)
                rate_old = lv.reacted(old[0], old[1], 0.0, 0.0, feed, both)
                for s in range(2):
                    total = new[s] + j1s[s] + HALF_STEP * (rate_new[s] - rate_old[s])
                    lv.put(cs, C_NEW + s, row, total)

            return body

        def corrections(starts):
            def body(row):
                for k, first in enumerate(starts):
                    for s in range(2):
                        d = lv.at(cs, first + s, row)
                        ring = [lv.at(cs, first + s, row, -1), lv.at(cs, first + s, row, 1), lv.left(d), lv.right(d)]
                        north, south, west, east = (lv.scaled(x - d, (DIFF_U, DIFF_V)[s]) for x in ring)
                        for p, (a, b) in enumerate(PHASES):
                            lv.set(lv.tl, k * 8 + s * 4 + p, row, (south if a else north) + (east if b else west))

            return body

        if start:
            lv.each(first_sweep)
            lv.each(second_sweep)
            lv.each(third_sweep)

        def one_slice(n, carry):
            lv.each(middle_nodes)
            lv.each(end_nodes(C_D2 + 2 * lax.rem(n, 2)))
            return carry

        if start:
            lax.fori_loop(1, own + 1, one_slice, 0)
        if not finish:
            return

        first = own == 0
        now = C_D2 + 2 * lax.rem(own, 2)
        before = jnp.where(first, C_D1, 2 * C_D2 + 2 - now)
        origin = jnp.where(first, 0, 2)
        lv.each(corrections((before, C_D1, now)))

        def own_nodes(row):
            for p in range(4):
                for t in range(0, lv.lanes, 128):
                    lane = pl.ds(t, 128)
                    high = pl.ds(GUARD + row, 8)
                    low = pl.ds(row, 8)
                    feed, both = lv.coef[p, low, lane], lv.coef[4 + p, low, lane]
                    rates, start = [], None
                    for k, (base, d) in enumerate(((origin, before), (1, C_D1), (2, now))):
                        pair = [lv.fine[base * 8 + s * 4 + p, high, lane] + cs[d + s, high, lane] for s in range(2)]
                        lin = [lv.lin[base * 8 + s * 4 + p, low, lane] + lv.tl[k * 8 + s * 4 + p, low, lane] for s in range(2)]
                        rates.append(lv.reacted(pair[0], pair[1], lin[0], lin[1], feed, both))
                        start = pair if k == 0 else start
                    for s in range(2):
                        f0, f1, f2 = (r[s] for r in rates)
                        second = start[s] + (W0[0] * f0 + W0[1] * f1 + W0[2] * f2)
                        lv.put(lv.fresh, s * 4 + p, row, second, lane)
                        lv.rest[s * 4 + p, low, lane] = second + (W1[0] * f0 + (W1[1] - HALF_STEP) * f1 + W1[2] * f2)

        lv.each(own_nodes)

        def last_node(row):
            _, _, rates = lv.fine_rates(3, row)
            for s in range(2):
                ends = [lv.get(lv.rest, s * 4 + p, row) + HALF_STEP * rates[p][s] for p in range(4)]
                fix = lv.at(cs, C_NEW + s, row) - lv.block_mean(ends)
                for p in range(4):
                    lv.set(lv.rest, s * 4 + p, row, ends[p] + fix)

        lv.each(last_node)


def load_planes(level, sources, columns, natural):
    count = level.lanes // 128
    matrix = group_matrix(count, False)
    slot = slots(count)
    for read, first in sources:
        blocks = []
        for k in range(count):
            values = [read(plane, k) for plane in range(4)]
            blocks.append(permuted(jnp.concatenate(values, axis=0), matrix))
        rows = blocks[0].shape[0] // 4
        for b in range(2):
            tiles = exchanged([block[:, 128 * b : 128 * b + 128] for block in blocks], slot)
            for q, tile in enumerate(tiles):
                for plane in range(4):
                    natural[plane, 2 * q + b, pl.ds(first, rows), :] = tile[plane * rows : (plane + 1) * rows]
    chunks = level.chunks
    for q in range(count):
        for p, (a, b) in enumerate(PHASES):
            for t in range(chunks):
                picked = [natural[plane, 2 * q + b, pl.ds(2 * t + a, 8, stride=2 * chunks), :] for plane in range(4)]
                lane, row = pl.ds(128 * q, 128), 8 * t
                for s in range(2):
                    level.fine[s * 4 + p, pl.ds(GUARD + row, 8), lane] = picked[s]
                level.coef[p, pl.ds(row, 8), lane] = picked[2]
                level.coef[4 + p, pl.ds(row, 8), lane] = picked[2] + picked[3]
    for plane in range(8):
        for row in {0, level.rows - 8}:
            level.put(level.fine, plane, row, level.at(level.fine, plane, row))


def spread(level, natural):
    count, chunks = level.lanes // 128, level.chunks
    for s in range(2):
        for q in range(count):
            for p, (a, b) in enumerate(PHASES):
                for t in range(chunks):
                    value = level.rest[s * 4 + p, pl.ds(8 * t, 8), pl.ds(128 * q, 128)]
                    natural[s, 2 * q + b, pl.ds(2 * t + a, 8, stride=2 * chunks), :] = value


def merged(level, first, rows, natural):
    count = level.lanes // 128
    matrix = group_matrix(count, True)
    slot = slots(count)
    halves = []
    for b in range(2):
        tiles = []
        for q in range(count):
            tiles.append(jnp.concatenate([natural[s, 2 * q + b, pl.ds(first, rows), :] for s in range(2)], axis=0))
        halves.append(exchanged(tiles, slot))
    blocks = [permuted(jnp.concatenate([halves[0][k], halves[1][k]], axis=1), matrix) for k in range(count)]
    return [[block[s * rows : (s + 1) * rows] for block in blocks] for s in range(2)]


def own_first(rows):
    return pl.multiple_of(lax.axis_index("gx") * rows, rows)


def source_list(refs, rows, parts):
    if parts == 2:
        mine = own_first(rows)
        state, feed, kill = refs[4:]
        other = [state.at[0], state.at[1], feed, kill]
        return [(refs[:4], mine), (other, pl.multiple_of(rows - mine, rows))]
    state, feed, kill = refs
    return [([state.at[g, 0], state.at[g, 1], feed.at[g], kill.at[g]], g * rows) for g in range(parts)]


def interior_kernel(parts, rows, columns, halo, depth, width, start, finish, *refs):
    refs = list(refs)
    take = lambda count: [refs.pop(0) for _ in range(count)]
    here = columns // 2 if parts == 2 else columns
    origin = pl.multiple_of(lax.axis_index("gx") * here, here) if parts == 2 else 0
    seam = 4 * depth if parts == 2 else 0
    side = (width - seam) // 2 - halo
    ins = take(7 if parts == 2 else 3) if start else []
    given = [] if start else take(7)
    window = take(1)[0] if start else None
    outs = take(2 if parts == 2 else 1) if finish else []
    state = take(7) if start else given
    late = take(3) if finish else []
    (natural,) = take(1)
    level = Level(state + late, parts * rows // 2, here // 2, None)

    def reader(planes):
        return lambda plane, block: planes[plane][:, pl.ds(origin + 256 * block, 256)]

    if start:
        sources = []
        for planes, first in source_list(ins, rows, parts):
            sources.append((reader(planes), first))
            for plane in range(4):
                value = planes[plane][...]
                cuts = [value[:, :halo], value[:, :side], value[:, (columns - seam) // 2 : (columns + seam) // 2]]
                cuts += [value[:, columns - side :], value[:, columns - halo :]]
                window[plane, pl.ds(first, rows), :] = jnp.concatenate([cut for cut in cuts if cut.shape[1]], axis=1)
        load_planes(level, sources, here, natural)
    level.run(lax.axis_index("ta"), start, finish)
    if finish:
        spread(level, natural)
        mine = own_first(rows)
        firsts = [mine, pl.multiple_of(rows - mine, rows)] if parts == 2 else [mine]
        for target, first in zip(outs, firsts):
            blocks = merged(level, first, rows, natural)
            for s in range(2):
                for k, block in enumerate(blocks[s]):
                    target[s, :, pl.ds(256 * k, 256)] = block


def border_kernel(parts, rows, halo, depth, width, window, near, far, out, *work):
    lanes = width // 2
    index, size = lax.axis_index("gy"), lax.axis_size("gy")
    swap = lax.rem(index, 2) == 0
    if parts == 2:
        swap = swap == (lax.axis_index("gx") == 0)
    tiles = lanes // 128
    at = lax.broadcasted_iota(jnp.int32, (1, lanes), 1)
    at = tiles * (at % 128) + at // 128
    outside = ((at < halo // 2) & (index == 0)) | ((at >= lanes - halo // 2) & (index == size - 1))
    level = Level(work[:-1], parts * rows // 2, lanes, jnp.where(outside, 0.0, 1.0))

    def reader(first):
        def read(plane, block):
            part = slice(halo * plane, halo * plane + halo)
            a, b = near[pl.ds(first, rows), :][:, part], far[pl.ds(first, rows), :][:, part]
            low, high = jnp.where(swap, b, a), jnp.where(swap, a, b)
            low, high = jnp.where(index == 0, 0.0, low), jnp.where(index == size - 1, 0.0, high)
            own = window[plane, pl.ds(first, rows), :]
            whole = jnp.concatenate([low, own[:, halo : width - halo], high], axis=1)
            return whole[:, 256 * block : 256 * block + 256]

        return read

    load_planes(level, [(reader(g * rows), g * rows) for g in range(parts)], width, work[-1])
    level.run(lax.axis_index("ta"))
    spread(level, work[-1])
    natural = merged(level, own_first(rows), rows, work[-1])
    for s in range(2):
        for k, block in enumerate(natural[s]):
            out[s, :, pl.ds(256 * k, 256)] = block


def final_kernel(halo, depth, width, *refs):
    inner, border, out = refs[:-2], refs[-2], refs[-1]
    total = out.shape[-1]
    share = total // len(inner)
    for k, value in enumerate(inner):
        origin = lax.axis_index("gx") * share
        origin = 0 if len(inner) == 1 else pl.multiple_of(origin if k == 0 else share - origin, share)
        out[0, :, :, pl.ds(origin, share)] = value[...]
    pieces = [(0, halo, depth), (total - depth, width - halo - depth, depth)]
    if len(inner) > 1:
        pieces.append((total // 2 - depth, width // 2 - depth, depth))
        pieces.append((total // 2, width // 2, depth))
    for s in range(2):
        whole = border[s]
        for column, source, size in pieces:
            low = column // 128 * 128
            high = round_up(column + size, 128)
            old = out[0, s, :, pl.ds(low, high - low)]
            parts_of = [old[:, : column - low], whole[:, source : source + size], old[:, column + size - low :]]
            out[0, s, :, pl.ds(low, high - low)] = jnp.concatenate([x for x in parts_of if x.shape[1]], axis=1)


def pack_kernel(parts, rows, halo, *refs):
    count = 7 if parts == 2 else 3
    ins, outs = refs[:count], refs[count:]
    even = lax.rem(lax.axis_index("gy"), 2) == 0
    if parts == 2:
        even = even == (lax.axis_index("gx") == 0)
    for planes, first in source_list(ins, rows, parts):
        total = planes[0].shape[-1]
        tile = round_up(halo, 128)
        low = jnp.concatenate([ref[:, pl.ds(0, tile)][:, :halo] for ref in planes], axis=1)
        high = jnp.concatenate([ref[:, pl.ds(total - tile, tile)][:, tile - halo :] for ref in planes], axis=1)
        for k, out in enumerate(outs):
            out[pl.ds(first, rows), :] = jnp.where(even, low, high) if k else jnp.where(even, high, low)


def fetch_kernel(state, feed, kill, *refs):
    planes, sems = refs[:4], refs[4]
    sources = (state.at[0], state.at[1], feed, kill)
    copies = [pltpu.make_async_copy(sources[i], planes[i], sems.at[i]) for i in range(4)]
    for copy in copies:
        copy.start()
    for copy in copies:
        copy.wait()


def both_ways(pairs):
    return [pair for low, high in pairs for pair in ((low, high), (high, low))]


VMEM = pl.BlockSpec(memory_space=pltpu.VMEM)
ANY = pl.BlockSpec(memory_space=pl.ANY)


def arrays(shapes):
    return [jax.ShapeDtypeStruct(shape, F32) for shape in shapes]


def buffers(shapes):
    return [pltpu.VMEM(shape, F32) for shape in shapes]


def size_of(shapes):
    return sum(4 * math.prod(shape) for shape in shapes)


def called(name, kernel, outs, scratch, limit, inputs, specs=VMEM, flops=0):
    return pl.pallas_call(
        kernel,
        out_shape=outs,
        in_specs=[specs] * len(inputs),
        out_specs=[VMEM] * len(outs),
        scratch_shapes=scratch,
        compiler_params=pltpu.CompilerParams(vmem_limit_bytes=limit),
        cost_estimate=pl.CostEstimate(flops=flops, bytes_accessed=flops // 2, transcendentals=0),
        name=name,
    )(*inputs)


def per_device(initial_state, feed_rate, kill_rate):
    slices, parts, blocks = (lax.axis_size(axis) for axis in ("ta", "gx", "gy"))
    _, rows, columns = initial_state.shape
    depth = 2 * (2 * slices + 2)
    halo = round_up(depth, 32)
    seam = 4 * depth if parts == 2 else 0
    width = round_up(2 * halo + 4 * depth + seam, 256)
    every = parts * rows
    here = columns // 2 if parts == 2 else columns
    given = (initial_state, feed_rate, kill_rate)
    plane_bytes = 4 * every * columns

    low_pairs = both_ways([(i, i + 1) for i in range(0, blocks - 1, 2)])
    high_pairs = both_ways([(i, (i + 1) % blocks) for i in range(1, blocks - blocks % 2, 2)])

    def crossed(value):
        return lax.ppermute(value, "gx", [(0, 1), (1, 0)])

    if parts == 2:
        others = [crossed(value) for value in given]
        limit = 1709 * 2**15
        own = called("fetch", fetch_kernel, arrays([(rows, columns)] * 4), [pltpu.SemaphoreType.DMA((4,))], limit, given, ANY)
        fields = [*own, *others]
    else:
        fields = [lax.all_gather(value, "gx") for value in given]
    pack = functools.partial(pack_kernel, parts, rows, halo)
    sent = called("pack", pack, arrays([(every, 4 * halo)] * (1 if parts == 2 else 2)), [], 8 * plane_bytes + 2**22, fields)
    if parts == 2:
        pairs = low_pairs + [(blocks + source, blocks + target) for source, target in high_pairs]
        near = lax.ppermute(sent[0], ("gx", "gy"), pairs)
    else:
        near = lax.ppermute(sent[0], "gy", low_pairs)
        far = lax.ppermute(sent[1], "gy", high_pairs)

    state, late = state_shapes(every // 2, here // 2), late_shapes(every // 2, here // 2)
    natural = natural_shape(every // 2, here // 2)
    limit = size_of(state + late + [natural]) + 32 * every * (columns + width) + 2**22
    interior = functools.partial(interior_kernel, parts, rows, columns, halo, depth, width)
    window_shape = (4, every, width)
    result_shape = (2, rows, here)
    if parts == 2:
        first = functools.partial(interior, True, False)
        made = called("interior", first, arrays([window_shape] + state), buffers([natural]), limit, fields, flops=2**24)
        near, window, *made = lax.optimization_barrier((near, *made))
        far = crossed(near)
        last = functools.partial(interior, False, True)
        keep, give = called("own", last, arrays([result_shape] * 2), buffers(late + [natural]), limit, made, flops=2**23)
        far, give = lax.optimization_barrier((far, give))
        inner = [keep, crossed(give)]
    else:
        whole = functools.partial(interior, True, True)
        scratch = buffers(state + late + [natural])
        window, *inner = called("interior", whole, arrays([window_shape, result_shape]), scratch, limit, fields, flops=2**24)
    work = state_shapes(every // 2, width // 2) + late_shapes(every // 2, width // 2)
    work.append(natural_shape(every // 2, width // 2))
    limit = size_of(work) + 32 * every * width + 2**23
    border = functools.partial(border_kernel, parts, rows, halo, depth, width)
    (edges,) = called("border", border, arrays([(2, rows, width)]), buffers(work), limit, (window, near, far), flops=2**23)
    final = functools.partial(final_kernel, halo, depth, width)
    (out,) = called("final", final, arrays([(1, 2, rows, columns)]), [], 16 * plane_bytes + 2**22, (*inner, edges))
    return out


def solution(mesh):
    placed = (P(None, "gx", "gy"), P("gx", "gy"), P("gx", "gy"))
    return jax.shard_map(
        per_device, mesh=mesh, in_specs=placed, out_specs=P("ta", None, "gx", "gy"), check_vma=False
    )
```

```python
import functools
import math

import jax
import jax.numpy as jnp
from jax import lax
from jax.experimental import pallas as pl
from jax.experimental.pallas import tpu as pltpu
from jax.sharding import PartitionSpec as P

TURNS = 2

DIFF_U = 0.2
DIFF_V = 0.1
HALF_STEP = 0.5
W0 = (5.0 / 24.0, 1.0 / 3.0, -1.0 / 24.0)
W1 = (-1.0 / 24.0, 1.0 / 3.0, 5.0 / 24.0)
F32 = jnp.float32
BF16 = jnp.bfloat16
PHASES = ((0, 0), (0, 1), (1, 0), (1, 1))


def round_up(value, step):
    return -(-value // step) * step


def thirds(value):
    high = value.astype(BF16)
    rest = value - high.astype(F32)
    middle = rest.astype(BF16)
    low = (rest - middle.astype(F32)).astype(BF16)
    return high, middle, low


def permuted(value, matrix):
    rows = value.shape[0]
    parts = jnp.concatenate(thirds(value), axis=0)
    moved = jnp.dot(parts, matrix, preferred_element_type=F32)
    return (moved[2 * rows :] + moved[rows : 2 * rows]) + moved[:rows]


def group_matrix(tiles, inverse):
    group, bits = 128 // tiles, (tiles - 1).bit_length()
    source = lax.broadcasted_iota(jnp.int32, (256, 256), 0)
    target = lax.broadcasted_iota(jnp.int32, (1, 256), 1)
    if inverse:
        wanted = ((target & 1) << 7) + (((target >> 1) & (tiles - 1)) << (7 - bits)) + (target >> (1 + bits))
    else:
        wanted = ((target & (group - 1)) << (1 + bits)) + (((target & 127) >> (7 - bits)) << 1) + (target >> 7)
    return jnp.where(source == wanted, 1.0, 0.0).astype(BF16)


def exchanged(tiles, slot):
    count = len(tiles)
    if count == 1:
        return tiles
    group = 128 // count
    turned = [pltpu.roll(tile, k * group, 1) if k else tile for k, tile in enumerate(tiles)]
    results = []
    for q in range(count):
        value = turned[(count - q) % count]
        for at in range(1, count):
            value = jnp.where(slot == at, turned[(at - q) % count], value)
        results.append(pltpu.roll(value, (count - q) * group, 1) if q else value)
    return results


def slots(tiles):
    return lax.broadcasted_iota(jnp.int32, (1, 128), 1) >> (7 - (tiles - 1).bit_length())


C_X0, C_X1, C_X2, C_END, C_C1, C_NEW, C_E1, C_D1, C_D2, C_D2_BEFORE = (2 * i for i in range(10))
COARSE_STENCIL = 20
N_LAST, N_K0, N_K1, N_G0, N_RA, N_RB, N_RE, N_F1, N_RF2 = (2 * i for i in range(9))
COARSE_PLAIN = 18


def state_shapes(rows, lanes):
    return [
        (24, rows, lanes),
        (24, rows, lanes),
        (8, rows, lanes),
        (COARSE_STENCIL, rows, lanes),
        (COARSE_PLAIN, rows, lanes),
        (2, rows, lanes),
        (8, rows, lanes),
    ]


def late_shapes(rows, lanes):
    return [
        (8, rows, lanes),
        (8, rows, lanes),
        (24, rows, lanes),
    ]


def natural_shape(rows, lanes):
    return (4, 2 * lanes // 128, 2 * rows, 128)


class Level:
    def __init__(self, refs, rows, lanes, mask):
        self.fine, self.lin, self.coef, self.cs, self.cp, self.cc, self.mom, *late = refs
        self.fresh, self.rest, self.tl = late or (None, None, None)
        self.rows, self.lanes, self.mask = rows, lanes, mask
        self.chunks = rows // 8

    def each(self, body):
        if self.chunks <= 4:
            for i in range(self.chunks):
                body(8 * i)
        else:
            pl.loop(0, self.chunks)(lambda i: body(pl.multiple_of(8 * i, 8)))

    def left(self, value):
        if self.lanes == 128:
            return pltpu.roll(value, 1, 1)
        return jnp.concatenate([pltpu.roll(value[:, -128:], 1, 1), value[:, :-128]], axis=1)

    def right(self, value):
        if self.lanes == 128:
            return pltpu.roll(value, 127, 1)
        return jnp.concatenate([value[:, 128:], pltpu.roll(value[:, :128], 127, 1)], axis=1)

    def scaled(self, value, factor):
        if self.mask is None:
            return factor * value
        return (factor * self.mask) * value

    def at(self, ref, plane, row, shift=0):
        target = row + 8 * shift
        if isinstance(row, int) and 0 <= target < self.rows:
            return ref[plane, pl.ds(target, 8), :]
        sublane = lax.broadcasted_iota(jnp.int32, (8, 1), 0)
        if isinstance(row, int):
            value = ref[plane, pl.ds(target % self.rows, 8), :]
            return jnp.where(sublane == (0 if shift < 0 else 7), 0.0, pltpu.roll(value, 1 if shift < 0 else 7, 0))
        if shift == 0:
            return ref[plane, pl.ds(row, 8), :]
        inside = (target >= 0) & (target < self.rows)
        value = ref[plane, pl.ds(pl.multiple_of(lax.rem(target + self.rows, self.rows), 8), 8), :]
        wrapped = jnp.where(sublane == (0 if shift < 0 else 7), 0.0, pltpu.roll(value, 1 if shift < 0 else 7, 0))
        return jnp.where(inside, value, wrapped)

    def put(self, ref, plane, row, value, lane=slice(None)):
        ref[plane, pl.ds(row, 8), lane] = value

    def get(self, ref, plane, row):
        return ref[plane, pl.ds(row, 8), :]

    def set(self, ref, plane, row, value):
        ref[plane, pl.ds(row, 8), :] = value

    def fine_rates(self, base, row):
        ref, base = (self.fresh, 0) if base == 3 else (self.fine, base)
        state = [[self.at(ref, base * 8 + s * 4 + p, row) for p in range(4)] for s in range(2)]
        linear, rates = [], []
        for p, (a, b) in enumerate(PHASES):
            laps = []
            for s in range(2):
                across = state[s][2 * a + 1 - b]
                along = state[s][2 * (1 - a) + b]
                moved = self.at(ref, base * 8 + s * 4 + 2 * (1 - a) + b, row, 1 if a else -1)
                side = self.right(across) if b else self.left(across)
                laps.append((along + moved) + (across + side) - 4.0 * state[s][p])
            u, v = state[0][p], state[1][p]
            feed = self.get(self.coef, p, row)
            both = self.get(self.coef, 4 + p, row)
            lin_u = self.scaled(laps[0], DIFF_U) + feed
            lin_v = self.scaled(laps[1], DIFF_V)
            linear.append((lin_u, lin_v))
            rates.append(self.reacted(u, v, lin_u, lin_v, feed, both))
        return state, linear, rates

    def reacted(self, u, v, lin_u, lin_v, feed, both):
        return lin_u - u * (feed + v * v), lin_v + v * (u * v - both)

    def neighbours(self, plane, row, value):
        rows = self.at(self.cs, plane, row, -1) + self.at(self.cs, plane, row, 1)
        return rows + (self.left(value) + self.right(value))

    def laplacians(self, first, row):
        pair = [self.at(self.cs, first + s, row) for s in range(2)]
        return pair, [self.neighbours(first + s, row, pair[s]) - 4.0 * pair[s] for s in range(2)]

    def coarse_rates(self, first, row):
        (u, v), laps = self.laplacians(first, row)
        scaled = [self.scaled(laps[s], 0.25 * (DIFF_U, DIFF_V)[s]) for s in range(2)]
        feed, both = self.get(self.cc, 0, row), self.get(self.cc, 1, row)
        return (u, v), scaled, self.reacted(u, v, scaled[0] + feed, scaled[1], feed, both)

    def moved_rates(self, shift, scaled, which, base, row):
        a, b = shift
        m_vv, m_uv, m_u, m_v = (self.get(self.mom, 4 * which + k, row) for k in range(4))
        react = a * (m_vv + b * (2.0 * m_v + b)) + b * (2.0 * m_uv + b * m_u)
        feed, both = self.get(self.cc, 0, row), self.get(self.cc, 1, row)
        rate_u = (self.get(self.cp, base, row) + 2.0 * scaled[0]) - (feed * a + react)
        rate_v = (self.get(self.cp, base + 1, row) + 2.0 * scaled[1]) + (react - both * b)
        return rate_u, rate_v

    def block_mean(self, values):
        return 0.25 * ((values[0] + values[1]) + (values[2] + values[3]))

    def run(self, own, start=True, finish=True):
        lv = self
        cs, cp = self.cs, self.cp

        def first_sweep(row):
            for k in range(2):
                lv.set(lv.cc, k, row, lv.block_mean([lv.get(lv.coef, 4 * k + p, row) for p in range(4)]))
            state, linear, rates = lv.fine_rates(0, row)
            for s in range(2):
                for p in range(4):
                    lv.set(lv.lin, s * 4 + p, row, linear[p][s])
                    lv.put(lv.fine, 8 + s * 4 + p, row, state[s][p] + HALF_STEP * rates[p][s])
                mean = lv.block_mean([r[s] for r in rates])
                start = lv.block_mean(state[s])
                lv.set(cp, N_RA + s, row, mean)
                lv.put(cs, C_X0 + s, row, start)
                lv.put(cs, C_X1 + s, row, start + HALF_STEP * mean)
                lv.put(cs, C_END + s, row, start + mean)
                lv.put(cs, C_D1 + s, row, jnp.zeros_like(mean))
                lv.put(cs, C_D2 + s, row, jnp.zeros_like(mean))

        def moments(which, state, row):
            u, v = state
            lv.set(lv.mom, 4 * which, row, lv.block_mean([v[p] * v[p] for p in range(4)]))
            lv.set(lv.mom, 4 * which + 1, row, lv.block_mean([u[p] * v[p] for p in range(4)]))
            lv.set(lv.mom, 4 * which + 2, row, lv.block_mean(u))
            lv.set(lv.mom, 4 * which + 3, row, lv.block_mean(v))

        def second_sweep(row):
            state, linear, rates = lv.fine_rates(1, row)
            _, _, g0 = lv.coarse_rates(C_X0, row)
            first, scaled, g1 = lv.coarse_rates(C_X1, row)
            for s in range(2):
                for p in range(4):
                    lv.set(lv.lin, 8 + s * 4 + p, row, linear[p][s])
                    lv.put(lv.fine, 16 + s * 4 + p, row, state[s][p] + HALF_STEP * rates[p][s])
                mean = lv.block_mean([r[s] for r in rates])
                lv.set(cp, N_F1 + s, row, mean)
                lv.set(cp, N_RB + s, row, mean - 2.0 * scaled[s])
                lv.put(cs, C_X2 + s, row, first[s] + HALF_STEP * mean)
                integral = HALF_STEP * lv.get(cp, N_RA + s, row)
                lv.set(cp, N_K0 + s, row, integral - HALF_STEP * g0[s])
                lv.set(cp, N_K1 + s, row, integral - HALF_STEP * g1[s])
            moments(0, state, row)

        def third_sweep(row):
            state, linear, rates = lv.fine_rates(2, row)
            for s in range(2):
                for p in range(4):
                    lv.set(lv.lin, 16 + s * 4 + p, row, linear[p][s])
            moments(1, state, row)
            second, laps = lv.laplacians(C_X2, row)
            for s in range(2):
                mean = lv.block_mean([r[s] for r in rates])
                lv.set(cp, N_RE + s, row, mean - lv.scaled(laps[s], 0.5 * (DIFF_U, DIFF_V)[s]))
            end, last = slice_end(row)
            for s in range(2):
                j0, j1 = integrals(lv.get(cp, N_RA + s, row), lv.get(cp, N_F1 + s, row), last[s])
                lv.put(cs, C_NEW + s, row, lv.at(cs, C_X0 + s, row) + (j0 + j1))

        def integrals(f0, f1, f2):
            middle = W0[1] * f1
            return middle + (W0[0] * f0 + W0[2] * f2), middle + (W1[0] * f0 + W1[2] * f2)

        def slice_end(row):
            end, scaled, rate = lv.coarse_rates(C_END, row)
            shift = [end[s] - lv.at(cs, C_X2 + s, row) for s in range(2)]
            last = lv.moved_rates(shift, scaled, 1, N_RE, row)
            for s in range(2):
                half = HALF_STEP * rate[s]
                lv.set(cp, N_G0 + s, row, half)
                lv.put(cs, C_C1 + s, row, end[s] + half + lv.get(cp, N_K0 + s, row))
                lv.put(cs, C_D2_BEFORE + s, row, lv.at(cs, C_D2 + s, row))
                lv.put(cs, C_D2 + s, row, shift[s])
                lv.set(cp, N_RF2 + s, row, last[s])
            return end, last

        def middle_nodes(row):
            mid, scaled, rate = lv.coarse_rates(C_C1, row)
            new, _, new_rate = lv.coarse_rates(C_NEW, row)
            shift = [mid[s] - lv.at(cs, C_X1 + s, row) for s in range(2)]
            f1 = lv.moved_rates(shift, scaled, 0, N_RB, row)
            for s in range(2):
                old = lv.at(cs, C_END + s, row)
                lv.set(cp, N_LAST + s, row, old)
                lv.set(cp, N_F1 + s, row, f1[s])
                lv.put(cs, C_D1 + s, row, shift[s])
                lv.put(cs, C_END + s, row, mid[s] + HALF_STEP * rate[s] + lv.get(cp, N_K1 + s, row))
                change = HALF_STEP * new_rate[s] - lv.get(cp, N_G0 + s, row)
                lv.put(cs, C_E1 + s, row, (new[s] - old) + change)

        def end_nodes(row):
            before = [lv.get(cp, N_RF2 + s, row) for s in range(2)]
            _, last = slice_end(row)
            change, laps = lv.laplacians(C_E1, row)
            old, new, j1s = [], [], []
            for s in range(2):
                j0, j1 = integrals(before[s], lv.get(cp, N_F1 + s, row), last[s])
                old.append(lv.get(cp, N_LAST + s, row) + j0)
                new.append(old[s] + change[s])
                j1s.append(j1)
            feed, both = lv.get(lv.cc, 0, row), lv.get(lv.cc, 1, row)
            lin = [lv.scaled(laps[s], 0.25 * (DIFF_U, DIFF_V)[s]) for s in range(2)]
            rate_new = lv.reacted(new[0], new[1], lin[0], lin[1], feed, both)
            rate_old = lv.reacted(old[0], old[1], 0.0, 0.0, feed, both)
            for s in range(2):
                total = new[s] + j1s[s] + HALF_STEP * (rate_new[s] - rate_old[s])
                lv.put(cs, C_NEW + s, row, total)

        def corrections(starts):
            def body(row):
                for k, first in enumerate(starts):
                    for s in range(2):
                        d = lv.at(cs, first + s, row)
                        ring = [lv.at(cs, first + s, row, -1), lv.at(cs, first + s, row, 1), lv.left(d), lv.right(d)]
                        north, south, west, east = (lv.scaled(x - d, (DIFF_U, DIFF_V)[s]) for x in ring)
                        for p, (a, b) in enumerate(PHASES):
                            lv.set(lv.tl, k * 8 + s * 4 + p, row, (south if a else north) + (east if b else west))

            return body

        if start:
            lv.each(first_sweep)
            lv.each(second_sweep)
            lv.each(third_sweep)

        def one_slice(n, carry):
            lv.each(middle_nodes)
            lv.each(end_nodes)
            return carry

        if start:
            lax.fori_loop(1, own + 1, one_slice, 0)
        if not finish:
            return

        origin = jnp.where(own == 0, 0, 2)
        starts = (C_D2_BEFORE, C_D1, C_D2)
        lv.each(corrections(starts))

        def own_nodes(row):
            for p in range(4):
                for t in range(0, lv.lanes, 128):
                    lane = pl.ds(t, 128)
                    tile = pl.ds(row, 8)
                    feed, both = lv.coef[p, tile, lane], lv.coef[4 + p, tile, lane]
                    rates, start = [], None
                    for k, (base, d) in enumerate(zip((origin, 1, 2), starts)):
                        pair = [lv.fine[base * 8 + s * 4 + p, tile, lane] + cs[d + s, tile, lane] for s in range(2)]
                        lin = [lv.lin[base * 8 + s * 4 + p, tile, lane] + lv.tl[k * 8 + s * 4 + p, tile, lane] for s in range(2)]
                        rates.append(lv.reacted(pair[0], pair[1], lin[0], lin[1], feed, both))
                        start = pair if k == 0 else start
                    for s in range(2):
                        f0, f1, f2 = (r[s] for r in rates)
                        second = start[s] + (W0[0] * f0 + W0[1] * f1 + W0[2] * f2)
                        lv.put(lv.fresh, s * 4 + p, row, second, lane)
                        lv.rest[s * 4 + p, tile, lane] = second + (W1[0] * f0 + (W1[1] - HALF_STEP) * f1 + W1[2] * f2)

        lv.each(own_nodes)

        def last_node(row):
            _, _, rates = lv.fine_rates(3, row)
            for s in range(2):
                ends = [lv.get(lv.rest, s * 4 + p, row) + HALF_STEP * rates[p][s] for p in range(4)]
                fix = lv.at(cs, C_NEW + s, row) - lv.block_mean(ends)
                for p in range(4):
                    lv.set(lv.rest, s * 4 + p, row, ends[p] + fix)

        lv.each(last_node)


def load_planes(level, sources, columns, natural):
    count = level.lanes // 128
    matrix = group_matrix(count, False)
    slot = slots(count)
    for read, first in sources:
        blocks = []
        for k in range(count):
            values = [read(plane, k) for plane in range(4)]
            blocks.append(permuted(jnp.concatenate(values, axis=0), matrix))
        rows = blocks[0].shape[0] // 4
        for b in range(2):
            tiles = exchanged([block[:, 128 * b : 128 * b + 128] for block in blocks], slot)
            for q, tile in enumerate(tiles):
                for plane in range(4):
                    natural[plane, 2 * q + b, pl.ds(first, rows), :] = tile[plane * rows : (plane + 1) * rows]
    chunks = level.chunks
    for q in range(count):
        for p, (a, b) in enumerate(PHASES):
            for t in range(chunks):
                picked = [natural[plane, 2 * q + b, pl.ds(2 * t + a, 8, stride=2 * chunks), :] for plane in range(4)]
                lane, row = pl.ds(128 * q, 128), 8 * t
                for s in range(2):
                    level.fine[s * 4 + p, pl.ds(row, 8), lane] = picked[s]
                level.coef[p, pl.ds(row, 8), lane] = picked[2]
                level.coef[4 + p, pl.ds(row, 8), lane] = picked[2] + picked[3]


def spread(level, natural):
    count, chunks = level.lanes // 128, level.chunks
    for s in range(2):
        for q in range(count):
            for p, (a, b) in enumerate(PHASES):
                for t in range(chunks):
                    value = level.rest[s * 4 + p, pl.ds(8 * t, 8), pl.ds(128 * q, 128)]
                    natural[s, 2 * q + b, pl.ds(2 * t + a, 8, stride=2 * chunks), :] = value


def merged(level, first, rows, natural, matrix):
    count = level.lanes // 128
    slot = slots(count)
    halves = []
    for b in range(2):
        tiles = []
        for q in range(count):
            tiles.append(jnp.concatenate([natural[s, 2 * q + b, pl.ds(first, rows), :] for s in range(2)], axis=0))
        halves.append(exchanged(tiles, slot))
    blocks = [permuted(jnp.concatenate([halves[0][k], halves[1][k]], axis=1), matrix) for k in range(count)]
    return [[block[s * rows : (s + 1) * rows] for block in blocks] for s in range(2)]


def woven(natural, first, rows):
    lane = lax.broadcasted_iota(jnp.int32, (8, 128), 1)
    results = []
    for s in range(2):
        blocks = []
        for at in range(0, rows, 8):
            pair = [natural[s, b, pl.ds(pl.multiple_of(first + at, 8), 8), :] for b in range(2)]
            halves = []
            for k in range(2):
                even, odd = (jnp.take_along_axis(x, (lane >> 1) + 64 * k, axis=1) for x in pair)
                halves.append(jnp.where((lane & 1) == 0, even, odd))
            blocks.append(jnp.concatenate(halves, axis=1))
        results.append([jnp.concatenate(blocks, axis=0)])
    return results


def own_first(rows):
    return pl.multiple_of(lax.axis_index("gx") * rows, rows)


def source_list(refs, rows, parts):
    if parts == 2:
        mine = own_first(rows)
        state, feed, kill = refs[4:]
        other = [state.at[0], state.at[1], feed, kill]
        return [(refs[:4], mine), (other, pl.multiple_of(rows - mine, rows))]
    state, feed, kill = refs
    return [([state.at[g, 0], state.at[g, 1], feed.at[g], kill.at[g]], g * rows) for g in range(parts)]


def interior_kernel(parts, rows, columns, halo, depth, width, start, finish, *refs):
    refs = list(refs)
    take = lambda count: [refs.pop(0) for _ in range(count)]
    here = columns // 2 if parts == 2 else columns
    origin = pl.multiple_of(lax.axis_index("gx") * here, here) if parts == 2 else 0
    seam = 4 * depth if parts == 2 else 0
    side = (width - seam) // 2 - halo
    ins = take(7 if parts == 2 else 3) if start else []
    given = [] if start else take(7)
    window = take(1)[0] if start else None
    outs = take(2 if parts == 2 else 1) if finish else []
    state = take(7) if start else given
    late = take(3) if finish else []
    (natural,) = take(1)
    level = Level(state + late, parts * rows // 2, here // 2, None)

    def reader(planes):
        return lambda plane, block: planes[plane][:, pl.ds(origin + 256 * block, 256)]

    if start:
        sources = []
        for planes, first in source_list(ins, rows, parts):
            sources.append((reader(planes), first))
            for plane in range(4):
                value = planes[plane][...]
                blank = jnp.zeros((rows, halo), F32)
                cuts = [blank, value[:, :side], value[:, (columns - seam) // 2 : (columns + seam) // 2]]
                cuts += [value[:, columns - side :], blank]
                window[plane, pl.ds(first, rows), :] = jnp.concatenate([cut for cut in cuts if cut.shape[1]], axis=1)
        load_planes(level, sources, here, natural)
    level.run(lax.axis_index("ta"), start, finish)
    if finish:
        spread(level, natural)
        matrix = group_matrix(level.lanes // 128, True)
        mine = own_first(rows)
        firsts = [mine, pl.multiple_of(rows - mine, rows)] if parts == 2 else [mine]
        for target, first in zip(outs, firsts):
            blocks = merged(level, first, rows, natural, matrix)
            for s in range(2):
                for k, block in enumerate(blocks[s]):
                    target[s, :, pl.ds(256 * k, 256)] = block


def border_kernel(parts, rows, halo, depth, width, window, near, far, out, *work):
    lanes = width // 2
    index, size = lax.axis_index("gy"), lax.axis_size("gy")
    swap = lax.rem(index, 2) == 0
    if parts == 2:
        swap = swap == (lax.axis_index("gx") == 0)
    tiles = lanes // 128
    at = lax.broadcasted_iota(jnp.int32, (1, lanes), 1)
    at = tiles * (at % 128) + at // 128
    outside = ((at < halo // 2) & (index == 0)) | ((at >= lanes - halo // 2) & (index == size - 1))
    level = Level(work[:-1], parts * rows // 2, lanes, jnp.where(outside, 0.0, 1.0))

    strips = []
    for edge, (a, b) in ((0, (far, near)), (size - 1, (near, far))):
        strip = jnp.where(index == edge, 0.0, jnp.where(swap, a[...], b[...]))
        strips.append(unfolded(strip, parts * rows, 4 * depth))

    def reader(first):
        def read(plane, block):
            low, high = (strip[first : first + rows, depth * plane : depth * plane + depth] for strip in strips)
            own = window[plane, pl.ds(first, rows), :]
            cuts = [own[:, : halo - depth], low, own[:, halo : width - halo], high, own[:, width - halo + depth :]]
            whole = jnp.concatenate([cut for cut in cuts if cut.shape[1]], axis=1)
            return whole[:, 256 * block : 256 * block + 256]

        return read

    load_planes(level, [(reader(g * rows), g * rows) for g in range(parts)], width, work[-1])
    level.run(lax.axis_index("ta"))
    spread(level, work[-1])
    natural = woven(work[-1], own_first(rows), rows) if tiles == 1 else None
    natural = natural or merged(level, own_first(rows), rows, work[-1], group_matrix(tiles, True))
    for s in range(2):
        for k, block in enumerate(natural[s]):
            out[s, :, pl.ds(256 * k, 256)] = block


def final_kernel(halo, depth, width, inner, border, out):
    total = out.shape[-1]
    out[0] = inner[...]
    for s in range(2):
        for column, source in ((0, halo), (total - depth, width - halo - depth)):
            low = column // 128 * 128
            high = round_up(column + depth, 128)
            old, new = out[0, s, :, pl.ds(low, high - low)], border[s][:, source : source + depth]
            parts_of = [old[:, : column - low], new, old[:, column + depth - low :]]
            out[0, s, :, pl.ds(low, high - low)] = jnp.concatenate([x for x in parts_of if x.shape[1]], axis=1)


def joined_kernel(halo, depth, width, keep, got, border, out, ends, middle, sems):
    total = out.shape[-1]
    half = total // 2
    tile = round_up(depth, 128)
    core = lax.axis_index("gx")
    copies = []
    for k, value in enumerate((keep, got)):
        origin = pl.multiple_of((core if k == 0 else 1 - core) * half + tile, 128)
        inside = pl.ds(tile, half - 2 * tile)
        target = out.at[0, :, :, pl.ds(origin, half - 2 * tile)]
        copies.append(pltpu.make_async_copy(value.at[:, :, inside], target, sems.at[k]))
        copies[-1].start()
    first = core == 0
    low, high = pl.ds(0, tile), pl.ds(half - tile, tile)
    for s in range(2):
        old = [jnp.where(first, a[s, :, at], b[s, :, at]) for a, b in ((keep, got), (got, keep)) for at in (low, high)]
        new = border[s]
        starts = (halo, width // 2 - depth, width // 2, width - halo - depth)
        new = [new[:, at : at + depth] for at in starts]
        ends[0, s] = jnp.concatenate([new[0], old[0][:, depth:]], axis=1)
        ends[1, s] = jnp.concatenate([old[3][:, : tile - depth], new[3]], axis=1)
        middle[s] = jnp.concatenate([old[1][:, : tile - depth], new[1], new[2], old[2][:, depth:]], axis=1)
    copies.append(pltpu.make_async_copy(ends.at[0], out.at[0, :, :, pl.ds(0, tile)], sems.at[2]))
    copies.append(pltpu.make_async_copy(ends.at[1], out.at[0, :, :, pl.ds(total - tile, tile)], sems.at[3]))
    copies.append(pltpu.make_async_copy(middle, out.at[0, :, :, pl.ds(half - tile, 2 * tile)], sems.at[4]))
    for copy in copies[2:]:
        copy.start()
    for copy in copies:
        copy.wait()


def folds(rows, lanes):
    return 8 * -(-(rows // 8 * lanes) // 128) if lanes < 128 else rows


def folded(strip):
    rows, lanes = strip.shape
    kept, spare = folds(rows, lanes), 128 - lanes
    if lanes >= 128:
        return strip
    stream = [strip[at : at + 8] for at in range(kept, rows, 8)]
    missing = kept // 8 * spare - (rows - kept) // 8 * lanes
    stream = jnp.concatenate(stream + [jnp.zeros((8, missing), F32)] * (missing > 0), axis=1)
    groups = []
    for k in range(kept // 8):
        groups.append(jnp.concatenate([strip[8 * k : 8 * k + 8], stream[:, k * spare : (k + 1) * spare]], axis=1))
    return jnp.concatenate(groups, axis=0)


def unfolded(value, rows, lanes):
    kept = folds(rows, lanes)
    if lanes >= 128:
        return value
    stream = jnp.concatenate([value[at : at + 8, lanes:] for at in range(0, kept, 8)], axis=1)
    tail = [stream[:, k * lanes : (k + 1) * lanes] for k in range((rows - kept) // 8)]
    return jnp.concatenate([value[:, :lanes], *tail], axis=0)


def pack_kernel(parts, rows, depth, *refs):
    count = 7 if parts == 2 else 3
    ins, outs = refs[:count], refs[count:]
    even = lax.rem(lax.axis_index("gy"), 2) == 0
    if parts == 2:
        even = even == (lax.axis_index("gx") == 0)
    strips = []
    for planes, _ in source_list(ins, rows, parts):
        total = planes[0].shape[-1]
        tile = round_up(depth, 128)
        low = jnp.concatenate([ref[:, pl.ds(0, tile)][:, :depth] for ref in planes], axis=1)
        high = jnp.concatenate([ref[:, pl.ds(total - tile, tile)][:, tile - depth :] for ref in planes], axis=1)
        strips.append((jnp.where(even, high, low), jnp.where(even, low, high)))
    if parts == 2:
        (own, _), (other, _) = strips
        first = lax.axis_index("gx") == 0
        whole = [jnp.concatenate([jnp.where(first, own, other), jnp.where(first, other, own)], axis=0)]
    else:
        whole = [jnp.concatenate(each, axis=0) for each in zip(*strips)]
    for out, strip in zip(outs, whole):
        out[...] = folded(strip)


def fetch_kernel(state, feed, kill, *refs):
    planes, sems = refs[:4], refs[4]
    sources = (state.at[0], state.at[1], feed, kill)
    copies = [pltpu.make_async_copy(sources[i], planes[i], sems.at[i]) for i in range(4)]
    for copy in copies:
        copy.start()
    for copy in copies:
        copy.wait()


def both_ways(pairs):
    return [pair for low, high in pairs for pair in ((low, high), (high, low))]


VMEM = pl.BlockSpec(memory_space=pltpu.VMEM)
ANY = pl.BlockSpec(memory_space=pl.ANY)


def arrays(shapes):
    return [jax.ShapeDtypeStruct(shape, F32) for shape in shapes]


def buffers(shapes):
    return [pltpu.VMEM(shape, F32) for shape in shapes]


def size_of(shapes):
    return sum(4 * math.prod(shape) for shape in shapes)


def called(name, kernel, outs, scratch, limit, inputs, specs=VMEM, out_specs=VMEM, flops=0):
    return pl.pallas_call(
        kernel,
        out_shape=outs,
        in_specs=[specs] * len(inputs),
        out_specs=[out_specs] * len(outs),
        scratch_shapes=scratch,
        compiler_params=pltpu.CompilerParams(vmem_limit_bytes=limit),
        cost_estimate=pl.CostEstimate(flops=flops, bytes_accessed=flops // 2, transcendentals=0),
        name=name,
    )(*inputs)


def per_device(initial_state, feed_rate, kill_rate):
    slices, parts, blocks = (lax.axis_size(axis) for axis in ("ta", "gx", "gy"))
    _, rows, columns = initial_state.shape
    depth = 2 * (2 * slices + 2)
    halo = round_up(depth, 32)
    seam = 4 * depth if parts == 2 else 0
    width = round_up(2 * halo + 4 * depth + seam, 256)
    every = parts * rows
    here = columns // 2 if parts == 2 else columns
    given = (initial_state, feed_rate, kill_rate)
    plane_bytes = 4 * every * columns

    low_pairs = both_ways([(i, i + 1) for i in range(0, blocks - 1, 2)])
    high_pairs = both_ways([(i, (i + 1) % blocks) for i in range(1, blocks - blocks % 2, 2)])

    def crossed(value):
        return lax.ppermute(value, "gx", [(0, 1), (1, 0)])

    if parts == 2:
        others = [crossed(value) for value in given]
        limit = 1709 * 2**15
        own = called("fetch", fetch_kernel, arrays([(rows, columns)] * 4), [pltpu.SemaphoreType.DMA((4,))], limit, given, ANY)
        fields = [*own, *others]
    else:
        fields = [lax.all_gather(value, "gx") for value in given]
    pack = functools.partial(pack_kernel, parts, rows, depth)
    strips = arrays([(folds(every, 4 * depth), max(4 * depth, 128))] * (1 if parts == 2 else 2))
    sent = called("pack", pack, strips, [], 8 * plane_bytes + 2**22, fields)
    if parts == 2:
        pairs = []
        for n in range(slices):
            base = n * 2 * blocks
            inner_pairs = both_ways([(i, i + 1) for i in range(1, blocks - 1, 2)])
            pairs += [(base + source, base + target) for source, target in low_pairs]
            pairs += [(base + blocks + source, base + blocks + target) for source, target in inner_pairs]
            if n ^ 1 < slices:
                met = {0, blocks - 1} - {source for source, _ in inner_pairs}
                pairs += [(base + blocks + i, (n ^ 1) * 2 * blocks + blocks + i) for i in sorted(met)]
        near = lax.ppermute(sent[0], ("ta", "gx", "gy"), pairs)
    else:
        near = lax.ppermute(sent[0], "gy", low_pairs)
        far = lax.ppermute(sent[1], "gy", high_pairs)

    state, late = state_shapes(every // 2, here // 2), late_shapes(every // 2, here // 2)
    natural = natural_shape(every // 2, here // 2)
    limit = size_of(state + late + [natural]) + 32 * every * (columns + width) + 2**22
    interior = functools.partial(interior_kernel, parts, rows, columns, halo, depth, width)
    window_shape = (4, every, width)
    result_shape = (2, rows, here)
    if parts == 2:
        first = functools.partial(interior, True, False)
        made = called("interior", first, arrays([window_shape] + state), buffers([natural]), limit, fields, flops=2**24)
        near, window, *made = lax.optimization_barrier((near, *made))
        far = crossed(near)
        last = functools.partial(interior, False, True)
        keep, give = called("own", last, arrays([result_shape] * 2), buffers(late + [natural]), limit, made, flops=2**23)
        far, give = lax.optimization_barrier((far, give))
        inner = [keep, crossed(give)]
    else:
        whole = functools.partial(interior, True, True)
        scratch = buffers(state + late + [natural])
        window, *inner = called("interior", whole, arrays([window_shape, result_shape]), scratch, limit, fields, flops=2**24)
    work = state_shapes(every // 2, width // 2) + late_shapes(every // 2, width // 2)
    work.append(natural_shape(every // 2, width // 2))
    limit = size_of(work) + 32 * every * width + 2**23
    border = functools.partial(border_kernel, parts, rows, halo, depth, width)
    (edges,) = called("border", border, arrays([(2, rows, width)]), buffers(work), limit, (window, near, far), flops=2**23)
    result = arrays([(1, 2, rows, columns)])
    if parts == 2:
        tile = round_up(depth, 128)
        scratch = buffers([(2, 2, rows, tile), (2, rows, 2 * tile)]) + [pltpu.SemaphoreType.DMA((5,))]
        final = functools.partial(joined_kernel, halo, depth, width)
        (out,) = called("final", final, result, scratch, 2**23, (*inner, edges), out_specs=ANY)
    else:
        final = functools.partial(final_kernel, halo, depth, width)
        (out,) = called("final", final, result, [], 16 * plane_bytes + 2**22, (*inner, edges))
    return out


def solution(mesh):
    placed = (P(None, "gx", "gy"), P("gx", "gy"), P("gx", "gy"))
    return jax.shard_map(
        per_device, mesh=mesh, in_specs=placed, out_specs=P("ta", None, "gx", "gy"), check_vma=False
    )
```

```python
import functools
import math

import jax
import jax.numpy as jnp
from jax import lax
from jax.experimental import pallas as pl
from jax.experimental.pallas import tpu as pltpu
from jax.sharding import PartitionSpec as P

TURNS = 2

DIFF_U = 0.2
DIFF_V = 0.1
HALF_STEP = 0.5
W0 = (5.0 / 24.0, 1.0 / 3.0, -1.0 / 24.0)
W1 = (-1.0 / 24.0, 1.0 / 3.0, 5.0 / 24.0)
F32 = jnp.float32
BF16 = jnp.bfloat16
PHASES = ((0, 0), (0, 1), (1, 0), (1, 1))


def round_up(value, step):
    return -(-value // step) * step


def thirds(value):
    high = value.astype(BF16)
    rest = value - high.astype(F32)
    middle = rest.astype(BF16)
    low = (rest - middle.astype(F32)).astype(BF16)
    return high, middle, low


def permuted(value, matrix):
    rows = value.shape[0]
    parts = jnp.concatenate(thirds(value), axis=0)
    moved = jnp.dot(parts, matrix, preferred_element_type=F32)
    return (moved[2 * rows :] + moved[rows : 2 * rows]) + moved[:rows]


def group_matrix(tiles, inverse):
    group, bits = 128 // tiles, (tiles - 1).bit_length()
    source = lax.broadcasted_iota(jnp.int32, (256, 256), 0)
    target = lax.broadcasted_iota(jnp.int32, (1, 256), 1)
    if inverse:
        wanted = ((target & 1) << 7) + (((target >> 1) & (tiles - 1)) << (7 - bits)) + (target >> (1 + bits))
    else:
        wanted = ((target & (group - 1)) << (1 + bits)) + (((target & 127) >> (7 - bits)) << 1) + (target >> 7)
    return jnp.where(source == wanted, 1.0, 0.0).astype(BF16)


def exchanged(tiles, slot):
    count = len(tiles)
    if count == 1:
        return tiles
    group = 128 // count
    turned = [pltpu.roll(tile, k * group, 1) if k else tile for k, tile in enumerate(tiles)]
    results = []
    for q in range(count):
        value = turned[(count - q) % count]
        for at in range(1, count):
            value = jnp.where(slot == at, turned[(at - q) % count], value)
        results.append(pltpu.roll(value, (count - q) * group, 1) if q else value)
    return results


def slots(tiles):
    return lax.broadcasted_iota(jnp.int32, (1, 128), 1) >> (7 - (tiles - 1).bit_length())


C_X0, C_X1, C_X2, C_END, C_C1, C_NEW, C_E1, C_D1, C_D2, C_D2_BEFORE = (2 * i for i in range(10))
COARSE_STENCIL = 20
N_LAST, N_K0, N_K1, N_G0, N_RA, N_RB, N_RE, N_F1, N_RF2 = (2 * i for i in range(9))
COARSE_PLAIN = 18


PLANES = {
    "fine": 24,
    "lin": 24,
    "coef": 8,
    "cs": COARSE_STENCIL,
    "cp": COARSE_PLAIN,
    "cc": 2,
    "mom": 8,
    "fresh": 8,
    "rest": 8,
    "tl": 24,
    "ends": 8,
}
HANDED = ("fresh", "rest", "coef", "cs")


def shapes_of(names, rows, lanes):
    return [(PLANES[name], rows, lanes) for name in names]


def natural_shape(rows, lanes):
    return (4, 2 * lanes // 128, 2 * rows, 128)


class Level:
    def __init__(self, refs, rows, lanes, mask):
        for name, ref in refs.items():
            setattr(self, name, ref)
        self.rows, self.lanes, self.mask = rows, lanes, mask
        self.chunks = rows // 8

    def each(self, body):
        if self.chunks <= 4:
            for i in range(self.chunks):
                body(8 * i)
        else:
            pl.loop(0, self.chunks)(lambda i: body(pl.multiple_of(8 * i, 8)))

    def left(self, value):
        if self.lanes == 128:
            return pltpu.roll(value, 1, 1)
        return jnp.concatenate([pltpu.roll(value[:, -128:], 1, 1), value[:, :-128]], axis=1)

    def right(self, value):
        if self.lanes == 128:
            return pltpu.roll(value, 127, 1)
        return jnp.concatenate([value[:, 128:], pltpu.roll(value[:, :128], 127, 1)], axis=1)

    def scaled(self, value, factor):
        if self.mask is None:
            return factor * value
        return (factor * self.mask) * value

    def at(self, ref, plane, row, shift=0):
        target = row + 8 * shift
        if isinstance(row, int) and 0 <= target < self.rows:
            return ref[plane, pl.ds(target, 8), :]
        sublane = lax.broadcasted_iota(jnp.int32, (8, 1), 0)
        if isinstance(row, int):
            value = ref[plane, pl.ds(target % self.rows, 8), :]
            return jnp.where(sublane == (0 if shift < 0 else 7), 0.0, pltpu.roll(value, 1 if shift < 0 else 7, 0))
        if shift == 0:
            return ref[plane, pl.ds(row, 8), :]
        inside = (target >= 0) & (target < self.rows)
        value = ref[plane, pl.ds(pl.multiple_of(lax.rem(target + self.rows, self.rows), 8), 8), :]
        wrapped = jnp.where(sublane == (0 if shift < 0 else 7), 0.0, pltpu.roll(value, 1 if shift < 0 else 7, 0))
        return jnp.where(inside, value, wrapped)

    def put(self, ref, plane, row, value, lane=slice(None)):
        ref[plane, pl.ds(row, 8), lane] = value

    def get(self, ref, plane, row):
        return ref[plane, pl.ds(row, 8), :]

    def set(self, ref, plane, row, value):
        ref[plane, pl.ds(row, 8), :] = value

    def fine_rates(self, base, row):
        ref, base = (self.fresh, 0) if base == 3 else (self.fine, base)
        state = [[self.at(ref, base * 8 + s * 4 + p, row) for p in range(4)] for s in range(2)]
        linear, rates = [], []
        for p, (a, b) in enumerate(PHASES):
            laps = []
            for s in range(2):
                across = state[s][2 * a + 1 - b]
                along = state[s][2 * (1 - a) + b]
                moved = self.at(ref, base * 8 + s * 4 + 2 * (1 - a) + b, row, 1 if a else -1)
                side = self.right(across) if b else self.left(across)
                laps.append((along + moved) + (across + side) - 4.0 * state[s][p])
            u, v = state[0][p], state[1][p]
            feed = self.get(self.coef, p, row)
            both = self.get(self.coef, 4 + p, row)
            lin_u = self.scaled(laps[0], DIFF_U) + feed
            lin_v = self.scaled(laps[1], DIFF_V)
            linear.append((lin_u, lin_v))
            rates.append(self.reacted(u, v, lin_u, lin_v, feed, both))
        return state, linear, rates

    def reacted(self, u, v, lin_u, lin_v, feed, both):
        return lin_u - u * (feed + v * v), lin_v + v * (u * v - both)

    def neighbours(self, plane, row, value):
        rows = self.at(self.cs, plane, row, -1) + self.at(self.cs, plane, row, 1)
        return rows + (self.left(value) + self.right(value))

    def laplacians(self, first, row):
        pair = [self.at(self.cs, first + s, row) for s in range(2)]
        return pair, [self.neighbours(first + s, row, pair[s]) - 4.0 * pair[s] for s in range(2)]

    def coarse_rates(self, first, row):
        (u, v), laps = self.laplacians(first, row)
        scaled = [self.scaled(laps[s], 0.25 * (DIFF_U, DIFF_V)[s]) for s in range(2)]
        feed, both = self.get(self.cc, 0, row), self.get(self.cc, 1, row)
        return (u, v), scaled, self.reacted(u, v, scaled[0] + feed, scaled[1], feed, both)

    def moved_rates(self, shift, scaled, which, base, row):
        a, b = shift
        m_vv, m_uv, m_u, m_v = (self.get(self.mom, 4 * which + k, row) for k in range(4))
        react = a * (m_vv + b * (2.0 * m_v + b)) + b * (2.0 * m_uv + b * m_u)
        feed, both = self.get(self.cc, 0, row), self.get(self.cc, 1, row)
        rate_u = (self.get(self.cp, base, row) + 2.0 * scaled[0]) - (feed * a + react)
        rate_v = (self.get(self.cp, base + 1, row) + 2.0 * scaled[1]) + (react - both * b)
        return rate_u, rate_v

    def block_mean(self, values):
        return 0.25 * ((values[0] + values[1]) + (values[2] + values[3]))

    def run(self, own, start=True, finish=True):
        lv = self
        cs, cp = self.cs, getattr(self, "cp", None)

        def first_sweep(row):
            for k in range(2):
                lv.set(lv.cc, k, row, lv.block_mean([lv.get(lv.coef, 4 * k + p, row) for p in range(4)]))
            state, linear, rates = lv.fine_rates(0, row)
            for s in range(2):
                for p in range(4):
                    lv.set(lv.lin, s * 4 + p, row, linear[p][s])
                    lv.put(lv.fine, 8 + s * 4 + p, row, state[s][p] + HALF_STEP * rates[p][s])
                mean = lv.block_mean([r[s] for r in rates])
                start = lv.block_mean(state[s])
                lv.set(cp, N_RA + s, row, mean)
                lv.put(cs, C_X0 + s, row, start)
                lv.put(cs, C_X1 + s, row, start + HALF_STEP * mean)
                lv.put(cs, C_END + s, row, start + mean)
                lv.put(cs, C_D1 + s, row, jnp.zeros_like(mean))
                lv.put(cs, C_D2 + s, row, jnp.zeros_like(mean))

        def moments(which, state, row):
            u, v = state
            lv.set(lv.mom, 4 * which, row, lv.block_mean([v[p] * v[p] for p in range(4)]))
            lv.set(lv.mom, 4 * which + 1, row, lv.block_mean([u[p] * v[p] for p in range(4)]))
            lv.set(lv.mom, 4 * which + 2, row, lv.block_mean(u))
            lv.set(lv.mom, 4 * which + 3, row, lv.block_mean(v))

        def second_sweep(row):
            state, linear, rates = lv.fine_rates(1, row)
            _, _, g0 = lv.coarse_rates(C_X0, row)
            first, scaled, g1 = lv.coarse_rates(C_X1, row)
            for s in range(2):
                for p in range(4):
                    lv.set(lv.lin, 8 + s * 4 + p, row, linear[p][s])
                    lv.put(lv.fine, 16 + s * 4 + p, row, state[s][p] + HALF_STEP * rates[p][s])
                mean = lv.block_mean([r[s] for r in rates])
                lv.set(cp, N_F1 + s, row, mean)
                lv.set(cp, N_RB + s, row, mean - 2.0 * scaled[s])
                lv.put(cs, C_X2 + s, row, first[s] + HALF_STEP * mean)
                integral = HALF_STEP * lv.get(cp, N_RA + s, row)
                lv.set(cp, N_K0 + s, row, integral - HALF_STEP * g0[s])
                lv.set(cp, N_K1 + s, row, integral - HALF_STEP * g1[s])
            moments(0, state, row)

        def third_sweep(row):
            state, linear, rates = lv.fine_rates(2, row)
            for s in range(2):
                for p in range(4):
                    lv.set(lv.lin, 16 + s * 4 + p, row, linear[p][s])
            moments(1, state, row)
            second, laps = lv.laplacians(C_X2, row)
            for s in range(2):
                mean = lv.block_mean([r[s] for r in rates])
                lv.set(cp, N_RE + s, row, mean - lv.scaled(laps[s], 0.5 * (DIFF_U, DIFF_V)[s]))
            end, last = slice_end(row)
            for s in range(2):
                j0, j1 = integrals(lv.get(cp, N_RA + s, row), lv.get(cp, N_F1 + s, row), last[s])
                lv.put(cs, C_NEW + s, row, lv.at(cs, C_X0 + s, row) + (j0 + j1))

        def integrals(f0, f1, f2):
            middle = W0[1] * f1
            return middle + (W0[0] * f0 + W0[2] * f2), middle + (W1[0] * f0 + W1[2] * f2)

        def slice_end(row):
            end, scaled, rate = lv.coarse_rates(C_END, row)
            shift = [end[s] - lv.at(cs, C_X2 + s, row) for s in range(2)]
            last = lv.moved_rates(shift, scaled, 1, N_RE, row)
            for s in range(2):
                half = HALF_STEP * rate[s]
                lv.set(cp, N_G0 + s, row, half)
                lv.put(cs, C_C1 + s, row, end[s] + half + lv.get(cp, N_K0 + s, row))
                lv.put(cs, C_D2_BEFORE + s, row, lv.at(cs, C_D2 + s, row))
                lv.put(cs, C_D2 + s, row, shift[s])
                lv.set(cp, N_RF2 + s, row, last[s])
            return end, last

        def middle_nodes(row):
            mid, scaled, rate = lv.coarse_rates(C_C1, row)
            new, _, new_rate = lv.coarse_rates(C_NEW, row)
            shift = [mid[s] - lv.at(cs, C_X1 + s, row) for s in range(2)]
            f1 = lv.moved_rates(shift, scaled, 0, N_RB, row)
            for s in range(2):
                old = lv.at(cs, C_END + s, row)
                lv.set(cp, N_LAST + s, row, old)
                lv.set(cp, N_F1 + s, row, f1[s])
                lv.put(cs, C_D1 + s, row, shift[s])
                lv.put(cs, C_END + s, row, mid[s] + HALF_STEP * rate[s] + lv.get(cp, N_K1 + s, row))
                change = HALF_STEP * new_rate[s] - lv.get(cp, N_G0 + s, row)
                lv.put(cs, C_E1 + s, row, (new[s] - old) + change)

        def end_nodes(row):
            before = [lv.get(cp, N_RF2 + s, row) for s in range(2)]
            _, last = slice_end(row)
            change, laps = lv.laplacians(C_E1, row)
            old, new, j1s = [], [], []
            for s in range(2):
                j0, j1 = integrals(before[s], lv.get(cp, N_F1 + s, row), last[s])
                old.append(lv.get(cp, N_LAST + s, row) + j0)
                new.append(old[s] + change[s])
                j1s.append(j1)
            feed, both = lv.get(lv.cc, 0, row), lv.get(lv.cc, 1, row)
            lin = [lv.scaled(laps[s], 0.25 * (DIFF_U, DIFF_V)[s]) for s in range(2)]
            rate_new = lv.reacted(new[0], new[1], lin[0], lin[1], feed, both)
            rate_old = lv.reacted(old[0], old[1], 0.0, 0.0, feed, both)
            for s in range(2):
                total = new[s] + j1s[s] + HALF_STEP * (rate_new[s] - rate_old[s])
                lv.put(cs, C_NEW + s, row, total)

        def corrections(starts):
            def body(row):
                for k, first in enumerate(starts):
                    for s in range(2):
                        d = lv.at(cs, first + s, row)
                        ring = [lv.at(cs, first + s, row, -1), lv.at(cs, first + s, row, 1), lv.left(d), lv.right(d)]
                        north, south, west, east = (lv.scaled(x - d, (DIFF_U, DIFF_V)[s]) for x in ring)
                        for p, (a, b) in enumerate(PHASES):
                            lv.set(lv.tl, k * 8 + s * 4 + p, row, (south if a else north) + (east if b else west))

            return body

        def one_slice(n, carry):
            lv.each(middle_nodes)
            lv.each(end_nodes)
            return carry

        origin = jnp.where(own == 0, 0, 2)
        starts = (C_D2_BEFORE, C_D1, C_D2)
        def own_nodes(row):
            for p in range(4):
                for t in range(0, lv.lanes, 128):
                    lane = pl.ds(t, 128)
                    tile = pl.ds(row, 8)
                    feed, both = lv.coef[p, tile, lane], lv.coef[4 + p, tile, lane]
                    rates, start = [], None
                    for k, (base, d) in enumerate(zip((origin, 1, 2), starts)):
                        pair = [lv.fine[base * 8 + s * 4 + p, tile, lane] + cs[d + s, tile, lane] for s in range(2)]
                        lin = [lv.lin[base * 8 + s * 4 + p, tile, lane] + lv.tl[k * 8 + s * 4 + p, tile, lane] for s in range(2)]
                        rates.append(lv.reacted(pair[0], pair[1], lin[0], lin[1], feed, both))
                        start = pair if k == 0 else start
                    for s in range(2):
                        f0, f1, f2 = (r[s] for r in rates)
                        second = start[s] + (W0[0] * f0 + W0[1] * f1 + W0[2] * f2)
                        lv.put(lv.fresh, s * 4 + p, row, second, lane)
                        lv.rest[s * 4 + p, tile, lane] = second + (W1[0] * f0 + (W1[1] - HALF_STEP) * f1 + W1[2] * f2)

        def last_node(row):
            _, _, rates = lv.fine_rates(3, row)
            for s in range(2):
                ends = [lv.get(lv.rest, s * 4 + p, row) + HALF_STEP * rates[p][s] for p in range(4)]
                fix = lv.at(cs, C_NEW + s, row) - lv.block_mean(ends)
                for p in range(4):
                    lv.set(lv.ends, s * 4 + p, row, ends[p] + fix)

        if start:
            lv.each(first_sweep)
            lv.each(second_sweep)
            lv.each(third_sweep)
            lax.fori_loop(1, own + 1, one_slice, 0)
            lv.each(corrections(starts))
            lv.each(own_nodes)
        if finish:
            lv.each(last_node)


def load_planes(level, sources, columns, natural):
    count = level.lanes // 128
    matrix = group_matrix(count, False)
    slot = slots(count)
    for read, first in sources:
        blocks = []
        for k in range(count):
            values = [read(plane, k) for plane in range(4)]
            blocks.append(permuted(jnp.concatenate(values, axis=0), matrix))
        rows = blocks[0].shape[0] // 4
        for b in range(2):
            tiles = exchanged([block[:, 128 * b : 128 * b + 128] for block in blocks], slot)
            for q, tile in enumerate(tiles):
                for plane in range(4):
                    natural[plane, 2 * q + b, pl.ds(first, rows), :] = tile[plane * rows : (plane + 1) * rows]
    chunks = level.chunks
    for q in range(count):
        for p, (a, b) in enumerate(PHASES):
            for t in range(chunks):
                picked = [natural[plane, 2 * q + b, pl.ds(2 * t + a, 8, stride=2 * chunks), :] for plane in range(4)]
                lane, row = pl.ds(128 * q, 128), 8 * t
                for s in range(2):
                    level.fine[s * 4 + p, pl.ds(row, 8), lane] = picked[s]
                level.coef[p, pl.ds(row, 8), lane] = picked[2]
                level.coef[4 + p, pl.ds(row, 8), lane] = picked[2] + picked[3]


def spread(level, natural):
    count, chunks = level.lanes // 128, level.chunks
    for s in range(2):
        for q in range(count):
            for p, (a, b) in enumerate(PHASES):
                for t in range(chunks):
                    value = level.ends[s * 4 + p, pl.ds(8 * t, 8), pl.ds(128 * q, 128)]
                    natural[s, 2 * q + b, pl.ds(2 * t + a, 8, stride=2 * chunks), :] = value


def merged(level, first, rows, natural, matrix):
    count = level.lanes // 128
    slot = slots(count)
    halves = []
    for b in range(2):
        tiles = []
        for q in range(count):
            tiles.append(jnp.concatenate([natural[s, 2 * q + b, pl.ds(first, rows), :] for s in range(2)], axis=0))
        halves.append(exchanged(tiles, slot))
    blocks = [permuted(jnp.concatenate([halves[0][k], halves[1][k]], axis=1), matrix) for k in range(count)]
    return [[block[s * rows : (s + 1) * rows] for block in blocks] for s in range(2)]


def woven(natural, first, rows):
    lane = lax.broadcasted_iota(jnp.int32, (8, 128), 1)
    results = []
    for s in range(2):
        blocks = []
        for at in range(0, rows, 8):
            pair = [natural[s, b, pl.ds(pl.multiple_of(first + at, 8), 8), :] for b in range(2)]
            halves = []
            for k in range(2):
                even, odd = (jnp.take_along_axis(x, (lane >> 1) + 64 * k, axis=1) for x in pair)
                halves.append(jnp.where((lane & 1) == 0, even, odd))
            blocks.append(jnp.concatenate(halves, axis=1))
        results.append([jnp.concatenate(blocks, axis=0)])
    return results


def own_first(rows):
    return pl.multiple_of(lax.axis_index("gx") * rows, rows)


def source_list(refs, rows, parts):
    if parts == 2:
        mine = own_first(rows)
        state, feed, kill = refs[4:]
        other = [state.at[0], state.at[1], feed, kill]
        return [(refs[:4], mine), (other, pl.multiple_of(rows - mine, rows))]
    state, feed, kill = refs
    return [([state.at[g, 0], state.at[g, 1], feed.at[g], kill.at[g]], g * rows) for g in range(parts)]


def interior_kernel(parts, rows, columns, halo, depth, width, start, finish, *refs):
    refs = list(refs)
    take = lambda count: [refs.pop(0) for _ in range(count)]
    here = columns // 2 if parts == 2 else columns
    origin = pl.multiple_of(lax.axis_index("gx") * here, here) if parts == 2 else 0
    seam = 4 * depth if parts == 2 else 0
    side = (width - seam) // 2 - halo
    ins = take(7 if parts == 2 else 3) if start else []
    names = [] if finish and start else list(HANDED)
    handed = take(len(names)) if not start else []
    window = take(1)[0] if start else None
    outs = take(2 if parts == 2 else 1) if finish else []
    handed = handed or take(len(names))
    names += [name for name in PLANES if name not in names] if start else ["ends"]
    handed += take(len(names) - len(handed))
    (natural,) = take(1)
    level = Level(dict(zip(names, handed)), parts * rows // 2, here // 2, None)

    def reader(planes):
        return lambda plane, block: planes[plane][:, pl.ds(origin + 256 * block, 256)]

    if start:
        sources = []
        for planes, first in source_list(ins, rows, parts):
            sources.append((reader(planes), first))
            for plane in range(4):
                value = planes[plane][...]
                blank = jnp.zeros((rows, halo), F32)
                cuts = [blank, value[:, :side], value[:, (columns - seam) // 2 : (columns + seam) // 2]]
                cuts += [value[:, columns - side :], blank]
                window[plane, pl.ds(first, rows), :] = jnp.concatenate([cut for cut in cuts if cut.shape[1]], axis=1)
        load_planes(level, sources, here, natural)
    level.run(lax.axis_index("ta"), start, finish)
    if finish:
        spread(level, natural)
        matrix = group_matrix(level.lanes // 128, True)
        mine = own_first(rows)
        firsts = [mine, pl.multiple_of(rows - mine, rows)] if parts == 2 else [mine]
        for target, first in zip(outs, firsts):
            blocks = merged(level, first, rows, natural, matrix)
            for s in range(2):
                for k, block in enumerate(blocks[s]):
                    target[s, :, pl.ds(256 * k, 256)] = block


def border_kernel(parts, rows, halo, depth, width, window, near, far, out, *work):
    lanes = width // 2
    index, size = lax.axis_index("gy"), lax.axis_size("gy")
    swap = lax.rem(index, 2) == 0
    if parts == 2:
        swap = swap == (lax.axis_index("gx") == 0)
    tiles = lanes // 128
    at = lax.broadcasted_iota(jnp.int32, (1, lanes), 1)
    at = tiles * (at % 128) + at // 128
    outside = ((at < halo // 2) & (index == 0)) | ((at >= lanes - halo // 2) & (index == size - 1))
    level = Level(dict(zip(PLANES, work)), parts * rows // 2, lanes, jnp.where(outside, 0.0, 1.0))

    strips = []
    for edge, (a, b) in ((0, (far, near)), (size - 1, (near, far))):
        strip = jnp.where(index == edge, 0.0, jnp.where(swap, a[...], b[...]))
        strips.append(strip)

    def reader(first):
        def read(plane, block):
            low, high = (unfolded(strip, first, rows, plane, depth, parts * rows) for strip in strips)
            own = window[plane, pl.ds(first, rows), :]
            cuts = [own[:, : halo - depth], low, own[:, halo : width - halo], high, own[:, width - halo + depth :]]
            whole = jnp.concatenate([cut for cut in cuts if cut.shape[1]], axis=1)
            return whole[:, 256 * block : 256 * block + 256]

        return read

    load_planes(level, [(reader(g * rows), g * rows) for g in range(parts)], width, work[-1])
    level.run(lax.axis_index("ta"))
    spread(level, work[-1])
    natural = woven(work[-1], own_first(rows), rows) if tiles == 1 else None
    natural = natural or merged(level, own_first(rows), rows, work[-1], group_matrix(tiles, True))
    for s in range(2):
        for k, block in enumerate(natural[s]):
            out[s, :, pl.ds(256 * k, 256)] = block


def final_kernel(halo, depth, width, inner, border, out):
    total = out.shape[-1]
    out[0] = inner[...]
    for s in range(2):
        for column, source in ((0, halo), (total - depth, width - halo - depth)):
            low = column // 128 * 128
            high = round_up(column + depth, 128)
            old, new = out[0, s, :, pl.ds(low, high - low)], border[s][:, source : source + depth]
            parts_of = [old[:, : column - low], new, old[:, column + depth - low :]]
            out[0, s, :, pl.ds(low, high - low)] = jnp.concatenate([x for x in parts_of if x.shape[1]], axis=1)


def joined_kernel(halo, depth, width, keep, got, border, out, ends, middle, sems):
    total = out.shape[-1]
    half = total // 2
    tile = round_up(depth, 128)
    core = lax.axis_index("gx")
    copies = []
    for k, value in enumerate((keep, got)):
        origin = pl.multiple_of((core if k == 0 else 1 - core) * half + tile, 128)
        inside = pl.ds(tile, half - 2 * tile)
        target = out.at[0, :, :, pl.ds(origin, half - 2 * tile)]
        copies.append(pltpu.make_async_copy(value.at[:, :, inside], target, sems.at[k]))
        copies[-1].start()
    first = core == 0
    low, high = pl.ds(0, tile), pl.ds(half - tile, tile)
    for s in range(2):
        old = [jnp.where(first, a[s, :, at], b[s, :, at]) for a, b in ((keep, got), (got, keep)) for at in (low, high)]
        new = border[s]
        starts = (halo, width // 2 - depth, width // 2, width - halo - depth)
        new = [new[:, at : at + depth] for at in starts]
        ends[0, s] = jnp.concatenate([new[0], old[0][:, depth:]], axis=1)
        ends[1, s] = jnp.concatenate([old[3][:, : tile - depth], new[3]], axis=1)
        middle[s] = jnp.concatenate([old[1][:, : tile - depth], new[1], new[2], old[2][:, depth:]], axis=1)
    copies.append(pltpu.make_async_copy(ends.at[0], out.at[0, :, :, pl.ds(0, tile)], sems.at[2]))
    copies.append(pltpu.make_async_copy(ends.at[1], out.at[0, :, :, pl.ds(total - tile, tile)], sems.at[3]))
    copies.append(pltpu.make_async_copy(middle, out.at[0, :, :, pl.ds(half - tile, 2 * tile)], sems.at[4]))
    for copy in copies[2:]:
        copy.start()
    for copy in copies:
        copy.wait()


def folds(rows, columns):
    tiles, spare = rows // 8, max(128 // columns - 4, 0)
    return (-(-4 * tiles // (spare + 4)), spare) if spare else (tiles, 0)


def folded(strip, columns):
    rows = strip.shape[0]
    kept, spare = folds(rows, columns)
    if not spare:
        return strip
    tail = [(row, plane) for row in range(8 * kept, rows, 8) for plane in range(4)]
    tiles = []
    for k in range(kept):
        beside = [strip[row : row + 8, p * columns : (p + 1) * columns] for row, p in tail[k * spare : (k + 1) * spare]]
        blank = jnp.zeros((8, 128 - (4 + len(beside)) * columns), F32)
        cuts = [strip[8 * k : 8 * k + 8], *beside, blank]
        tiles.append(jnp.concatenate([cut for cut in cuts if cut.shape[1]], axis=1))
    return jnp.concatenate(tiles, axis=0)


def unfolded(value, first, rows, plane, columns, total):
    kept, spare = folds(total, columns)
    tiles = []
    for row in range(first, first + rows, 8):
        at, lane = row, plane * columns
        if spare and row >= 8 * kept:
            index = (row // 8 - kept) * 4 + plane
            at, lane = index // spare * 8, (4 + index % spare) * columns
        tiles.append(value[at : at + 8, lane : lane + columns])
    return jnp.concatenate(tiles, axis=0)


def pack_kernel(parts, rows, depth, *refs):
    count = 7 if parts == 2 else 3
    ins, outs = refs[:count], refs[count:]
    even = lax.rem(lax.axis_index("gy"), 2) == 0
    sources = source_list(ins, rows, parts)
    total, tile = ins[-1].shape[-1], round_up(depth, 128)
    if parts == 2 and depth <= 32:
        first = lax.axis_index("gx") == 0
        upper = even == first
        column = pl.multiple_of(jnp.where(upper, total - tile, 0), 128)
        offset = jnp.where(upper, tile - depth, 0)
        lane = lax.broadcasted_iota(jnp.int32, (1, 128), 1)
        strip = jnp.zeros((2 * rows, 128), F32)
        for plane in range(4):
            own, other = (planes[plane][:, pl.ds(column, tile)] for planes, _ in sources)
            value = jnp.concatenate([jnp.where(first, own, other), jnp.where(first, other, own)], axis=0)
            value = pltpu.roll(value, lax.rem(plane * depth + 128 - offset, 128), 1)
            strip = jnp.where((lane >= plane * depth) & (lane < (plane + 1) * depth), value, strip)
        outs[0][...] = folded(strip[:, : 4 * depth], depth)
        return
    strips = []
    for planes, _ in sources:
        low = jnp.concatenate([ref[:, pl.ds(0, tile)][:, :depth] for ref in planes], axis=1)
        high = jnp.concatenate([ref[:, pl.ds(total - tile, tile)][:, tile - depth :] for ref in planes], axis=1)
        strips.append((jnp.where(even, high, low), jnp.where(even, low, high)))
    if parts == 2:
        first = lax.axis_index("gx") == 0
        (own_a, own_b), (other_a, other_b) = strips
        own, other = jnp.where(first, own_a, own_b), jnp.where(first, other_a, other_b)
        whole = [jnp.concatenate([jnp.where(first, own, other), jnp.where(first, other, own)], axis=0)]
    else:
        whole = [jnp.concatenate(each, axis=0) for each in zip(*strips)]
    for out, strip in zip(outs, whole):
        out[...] = folded(strip, depth)


def fetch_kernel(state, feed, kill, *refs):
    planes, sems = refs[:4], refs[4]
    sources = (state.at[0], state.at[1], feed, kill)
    copies = [pltpu.make_async_copy(sources[i], planes[i], sems.at[i]) for i in range(4)]
    for copy in copies:
        copy.start()
    for copy in copies:
        copy.wait()


def both_ways(pairs):
    return [pair for low, high in pairs for pair in ((low, high), (high, low))]


VMEM = pl.BlockSpec(memory_space=pltpu.VMEM)
ANY = pl.BlockSpec(memory_space=pl.ANY)


def arrays(shapes):
    return [jax.ShapeDtypeStruct(shape, F32) for shape in shapes]


def buffers(shapes):
    return [pltpu.VMEM(shape, F32) for shape in shapes]


def size_of(shapes):
    return sum(4 * math.prod(shape) for shape in shapes)


def called(name, kernel, outs, scratch, limit, inputs, specs=VMEM, out_specs=VMEM, flops=0):
    return pl.pallas_call(
        kernel,
        out_shape=outs,
        in_specs=[specs] * len(inputs),
        out_specs=[out_specs] * len(outs),
        scratch_shapes=scratch,
        compiler_params=pltpu.CompilerParams(vmem_limit_bytes=limit),
        cost_estimate=pl.CostEstimate(flops=flops, bytes_accessed=flops // 2, transcendentals=0),
        name=name,
    )(*inputs)


def per_device(initial_state, feed_rate, kill_rate):
    slices, parts, blocks = (lax.axis_size(axis) for axis in ("ta", "gx", "gy"))
    _, rows, columns = initial_state.shape
    depth = 2 * (2 * slices + 2)
    halo = round_up(depth, 32)
    seam = 4 * depth if parts == 2 else 0
    width = round_up(2 * halo + 4 * depth + seam, 256)
    every = parts * rows
    here = columns // 2 if parts == 2 else columns
    given = (initial_state, feed_rate, kill_rate)
    plane_bytes = 4 * every * columns

    low_pairs = both_ways([(i, i + 1) for i in range(0, blocks - 1, 2)])
    high_pairs = both_ways([(i, (i + 1) % blocks) for i in range(1, blocks - blocks % 2, 2)])

    def crossed(value):
        return lax.ppermute(value, "gx", [(0, 1), (1, 0)])

    if parts == 2:
        others = [crossed(value) for value in given]
        limit = 1709 * 2**15
        own = called("fetch", fetch_kernel, arrays([(rows, columns)] * 4), [pltpu.SemaphoreType.DMA((4,))], limit, given, ANY)
        fields = [*own, *others]
    else:
        fields = [lax.all_gather(value, "gx") for value in given]
    pack = functools.partial(pack_kernel, parts, rows, depth)
    kept, spare = folds(every, depth)
    strips = arrays([(8 * kept, 128 if spare else 4 * depth)] * (1 if parts == 2 else 2))
    sent = called("pack", pack, strips, [], 8 * plane_bytes + 2**22, fields)
    if parts == 2:
        pairs = []
        for n in range(slices):
            base = n * 2 * blocks
            inner_pairs = both_ways([(i, i + 1) for i in range(1, blocks - 1, 2)])
            pairs += [(base + source, base + target) for source, target in low_pairs]
            pairs += [(base + blocks + source, base + blocks + target) for source, target in inner_pairs]
            if n ^ 1 < slices:
                met = {0, blocks - 1} - {source for source, _ in inner_pairs}
                pairs += [(base + blocks + i, (n ^ 1) * 2 * blocks + blocks + i) for i in sorted(met)]
        near = lax.ppermute(sent[0], ("ta", "gx", "gy"), pairs)
    else:
        near = lax.ppermute(sent[0], "gy", low_pairs)
        far = lax.ppermute(sent[1], "gy", high_pairs)

    natural = natural_shape(every // 2, here // 2)
    everything = shapes_of(PLANES, every // 2, here // 2) + [natural]
    limit = size_of(everything) + 32 * every * (columns + width) + 2**22
    interior = functools.partial(interior_kernel, parts, rows, columns, halo, depth, width)
    window_shape = (4, every, width)
    result_shape = (2, rows, here)
    if parts == 2:
        first = functools.partial(interior, True, False)
        handed = shapes_of(HANDED, every // 2, here // 2)
        scratch = buffers(shapes_of([name for name in PLANES if name not in HANDED], every // 2, here // 2) + [natural])
        made = called("interior", first, arrays([window_shape] + handed), scratch, limit, fields, flops=2**24)
        near, window, *made = lax.optimization_barrier((near, *made))
        far = crossed(near)
        last = functools.partial(interior, False, True)
        scratch = buffers(shapes_of(["ends"], every // 2, here // 2) + [natural])
        keep, give = called("own", last, arrays([result_shape] * 2), scratch, limit, made, flops=2**34)
        inner = [keep, crossed(give)]
    else:
        whole = functools.partial(interior, True, True)
        shapes = [window_shape, result_shape]
        window, *inner = called("interior", whole, arrays(shapes), buffers(everything), limit, fields, flops=2**24)
    work = shapes_of(PLANES, every // 2, width // 2) + [natural_shape(every // 2, width // 2)]
    limit = size_of(work) + 32 * every * width + 2**23
    border = functools.partial(border_kernel, parts, rows, halo, depth, width)
    (edges,) = called("border", border, arrays([(2, rows, width)]), buffers(work), limit, (window, near, far), flops=2**34)
    result = arrays([(1, 2, rows, columns)])
    if parts == 2:
        tile = round_up(depth, 128)
        scratch = buffers([(2, 2, rows, tile), (2, rows, 2 * tile)]) + [pltpu.SemaphoreType.DMA((5,))]
        final = functools.partial(joined_kernel, halo, depth, width)
        (out,) = called("final", final, result, scratch, 2**23, (*inner, edges), out_specs=ANY)
    else:
        final = functools.partial(final_kernel, halo, depth, width)
        (out,) = called("final", final, result, [], 16 * plane_bytes + 2**22, (*inner, edges))
    return out


def solution(mesh):
    placed = (P(None, "gx", "gy"), P("gx", "gy"), P("gx", "gy"))
    return jax.shard_map(
        per_device, mesh=mesh, in_specs=placed, out_specs=P("ta", None, "gx", "gy"), check_vma=False
    )
```

```python
import functools
import math

import jax
import jax.numpy as jnp
from jax import lax
from jax.experimental import pallas as pl
from jax.experimental.pallas import tpu as pltpu
from jax.sharding import PartitionSpec as P

TURNS = 2

DIFF_U = 0.2
DIFF_V = 0.1
HALF_STEP = 0.5
W0 = (5.0 / 24.0, 1.0 / 3.0, -1.0 / 24.0)
W1 = (-1.0 / 24.0, 1.0 / 3.0, 5.0 / 24.0)
F32 = jnp.float32
BF16 = jnp.bfloat16
PHASES = ((0, 0), (0, 1), (1, 0), (1, 1))


def round_up(value, step):
    return -(-value // step) * step


def thirds(value):
    high = value.astype(BF16)
    rest = value - high.astype(F32)
    middle = rest.astype(BF16)
    low = (rest - middle.astype(F32)).astype(BF16)
    return high, middle, low


def permuted(value, matrix):
    rows = value.shape[0]
    parts = jnp.concatenate(thirds(value), axis=0)
    moved = jnp.dot(parts, matrix, preferred_element_type=F32)
    return (moved[2 * rows :] + moved[rows : 2 * rows]) + moved[:rows]


def group_matrix(tiles, inverse):
    group, bits = 128 // tiles, (tiles - 1).bit_length()
    source = lax.broadcasted_iota(jnp.int32, (256, 256), 0)
    target = lax.broadcasted_iota(jnp.int32, (1, 256), 1)
    if inverse:
        wanted = ((target & 1) << 7) + (((target >> 1) & (tiles - 1)) << (7 - bits)) + (target >> (1 + bits))
    else:
        wanted = ((target & (group - 1)) << (1 + bits)) + (((target & 127) >> (7 - bits)) << 1) + (target >> 7)
    return jnp.where(source == wanted, 1.0, 0.0).astype(BF16)


def exchanged(tiles, slot):
    count = len(tiles)
    if count == 1:
        return tiles
    group = 128 // count
    turned = [pltpu.roll(tile, k * group, 1) if k else tile for k, tile in enumerate(tiles)]
    results = []
    for q in range(count):
        value = turned[(count - q) % count]
        for at in range(1, count):
            value = jnp.where(slot == at, turned[(at - q) % count], value)
        results.append(pltpu.roll(value, (count - q) * group, 1) if q else value)
    return results


def slots(tiles):
    return lax.broadcasted_iota(jnp.int32, (1, 128), 1) >> (7 - (tiles - 1).bit_length())


C_X0, C_X1, C_X2, C_END, C_C1, C_NEW, C_E1, C_D1, C_D2, C_D2_BEFORE = (2 * i for i in range(10))
COARSE_STENCIL = 20
N_LAST, N_K0, N_K1, N_G0, N_RA, N_RB, N_RE, N_F1, N_RF2 = (2 * i for i in range(9))
COARSE_PLAIN = 18


PLANES = {
    "fine": 24,
    "lin": 24,
    "coef": 8,
    "cs": COARSE_STENCIL,
    "cp": COARSE_PLAIN,
    "cc": 2,
    "mom": 8,
    "fresh": 8,
    "rest": 8,
    "tl": 24,
    "ends": 8,
}
HANDED = ("fresh", "rest", "coef", "cs")


def shapes_of(names, rows, lanes):
    return [(PLANES[name], rows, lanes) for name in names]


def natural_shape(rows, lanes):
    return (4, 2 * lanes // 128, 2 * rows, 128)


class Level:
    def __init__(self, refs, rows, lanes, mask, slices=0):
        self.slices = slices
        for name, ref in refs.items():
            setattr(self, name, ref)
        self.rows, self.lanes, self.mask = rows, lanes, mask
        self.chunks = rows // 8
        self.recent = {}

    def each(self, body):
        if self.chunks <= 4:
            for i in range(self.chunks):
                body(8 * i)
        else:
            pl.loop(0, self.chunks)(lambda i: body(pl.multiple_of(8 * i, 8)))

    def left(self, value):
        if self.lanes == 128:
            return pltpu.roll(value, 1, 1)
        return jnp.concatenate([pltpu.roll(value[:, -128:], 1, 1), value[:, :-128]], axis=1)

    def right(self, value):
        if self.lanes == 128:
            return pltpu.roll(value, 127, 1)
        return jnp.concatenate([value[:, 128:], pltpu.roll(value[:, :128], 127, 1)], axis=1)

    def scaled(self, value, factor):
        if self.mask is None:
            return factor * value
        return (factor * self.mask) * value

    def known(self, ref, plane, row):
        return self.recent.get((id(ref), plane, row)) if self.slices else None

    def note(self, ref, plane, row, value):
        if self.slices:
            self.recent[id(ref), plane, row] = value

    def at(self, ref, plane, row, shift=0):
        target = row + 8 * shift
        if isinstance(row, int) and 0 <= target < self.rows:
            return self.get(ref, plane, target)
        sublane = lax.broadcasted_iota(jnp.int32, (8, 1), 0)
        if isinstance(row, int):
            value = self.get(ref, plane, target % self.rows)
            return jnp.where(sublane == (0 if shift < 0 else 7), 0.0, pltpu.roll(value, 1 if shift < 0 else 7, 0))
        if shift == 0:
            return ref[plane, pl.ds(row, 8), :]
        inside = (target >= 0) & (target < self.rows)
        value = ref[plane, pl.ds(pl.multiple_of(lax.rem(target + self.rows, self.rows), 8), 8), :]
        wrapped = jnp.where(sublane == (0 if shift < 0 else 7), 0.0, pltpu.roll(value, 1 if shift < 0 else 7, 0))
        return jnp.where(inside, value, wrapped)

    def put(self, ref, plane, row, value, lane=slice(None)):
        ref[plane, pl.ds(row, 8), lane] = value
        if isinstance(row, int) and (lane == slice(None) or self.lanes == 128):
            self.note(ref, plane, row, value)

    def get(self, ref, plane, row):
        value = self.known(ref, plane, row)
        return ref[plane, pl.ds(row, 8), :] if value is None else value

    def set(self, ref, plane, row, value):
        self.put(ref, plane, row, value)

    def fine_rates(self, base, row):
        ref, base = (self.fresh, 0) if base == 3 else (self.fine, base)
        state = [[self.at(ref, base * 8 + s * 4 + p, row) for p in range(4)] for s in range(2)]
        linear, rates = [], []
        for p, (a, b) in enumerate(PHASES):
            laps = []
            for s in range(2):
                across = state[s][2 * a + 1 - b]
                along = state[s][2 * (1 - a) + b]
                moved = self.at(ref, base * 8 + s * 4 + 2 * (1 - a) + b, row, 1 if a else -1)
                side = self.right(across) if b else self.left(across)
                laps.append((along + moved) + (across + side) - 4.0 * state[s][p])
            u, v = state[0][p], state[1][p]
            feed = self.get(self.coef, p, row)
            both = self.get(self.coef, 4 + p, row)
            lin_u = self.scaled(laps[0], DIFF_U) + feed
            lin_v = self.scaled(laps[1], DIFF_V)
            linear.append((lin_u, lin_v))
            rates.append(self.reacted(u, v, lin_u, lin_v, feed, both))
        return state, linear, rates

    def reacted(self, u, v, lin_u, lin_v, feed, both):
        return lin_u - u * (feed + v * v), lin_v + v * (u * v - both)

    def neighbours(self, plane, row, value):
        rows = self.at(self.cs, plane, row, -1) + self.at(self.cs, plane, row, 1)
        return rows + (self.left(value) + self.right(value))

    def laplacians(self, first, row):
        pair = [self.at(self.cs, first + s, row) for s in range(2)]
        return pair, [self.neighbours(first + s, row, pair[s]) - 4.0 * pair[s] for s in range(2)]

    def coarse_rates(self, first, row):
        (u, v), laps = self.laplacians(first, row)
        scaled = [self.scaled(laps[s], 0.25 * (DIFF_U, DIFF_V)[s]) for s in range(2)]
        feed, both = self.get(self.cc, 0, row), self.get(self.cc, 1, row)
        return (u, v), scaled, self.reacted(u, v, scaled[0] + feed, scaled[1], feed, both)

    def moved_rates(self, shift, scaled, which, base, row):
        a, b = shift
        m_vv, m_uv, m_u, m_v = (self.get(self.mom, 4 * which + k, row) for k in range(4))
        react = a * (m_vv + b * (2.0 * m_v + b)) + b * (2.0 * m_uv + b * m_u)
        feed, both = self.get(self.cc, 0, row), self.get(self.cc, 1, row)
        rate_u = (self.get(self.cp, base, row) + 2.0 * scaled[0]) - (feed * a + react)
        rate_v = (self.get(self.cp, base + 1, row) + 2.0 * scaled[1]) + (react - both * b)
        return rate_u, rate_v

    def block_mean(self, values):
        return 0.25 * ((values[0] + values[1]) + (values[2] + values[3]))

    def run(self, own, start=True, finish=True):
        lv = self
        cs, cp = self.cs, getattr(self, "cp", None)

        def first_sweep(row):
            for k in range(2):
                lv.set(lv.cc, k, row, lv.block_mean([lv.get(lv.coef, 4 * k + p, row) for p in range(4)]))
            state, linear, rates = lv.fine_rates(0, row)
            for s in range(2):
                for p in range(4):
                    lv.set(lv.lin, s * 4 + p, row, linear[p][s])
                    lv.put(lv.fine, 8 + s * 4 + p, row, state[s][p] + HALF_STEP * rates[p][s])
                mean = lv.block_mean([r[s] for r in rates])
                start = lv.block_mean(state[s])
                lv.set(cp, N_RA + s, row, mean)
                lv.put(cs, C_X0 + s, row, start)
                lv.put(cs, C_X1 + s, row, start + HALF_STEP * mean)
                lv.put(cs, C_END + s, row, start + mean)
                lv.put(cs, C_D1 + s, row, jnp.zeros_like(mean))
                lv.put(cs, C_D2 + s, row, jnp.zeros_like(mean))

        def moments(which, state, row):
            u, v = state
            lv.set(lv.mom, 4 * which, row, lv.block_mean([v[p] * v[p] for p in range(4)]))
            lv.set(lv.mom, 4 * which + 1, row, lv.block_mean([u[p] * v[p] for p in range(4)]))
            lv.set(lv.mom, 4 * which + 2, row, lv.block_mean(u))
            lv.set(lv.mom, 4 * which + 3, row, lv.block_mean(v))

        def second_sweep(row):
            state, linear, rates = lv.fine_rates(1, row)
            _, _, g0 = lv.coarse_rates(C_X0, row)
            first, scaled, g1 = lv.coarse_rates(C_X1, row)
            for s in range(2):
                for p in range(4):
                    lv.set(lv.lin, 8 + s * 4 + p, row, linear[p][s])
                    lv.put(lv.fine, 16 + s * 4 + p, row, state[s][p] + HALF_STEP * rates[p][s])
                mean = lv.block_mean([r[s] for r in rates])
                lv.set(cp, N_F1 + s, row, mean)
                lv.set(cp, N_RB + s, row, mean - 2.0 * scaled[s])
                lv.put(cs, C_X2 + s, row, first[s] + HALF_STEP * mean)
                integral = HALF_STEP * lv.get(cp, N_RA + s, row)
                lv.set(cp, N_K0 + s, row, integral - HALF_STEP * g0[s])
                lv.set(cp, N_K1 + s, row, integral - HALF_STEP * g1[s])
            moments(0, state, row)

        def third_sweep(row):
            state, linear, rates = lv.fine_rates(2, row)
            for s in range(2):
                for p in range(4):
                    lv.set(lv.lin, 16 + s * 4 + p, row, linear[p][s])
            moments(1, state, row)
            second, laps = lv.laplacians(C_X2, row)
            for s in range(2):
                mean = lv.block_mean([r[s] for r in rates])
                lv.set(cp, N_RE + s, row, mean - lv.scaled(laps[s], 0.5 * (DIFF_U, DIFF_V)[s]))
            end, last = slice_end(row)
            for s in range(2):
                j0, j1 = integrals(lv.get(cp, N_RA + s, row), lv.get(cp, N_F1 + s, row), last[s])
                lv.put(cs, C_NEW + s, row, lv.at(cs, C_X0 + s, row) + (j0 + j1))

        def integrals(f0, f1, f2):
            middle = W0[1] * f1
            return middle + (W0[0] * f0 + W0[2] * f2), middle + (W1[0] * f0 + W1[2] * f2)

        def slice_end(row):
            end, scaled, rate = lv.coarse_rates(C_END, row)
            shift = [end[s] - lv.at(cs, C_X2 + s, row) for s in range(2)]
            last = lv.moved_rates(shift, scaled, 1, N_RE, row)
            for s in range(2):
                half = HALF_STEP * rate[s]
                lv.set(cp, N_G0 + s, row, half)
                lv.put(cs, C_C1 + s, row, end[s] + half + lv.get(cp, N_K0 + s, row))
                lv.put(cs, C_D2_BEFORE + s, row, lv.at(cs, C_D2 + s, row))
                lv.put(cs, C_D2 + s, row, shift[s])
                lv.set(cp, N_RF2 + s, row, last[s])
            return end, last

        def middle_nodes(row):
            mid, scaled, rate = lv.coarse_rates(C_C1, row)
            new, _, new_rate = lv.coarse_rates(C_NEW, row)
            shift = [mid[s] - lv.at(cs, C_X1 + s, row) for s in range(2)]
            f1 = lv.moved_rates(shift, scaled, 0, N_RB, row)
            for s in range(2):
                old = lv.at(cs, C_END + s, row)
                lv.set(cp, N_LAST + s, row, old)
                lv.set(cp, N_F1 + s, row, f1[s])
                lv.put(cs, C_D1 + s, row, shift[s])
                lv.put(cs, C_END + s, row, mid[s] + HALF_STEP * rate[s] + lv.get(cp, N_K1 + s, row))
                change = HALF_STEP * new_rate[s] - lv.get(cp, N_G0 + s, row)
                lv.put(cs, C_E1 + s, row, (new[s] - old) + change)

        def end_nodes(row):
            before = [lv.get(cp, N_RF2 + s, row) for s in range(2)]
            _, last = slice_end(row)
            change, laps = lv.laplacians(C_E1, row)
            old, new, j1s = [], [], []
            for s in range(2):
                j0, j1 = integrals(before[s], lv.get(cp, N_F1 + s, row), last[s])
                old.append(lv.get(cp, N_LAST + s, row) + j0)
                new.append(old[s] + change[s])
                j1s.append(j1)
            feed, both = lv.get(lv.cc, 0, row), lv.get(lv.cc, 1, row)
            lin = [lv.scaled(laps[s], 0.25 * (DIFF_U, DIFF_V)[s]) for s in range(2)]
            rate_new = lv.reacted(new[0], new[1], lin[0], lin[1], feed, both)
            rate_old = lv.reacted(old[0], old[1], 0.0, 0.0, feed, both)
            for s in range(2):
                total = new[s] + j1s[s] + HALF_STEP * (rate_new[s] - rate_old[s])
                lv.put(cs, C_NEW + s, row, total)

        def corrections(starts):
            def body(row):
                for k, first in enumerate(starts):
                    for s in range(2):
                        d = lv.at(cs, first + s, row)
                        ring = [lv.at(cs, first + s, row, -1), lv.at(cs, first + s, row, 1), lv.left(d), lv.right(d)]
                        north, south, west, east = (lv.scaled(x - d, (DIFF_U, DIFF_V)[s]) for x in ring)
                        for p, (a, b) in enumerate(PHASES):
                            lv.set(lv.tl, k * 8 + s * 4 + p, row, (south if a else north) + (east if b else west))

            return body

        def one_slice(n, carry):
            lv.each(middle_nodes)
            lv.each(end_nodes)
            return carry

        origin = jnp.where(own == 0, 0, 2)
        starts = (C_D2_BEFORE, C_D1, C_D2)
        def own_nodes(row):
            for p in range(4):
                for t in range(0, lv.lanes, 128):
                    lane = pl.ds(t, 128)
                    tile = pl.ds(row, 8)
                    if lv.lanes == 128:
                        take = lambda ref, plane: lv.get(ref, plane, row)
                    else:
                        take = lambda ref, plane, lane=lane: ref[plane, tile, lane]
                    feed, both = take(lv.coef, p), take(lv.coef, 4 + p)
                    rates, start = [], None
                    for k, (base, d) in enumerate(zip((origin, 1, 2), starts)):
                        pair = [take(lv.fine, base * 8 + s * 4 + p) + take(cs, d + s) for s in range(2)]
                        lin = [take(lv.lin, base * 8 + s * 4 + p) + take(lv.tl, k * 8 + s * 4 + p) for s in range(2)]
                        rates.append(lv.reacted(pair[0], pair[1], lin[0], lin[1], feed, both))
                        start = pair if k == 0 else start
                    for s in range(2):
                        f0, f1, f2 = (r[s] for r in rates)
                        second = start[s] + (W0[0] * f0 + W0[1] * f1 + W0[2] * f2)
                        lv.put(lv.fresh, s * 4 + p, row, second, lane)
                        lv.put(lv.rest, s * 4 + p, row, second + (W1[0] * f0 + (W1[1] - HALF_STEP) * f1 + W1[2] * f2), lane)

        def last_node(row):
            _, _, rates = lv.fine_rates(3, row)
            for s in range(2):
                ends = [lv.get(lv.rest, s * 4 + p, row) + HALF_STEP * rates[p][s] for p in range(4)]
                fix = lv.at(cs, C_NEW + s, row) - lv.block_mean(ends)
                for p in range(4):
                    lv.set(lv.ends, s * 4 + p, row, ends[p] + fix)

        def sweeps():
            lv.each(first_sweep)
            lv.each(second_sweep)
            lv.each(third_sweep)

        def written_out(count):
            nonlocal origin
            origin = 0 if count == 0 else 2
            self.recent = {}
            sweeps()
            for n in range(1, count + 1):
                one_slice(n, 0)
            lv.each(corrections(starts))
            lv.each(own_nodes)
            if finish:
                lv.each(last_node)

        if start and self.slices:
            for count in range(self.slices):
                pl.when(own == count)(functools.partial(written_out, count))
            return
        if start:
            sweeps()
            lax.fori_loop(1, own + 1, one_slice, 0)
            lv.each(corrections(starts))
            lv.each(own_nodes)
        if finish:
            lv.each(last_node)


def load_planes(level, sources, columns, natural):
    count = level.lanes // 128
    matrix = group_matrix(count, False)
    slot = slots(count)
    for read, first in sources:
        blocks = []
        for k in range(count):
            values = [read(plane, k) for plane in range(4)]
            blocks.append(permuted(jnp.concatenate(values, axis=0), matrix))
        rows = blocks[0].shape[0] // 4
        for b in range(2):
            tiles = exchanged([block[:, 128 * b : 128 * b + 128] for block in blocks], slot)
            for q, tile in enumerate(tiles):
                for plane in range(4):
                    natural[plane, 2 * q + b, pl.ds(first, rows), :] = tile[plane * rows : (plane + 1) * rows]
    chunks = level.chunks
    for q in range(count):
        for p, (a, b) in enumerate(PHASES):
            for t in range(chunks):
                picked = [natural[plane, 2 * q + b, pl.ds(2 * t + a, 8, stride=2 * chunks), :] for plane in range(4)]
                lane, row = pl.ds(128 * q, 128), 8 * t
                for s in range(2):
                    level.fine[s * 4 + p, pl.ds(row, 8), lane] = picked[s]
                level.coef[p, pl.ds(row, 8), lane] = picked[2]
                level.coef[4 + p, pl.ds(row, 8), lane] = picked[2] + picked[3]


def spread(level, natural):
    count, chunks = level.lanes // 128, level.chunks
    for s in range(2):
        for q in range(count):
            for p, (a, b) in enumerate(PHASES):
                for t in range(chunks):
                    value = level.ends[s * 4 + p, pl.ds(8 * t, 8), pl.ds(128 * q, 128)]
                    natural[s, 2 * q + b, pl.ds(2 * t + a, 8, stride=2 * chunks), :] = value


def merged(level, first, rows, natural, matrix):
    count = level.lanes // 128
    slot = slots(count)
    halves = []
    for b in range(2):
        tiles = []
        for q in range(count):
            tiles.append(jnp.concatenate([natural[s, 2 * q + b, pl.ds(first, rows), :] for s in range(2)], axis=0))
        halves.append(exchanged(tiles, slot))
    blocks = [permuted(jnp.concatenate([halves[0][k], halves[1][k]], axis=1), matrix) for k in range(count)]
    return [[block[s * rows : (s + 1) * rows] for block in blocks] for s in range(2)]


def woven(natural, first, rows):
    lane = lax.broadcasted_iota(jnp.int32, (8, 128), 1)
    results = []
    for s in range(2):
        blocks = []
        for at in range(0, rows, 8):
            pair = [natural[s, b, pl.ds(pl.multiple_of(first + at, 8), 8), :] for b in range(2)]
            halves = []
            for k in range(2):
                even, odd = (jnp.take_along_axis(x, (lane >> 1) + 64 * k, axis=1) for x in pair)
                halves.append(jnp.where((lane & 1) == 0, even, odd))
            blocks.append(jnp.concatenate(halves, axis=1))
        results.append([jnp.concatenate(blocks, axis=0)])
    return results


def own_first(rows):
    return pl.multiple_of(lax.axis_index("gx") * rows, rows)


def source_list(refs, rows, parts):
    if parts == 2:
        mine = own_first(rows)
        state, feed, kill = refs[4:]
        other = [state.at[0], state.at[1], feed, kill]
        return [(refs[:4], mine), (other, pl.multiple_of(rows - mine, rows))]
    state, feed, kill = refs
    return [([state.at[g, 0], state.at[g, 1], feed.at[g], kill.at[g]], g * rows) for g in range(parts)]


def interior_kernel(parts, rows, columns, halo, depth, width, start, finish, *refs):
    refs = list(refs)
    take = lambda count: [refs.pop(0) for _ in range(count)]
    here = columns // 2 if parts == 2 else columns
    origin = pl.multiple_of(lax.axis_index("gx") * here, here) if parts == 2 else 0
    seam = 4 * depth if parts == 2 else 0
    side = (width - seam) // 2 - halo
    ins = take(7 if parts == 2 else 3) if start else []
    names = [] if finish and start else list(HANDED)
    handed = take(len(names)) if not start else []
    window = take(1)[0] if start else None
    outs = take(2 if parts == 2 else 1) if finish else []
    handed = handed or take(len(names))
    names += [name for name in PLANES if name not in names] if start else ["ends"]
    handed += take(len(names) - len(handed))
    (natural,) = take(1)
    level = Level(dict(zip(names, handed)), parts * rows // 2, here // 2, None)

    def reader(planes):
        return lambda plane, block: planes[plane][:, pl.ds(origin + 256 * block, 256)]

    if start:
        sources = []
        for planes, first in source_list(ins, rows, parts):
            sources.append((reader(planes), first))
            for plane in range(4):
                value = planes[plane][...]
                blank = jnp.zeros((rows, halo), F32)
                cuts = [blank, value[:, :side], value[:, (columns - seam) // 2 : (columns + seam) // 2]]
                cuts += [value[:, columns - side :], blank]
                window[plane, pl.ds(first, rows), :] = jnp.concatenate([cut for cut in cuts if cut.shape[1]], axis=1)
        load_planes(level, sources, here, natural)
    level.run(lax.axis_index("ta"), start, finish)
    if finish:
        spread(level, natural)
        matrix = group_matrix(level.lanes // 128, True)
        mine = own_first(rows)
        firsts = [mine, pl.multiple_of(rows - mine, rows)] if parts == 2 else [mine]
        for target, first in zip(outs, firsts):
            blocks = merged(level, first, rows, natural, matrix)
            for s in range(2):
                for k, block in enumerate(blocks[s]):
                    target[s, :, pl.ds(256 * k, 256)] = block


def few(count):
    return count if count <= 4 else 0


def border_kernel(parts, rows, halo, depth, width, window, near, far, out, *work):
    lanes = width // 2
    index, size = lax.axis_index("gy"), lax.axis_size("gy")
    swap = lax.rem(index, 2) == 0
    if parts == 2:
        swap = swap == (lax.axis_index("gx") == 0)
    tiles = lanes // 128
    at = lax.broadcasted_iota(jnp.int32, (1, lanes), 1)
    at = tiles * (at % 128) + at // 128
    outside = ((at < halo // 2) & (index == 0)) | ((at >= lanes - halo // 2) & (index == size - 1))
    level = Level(dict(zip(PLANES, work)), parts * rows // 2, lanes, jnp.where(outside, 0.0, 1.0), few(lax.axis_size("ta")))

    strips = []
    for edge, (a, b) in ((0, (far, near)), (size - 1, (near, far))):
        strip = jnp.where(index == edge, 0.0, jnp.where(swap, a[...], b[...]))
        strips.append(strip)

    def reader(first):
        def read(plane, block):
            low, high = (unfolded(strip, first, rows, plane, depth, parts * rows) for strip in strips)
            own = window[plane, pl.ds(first, rows), :]
            cuts = [own[:, : halo - depth], low, own[:, halo : width - halo], high, own[:, width - halo + depth :]]
            whole = jnp.concatenate([cut for cut in cuts if cut.shape[1]], axis=1)
            return whole[:, 256 * block : 256 * block + 256]

        return read

    load_planes(level, [(reader(g * rows), g * rows) for g in range(parts)], width, work[-1])
    level.run(lax.axis_index("ta"))
    spread(level, work[-1])
    natural = woven(work[-1], own_first(rows), rows) if tiles == 1 else None
    natural = natural or merged(level, own_first(rows), rows, work[-1], group_matrix(tiles, True))
    for s in range(2):
        for k, block in enumerate(natural[s]):
            out[s, :, pl.ds(256 * k, 256)] = block


def final_kernel(halo, depth, width, inner, border, out):
    total = out.shape[-1]
    out[0] = inner[...]
    for s in range(2):
        for column, source in ((0, halo), (total - depth, width - halo - depth)):
            low = column // 128 * 128
            high = round_up(column + depth, 128)
            old, new = out[0, s, :, pl.ds(low, high - low)], border[s][:, source : source + depth]
            parts_of = [old[:, : column - low], new, old[:, column + depth - low :]]
            out[0, s, :, pl.ds(low, high - low)] = jnp.concatenate([x for x in parts_of if x.shape[1]], axis=1)


def joined_kernel(halo, depth, width, keep, got, border, out, ends, middle, sems):
    total = out.shape[-1]
    half = total // 2
    tile = round_up(depth, 128)
    core = lax.axis_index("gx")
    copies = []
    for k, value in enumerate((keep, got)):
        origin = pl.multiple_of((core if k == 0 else 1 - core) * half + tile, 128)
        inside = pl.ds(tile, half - 2 * tile)
        target = out.at[0, :, :, pl.ds(origin, half - 2 * tile)]
        copies.append(pltpu.make_async_copy(value.at[:, :, inside], target, sems.at[k]))
        copies[-1].start()
    first = core == 0
    low, high = pl.ds(0, tile), pl.ds(half - tile, tile)
    for s in range(2):
        old = [jnp.where(first, a[s, :, at], b[s, :, at]) for a, b in ((keep, got), (got, keep)) for at in (low, high)]
        new = border[s]
        starts = (halo, width // 2 - depth, width // 2, width - halo - depth)
        new = [new[:, at : at + depth] for at in starts]
        ends[0, s] = jnp.concatenate([new[0], old[0][:, depth:]], axis=1)
        ends[1, s] = jnp.concatenate([old[3][:, : tile - depth], new[3]], axis=1)
        middle[s] = jnp.concatenate([old[1][:, : tile - depth], new[1], new[2], old[2][:, depth:]], axis=1)
    copies.append(pltpu.make_async_copy(ends.at[0], out.at[0, :, :, pl.ds(0, tile)], sems.at[2]))
    copies.append(pltpu.make_async_copy(ends.at[1], out.at[0, :, :, pl.ds(total - tile, tile)], sems.at[3]))
    copies.append(pltpu.make_async_copy(middle, out.at[0, :, :, pl.ds(half - tile, 2 * tile)], sems.at[4]))
    for copy in copies[2:]:
        copy.start()
    for copy in copies:
        copy.wait()


def folds(rows, columns):
    tiles, spare = rows // 8, max(128 // columns - 4, 0)
    return (-(-4 * tiles // (spare + 4)), spare) if spare else (tiles, 0)


def folded(strip, columns):
    rows = strip.shape[0]
    kept, spare = folds(rows, columns)
    if not spare:
        return strip
    tail = [(row, plane) for row in range(8 * kept, rows, 8) for plane in range(4)]
    tiles = []
    for k in range(kept):
        beside = [strip[row : row + 8, p * columns : (p + 1) * columns] for row, p in tail[k * spare : (k + 1) * spare]]
        blank = jnp.zeros((8, 128 - (4 + len(beside)) * columns), F32)
        cuts = [strip[8 * k : 8 * k + 8], *beside, blank]
        tiles.append(jnp.concatenate([cut for cut in cuts if cut.shape[1]], axis=1))
    return jnp.concatenate(tiles, axis=0)


def unfolded(value, first, rows, plane, columns, total):
    kept, spare = folds(total, columns)
    tiles = []
    for row in range(first, first + rows, 8):
        at, lane = row, plane * columns
        if spare and row >= 8 * kept:
            index = (row // 8 - kept) * 4 + plane
            at, lane = index // spare * 8, (4 + index % spare) * columns
        tiles.append(value[at : at + 8, lane : lane + columns])
    return jnp.concatenate(tiles, axis=0)


def pack_kernel(parts, rows, depth, *refs):
    count = 7 if parts == 2 else 3
    ins, outs = refs[:count], refs[count:]
    even = lax.rem(lax.axis_index("gy"), 2) == 0
    sources = source_list(ins, rows, parts)
    total, tile = ins[-1].shape[-1], round_up(depth, 128)
    if parts == 2 and depth <= 32:
        first = lax.axis_index("gx") == 0
        upper = even == first
        column = pl.multiple_of(jnp.where(upper, total - tile, 0), 128)
        offset = jnp.where(upper, tile - depth, 0)
        lane = lax.broadcasted_iota(jnp.int32, (1, 128), 1)
        strip = jnp.zeros((2 * rows, 128), F32)
        for plane in range(4):
            own, other = (planes[plane][:, pl.ds(column, tile)] for planes, _ in sources)
            value = jnp.concatenate([jnp.where(first, own, other), jnp.where(first, other, own)], axis=0)
            value = pltpu.roll(value, lax.rem(plane * depth + 128 - offset, 128), 1)
            strip = jnp.where((lane >= plane * depth) & (lane < (plane + 1) * depth), value, strip)
        outs[0][...] = folded(strip[:, : 4 * depth], depth)
        return
    strips = []
    for planes, _ in sources:
        low = jnp.concatenate([ref[:, pl.ds(0, tile)][:, :depth] for ref in planes], axis=1)
        high = jnp.concatenate([ref[:, pl.ds(total - tile, tile)][:, tile - depth :] for ref in planes], axis=1)
        strips.append((jnp.where(even, high, low), jnp.where(even, low, high)))
    if parts == 2:
        first = lax.axis_index("gx") == 0
        (own_a, own_b), (other_a, other_b) = strips
        own, other = jnp.where(first, own_a, own_b), jnp.where(first, other_a, other_b)
        whole = [jnp.concatenate([jnp.where(first, own, other), jnp.where(first, other, own)], axis=0)]
    else:
        whole = [jnp.concatenate(each, axis=0) for each in zip(*strips)]
    for out, strip in zip(outs, whole):
        out[...] = folded(strip, depth)


def fetch_kernel(state, feed, kill, *refs):
    planes, sems = refs[:4], refs[4]
    sources = (state.at[0], state.at[1], feed, kill)
    copies = [pltpu.make_async_copy(sources[i], planes[i], sems.at[i]) for i in range(4)]
    for copy in copies:
        copy.start()
    for copy in copies:
        copy.wait()


def both_ways(pairs):
    return [pair for low, high in pairs for pair in ((low, high), (high, low))]


VMEM = pl.BlockSpec(memory_space=pltpu.VMEM)
ANY = pl.BlockSpec(memory_space=pl.ANY)


def arrays(shapes):
    return [jax.ShapeDtypeStruct(shape, F32) for shape in shapes]


def buffers(shapes):
    return [pltpu.VMEM(shape, F32) for shape in shapes]


def size_of(shapes):
    return sum(4 * math.prod(shape) for shape in shapes)


def called(name, kernel, outs, scratch, limit, inputs, specs=VMEM, out_specs=VMEM, flops=0):
    return pl.pallas_call(
        kernel,
        out_shape=outs,
        in_specs=[specs] * len(inputs),
        out_specs=[out_specs] * len(outs),
        scratch_shapes=scratch,
        compiler_params=pltpu.CompilerParams(vmem_limit_bytes=limit),
        cost_estimate=pl.CostEstimate(flops=flops, bytes_accessed=flops // 2, transcendentals=0),
        name=name,
    )(*inputs)


def per_device(initial_state, feed_rate, kill_rate):
    slices, parts, blocks = (lax.axis_size(axis) for axis in ("ta", "gx", "gy"))
    _, rows, columns = initial_state.shape
    depth = 2 * (2 * slices + 2)
    halo = round_up(depth, 32)
    seam = 4 * depth if parts == 2 else 0
    width = round_up(2 * halo + 4 * depth + seam, 256)
    every = parts * rows
    here = columns // 2 if parts == 2 else columns
    given = (initial_state, feed_rate, kill_rate)
    plane_bytes = 4 * every * columns

    low_pairs = both_ways([(i, i + 1) for i in range(0, blocks - 1, 2)])
    high_pairs = both_ways([(i, (i + 1) % blocks) for i in range(1, blocks - blocks % 2, 2)])

    def crossed(value):
        return lax.ppermute(value, "gx", [(0, 1), (1, 0)])

    if parts == 2:
        others = [crossed(value) for value in given]
        limit = 1709 * 2**15
        own = called("fetch", fetch_kernel, arrays([(rows, columns)] * 4), [pltpu.SemaphoreType.DMA((4,))], limit, given, ANY)
        fields = [*own, *others]
    else:
        fields = [lax.all_gather(value, "gx") for value in given]
    pack = functools.partial(pack_kernel, parts, rows, depth)
    kept, spare = folds(every, depth)
    strips = arrays([(8 * kept, 128 if spare else 4 * depth)] * (1 if parts == 2 else 2))
    sent = called("pack", pack, strips, [], 8 * plane_bytes + 2**22, fields)
    if parts == 2:
        pairs = []
        for n in range(slices):
            base = n * 2 * blocks
            inner_pairs = both_ways([(i, i + 1) for i in range(1, blocks - 1, 2)])
            pairs += [(base + source, base + target) for source, target in low_pairs]
            pairs += [(base + blocks + source, base + blocks + target) for source, target in inner_pairs]
            if n ^ 1 < slices:
                met = {0, blocks - 1} - {source for source, _ in inner_pairs}
                pairs += [(base + blocks + i, (n ^ 1) * 2 * blocks + blocks + i) for i in sorted(met)]
        near = lax.ppermute(sent[0], ("ta", "gx", "gy"), pairs)
    else:
        near = lax.ppermute(sent[0], "gy", low_pairs)
        far = lax.ppermute(sent[1], "gy", high_pairs)

    natural = natural_shape(every // 2, here // 2)
    everything = shapes_of(PLANES, every // 2, here // 2) + [natural]
    limit = size_of(everything) + 32 * every * (columns + width) + 2**22
    interior = functools.partial(interior_kernel, parts, rows, columns, halo, depth, width)
    window_shape = (4, every, width)
    result_shape = (2, rows, here)
    if parts == 2:
        first = functools.partial(interior, True, False)
        handed = shapes_of(HANDED, every // 2, here // 2)
        scratch = buffers(shapes_of([name for name in PLANES if name not in HANDED], every // 2, here // 2) + [natural])
        made = called("interior", first, arrays([window_shape] + handed), scratch, limit, fields, flops=2**24)
        near, window, *made = lax.optimization_barrier((near, *made))
        far = crossed(near)
        last = functools.partial(interior, False, True)
        scratch = buffers(shapes_of(["ends"], every // 2, here // 2) + [natural])
        keep, give = called("own", last, arrays([result_shape] * 2), scratch, limit, made, flops=2**34)
        inner = [keep, crossed(give)]
    else:
        whole = functools.partial(interior, True, True)
        shapes = [window_shape, result_shape]
        window, *inner = called("interior", whole, arrays(shapes), buffers(everything), limit, fields, flops=2**24)
    work = shapes_of(PLANES, every // 2, width // 2) + [natural_shape(every // 2, width // 2)]
    limit = size_of(work) + 32 * every * width + 2**23
    border = functools.partial(border_kernel, parts, rows, halo, depth, width)
    (edges,) = called("border", border, arrays([(2, rows, width)]), buffers(work), limit, (window, near, far), flops=2**34)
    result = arrays([(1, 2, rows, columns)])
    if parts == 2:
        tile = round_up(depth, 128)
        scratch = buffers([(2, 2, rows, tile), (2, rows, 2 * tile)]) + [pltpu.SemaphoreType.DMA((5,))]
        final = functools.partial(joined_kernel, halo, depth, width)
        (out,) = called("final", final, result, scratch, 2**23, (*inner, edges), out_specs=ANY)
    else:
        final = functools.partial(final_kernel, halo, depth, width)
        (out,) = called("final", final, result, [], 16 * plane_bytes + 2**22, (*inner, edges))
    return out


def solution(mesh):
    placed = (P(None, "gx", "gy"), P("gx", "gy"), P("gx", "gy"))
    return jax.shard_map(
        per_device, mesh=mesh, in_specs=placed, out_specs=P("ta", None, "gx", "gy"), check_vma=False
    )
```

```python
import functools
import math

import jax
import jax.numpy as jnp
from jax import lax
from jax.experimental import pallas as pl
from jax.experimental.pallas import tpu as pltpu
from jax.sharding import PartitionSpec as P

TURNS = 2

DIFF_U = 0.2
DIFF_V = 0.1
HALF_STEP = 0.5
W0 = (5.0 / 24.0, 1.0 / 3.0, -1.0 / 24.0)
W1 = (-1.0 / 24.0, 1.0 / 3.0, 5.0 / 24.0)
F32 = jnp.float32
BF16 = jnp.bfloat16
PHASES = ((0, 0), (0, 1), (1, 0), (1, 1))


def round_up(value, step):
    return -(-value // step) * step


def thirds(value):
    high = value.astype(BF16)
    rest = value - high.astype(F32)
    middle = rest.astype(BF16)
    low = (rest - middle.astype(F32)).astype(BF16)
    return high, middle, low


def permuted(value, matrix):
    rows = value.shape[0]
    parts = jnp.concatenate(thirds(value), axis=0)
    moved = jnp.dot(parts, matrix, preferred_element_type=F32)
    return (moved[2 * rows :] + moved[rows : 2 * rows]) + moved[:rows]


def group_matrix(tiles, inverse):
    group, bits = 128 // tiles, (tiles - 1).bit_length()
    source = lax.broadcasted_iota(jnp.int32, (256, 256), 0)
    target = lax.broadcasted_iota(jnp.int32, (1, 256), 1)
    if inverse:
        wanted = ((target & 1) << 7) + (((target >> 1) & (tiles - 1)) << (7 - bits)) + (target >> (1 + bits))
    else:
        wanted = ((target & (group - 1)) << (1 + bits)) + (((target & 127) >> (7 - bits)) << 1) + (target >> 7)
    return jnp.where(source == wanted, 1.0, 0.0).astype(BF16)


def exchanged(tiles, slot):
    count = len(tiles)
    if count == 1:
        return tiles
    group = 128 // count
    turned = [pltpu.roll(tile, k * group, 1) if k else tile for k, tile in enumerate(tiles)]
    results = []
    for q in range(count):
        value = turned[(count - q) % count]
        for at in range(1, count):
            value = jnp.where(slot == at, turned[(at - q) % count], value)
        results.append(pltpu.roll(value, (count - q) * group, 1) if q else value)
    return results


def slots(tiles):
    return lax.broadcasted_iota(jnp.int32, (1, 128), 1) >> (7 - (tiles - 1).bit_length())


C_X0, C_X1, C_X2, C_END, C_C1, C_NEW, C_E1, C_D1, C_D2, C_D2_BEFORE = (2 * i for i in range(10))
COARSE_STENCIL = 20
N_LAST, N_K0, N_K1, N_G0, N_RA, N_RB, N_RE, N_F1, N_RF2 = (2 * i for i in range(9))
COARSE_PLAIN = 18


PLANES = {
    "fine": 24,
    "lin": 24,
    "coef": 8,
    "cs": COARSE_STENCIL,
    "cp": COARSE_PLAIN,
    "cc": 2,
    "mom": 8,
    "fresh": 8,
    "rest": 8,
    "tl": 24,
    "ends": 8,
}
HANDED = ("fresh", "rest", "coef", "cs")


def shapes_of(names, rows, lanes):
    return [(PLANES[name], rows, lanes) for name in names]


def natural_shape(rows, lanes):
    return (4, 2 * lanes // 128, 2 * rows, 128)


class Level:
    def __init__(self, refs, rows, lanes, mask, slices=0):
        self.slices = slices if rows <= 32 else 0
        for name, ref in refs.items():
            setattr(self, name, ref)
        self.rows, self.lanes, self.mask = rows, lanes, mask
        self.chunks = rows // 8
        self.recent = {}

    def each(self, body):
        if self.chunks <= 4:
            for i in range(self.chunks):
                body(8 * i)
        else:
            pl.loop(0, self.chunks)(lambda i: body(pl.multiple_of(8 * i, 8)))

    def left(self, value):
        if self.lanes == 128:
            return pltpu.roll(value, 1, 1)
        return jnp.concatenate([pltpu.roll(value[:, -128:], 1, 1), value[:, :-128]], axis=1)

    def right(self, value):
        if self.lanes == 128:
            return pltpu.roll(value, 127, 1)
        return jnp.concatenate([value[:, 128:], pltpu.roll(value[:, :128], 127, 1)], axis=1)

    def scaled(self, value, factor):
        if self.mask is None:
            return factor * value
        return (factor * self.mask) * value

    def known(self, ref, plane, row):
        return self.recent.get((id(ref), plane, row)) if self.slices else None

    def note(self, ref, plane, row, value):
        if self.slices:
            self.recent[id(ref), plane, row] = value

    def at(self, ref, plane, row, shift=0):
        target = row + 8 * shift
        if isinstance(row, int) and 0 <= target < self.rows:
            return self.get(ref, plane, target)
        sublane = lax.broadcasted_iota(jnp.int32, (8, 1), 0)
        if isinstance(row, int):
            value = self.get(ref, plane, target % self.rows)
            return jnp.where(sublane == (0 if shift < 0 else 7), 0.0, pltpu.roll(value, 1 if shift < 0 else 7, 0))
        if shift == 0:
            return ref[plane, pl.ds(row, 8), :]
        inside = (target >= 0) & (target < self.rows)
        value = ref[plane, pl.ds(pl.multiple_of(lax.rem(target + self.rows, self.rows), 8), 8), :]
        wrapped = jnp.where(sublane == (0 if shift < 0 else 7), 0.0, pltpu.roll(value, 1 if shift < 0 else 7, 0))
        return jnp.where(inside, value, wrapped)

    def put(self, ref, plane, row, value, lane=slice(None)):
        ref[plane, pl.ds(row, 8), lane] = value
        if isinstance(row, int) and (lane == slice(None) or self.lanes == 128):
            self.note(ref, plane, row, value)

    def get(self, ref, plane, row):
        value = self.known(ref, plane, row)
        return ref[plane, pl.ds(row, 8), :] if value is None else value

    def set(self, ref, plane, row, value):
        self.put(ref, plane, row, value)

    def fine_rates(self, base, row):
        ref, base = (self.fresh, 0) if base == 3 else (self.fine, base)
        state = [[self.at(ref, base * 8 + s * 4 + p, row) for p in range(4)] for s in range(2)]
        linear, rates = [], []
        for p, (a, b) in enumerate(PHASES):
            laps = []
            for s in range(2):
                across = state[s][2 * a + 1 - b]
                along = state[s][2 * (1 - a) + b]
                moved = self.at(ref, base * 8 + s * 4 + 2 * (1 - a) + b, row, 1 if a else -1)
                side = self.right(across) if b else self.left(across)
                laps.append((((along + moved) + across) - 4.0 * state[s][p]) + side)
            u, v = state[0][p], state[1][p]
            feed = self.get(self.coef, p, row)
            both = self.get(self.coef, 4 + p, row)
            rest_u, rest_v = self.reacted(u, v, feed, 0.0, feed, both)
            scaled_u, scaled_v = self.scaled(laps[0], DIFF_U), self.scaled(laps[1], DIFF_V)
            linear.append((scaled_u + feed, scaled_v))
            rates.append((scaled_u + rest_u, scaled_v + rest_v))
        return state, linear, rates

    def reacted(self, u, v, lin_u, lin_v, feed, both):
        return lin_u - u * (feed + v * v), lin_v + v * (u * v - both)

    def laplacians(self, first, row):
        pair, laps = [], []
        for plane in (first, first + 1):
            value = self.at(self.cs, plane, row)
            rows = self.at(self.cs, plane, row, -1) + self.at(self.cs, plane, row, 1)
            pair.append(value)
            laps.append((rows - 4.0 * value) + (self.left(value) + self.right(value)))
        return pair, laps

    def coarse_rates(self, first, row):
        (u, v), laps = self.laplacians(first, row)
        scaled = [self.scaled(laps[s], 0.25 * (DIFF_U, DIFF_V)[s]) for s in range(2)]
        feed, both = self.get(self.cc, 0, row), self.get(self.cc, 1, row)
        rest_u, rest_v = self.reacted(u, v, feed, 0.0, feed, both)
        return (u, v), scaled, (scaled[0] + rest_u, scaled[1] + rest_v)

    def moved_rates(self, shift, scaled, which, base, row):
        a, b = shift
        m_vv, m_uv, m_u, m_v = (self.get(self.mom, 4 * which + k, row) for k in range(4))
        react = a * (m_vv + b * (2.0 * m_v + b)) + b * (2.0 * m_uv + b * m_u)
        feed, both = self.get(self.cc, 0, row), self.get(self.cc, 1, row)
        rate_u = (self.get(self.cp, base, row) + 2.0 * scaled[0]) - (feed * a + react)
        rate_v = (self.get(self.cp, base + 1, row) + 2.0 * scaled[1]) + (react - both * b)
        return rate_u, rate_v

    def block_mean(self, values):
        return 0.25 * ((values[0] + values[1]) + (values[2] + values[3]))

    def run(self, own, start=True, finish=True):
        lv = self
        cs, cp = self.cs, getattr(self, "cp", None)

        def first_sweep(row):
            for k in range(2):
                lv.set(lv.cc, k, row, lv.block_mean([lv.get(lv.coef, 4 * k + p, row) for p in range(4)]))
            state, linear, rates = lv.fine_rates(0, row)
            for s in range(2):
                for p in range(4):
                    lv.set(lv.lin, s * 4 + p, row, linear[p][s])
                    lv.put(lv.fine, 8 + s * 4 + p, row, state[s][p] + HALF_STEP * rates[p][s])
                mean = lv.block_mean([r[s] for r in rates])
                start = lv.block_mean(state[s])
                lv.set(cp, N_RA + s, row, mean)
                lv.put(cs, C_X0 + s, row, start)
                lv.put(cs, C_X1 + s, row, start + HALF_STEP * mean)
                lv.put(cs, C_END + s, row, start + mean)
                lv.put(cs, C_D1 + s, row, jnp.zeros_like(mean))
                lv.put(cs, C_D2 + s, row, jnp.zeros_like(mean))

        def moments(which, state, row):
            u, v = state
            lv.set(lv.mom, 4 * which, row, lv.block_mean([v[p] * v[p] for p in range(4)]))
            lv.set(lv.mom, 4 * which + 1, row, lv.block_mean([u[p] * v[p] for p in range(4)]))
            lv.set(lv.mom, 4 * which + 2, row, lv.block_mean(u))
            lv.set(lv.mom, 4 * which + 3, row, lv.block_mean(v))

        def second_sweep(row):
            state, linear, rates = lv.fine_rates(1, row)
            _, _, g0 = lv.coarse_rates(C_X0, row)
            first, scaled, g1 = lv.coarse_rates(C_X1, row)
            for s in range(2):
                for p in range(4):
                    lv.set(lv.lin, 8 + s * 4 + p, row, linear[p][s])
                    lv.put(lv.fine, 16 + s * 4 + p, row, state[s][p] + HALF_STEP * rates[p][s])
                mean = lv.block_mean([r[s] for r in rates])
                lv.set(cp, N_F1 + s, row, mean)
                lv.set(cp, N_RB + s, row, mean - 2.0 * scaled[s])
                lv.put(cs, C_X2 + s, row, first[s] + HALF_STEP * mean)
                integral = HALF_STEP * lv.get(cp, N_RA + s, row)
                lv.set(cp, N_K0 + s, row, integral - HALF_STEP * g0[s])
                lv.set(cp, N_K1 + s, row, integral - HALF_STEP * g1[s])
            moments(0, state, row)

        def third_sweep(row):
            state, linear, rates = lv.fine_rates(2, row)
            for s in range(2):
                for p in range(4):
                    lv.set(lv.lin, 16 + s * 4 + p, row, linear[p][s])
            moments(1, state, row)
            second, laps = lv.laplacians(C_X2, row)
            for s in range(2):
                mean = lv.block_mean([r[s] for r in rates])
                lv.set(cp, N_RE + s, row, mean - lv.scaled(laps[s], 0.5 * (DIFF_U, DIFF_V)[s]))
            end, last = slice_end(row)
            for s in range(2):
                j0, j1 = integrals(lv.get(cp, N_RA + s, row), lv.get(cp, N_F1 + s, row), last[s])
                lv.put(cs, C_NEW + s, row, lv.at(cs, C_X0 + s, row) + (j0 + j1))

        def integrals(f0, f1, f2):
            middle = W0[1] * f1
            return middle + (W0[0] * f0 + W0[2] * f2), middle + (W1[0] * f0 + W1[2] * f2)

        def slice_end(row):
            end, scaled, rate = lv.coarse_rates(C_END, row)
            shift = [end[s] - lv.at(cs, C_X2 + s, row) for s in range(2)]
            last = lv.moved_rates(shift, scaled, 1, N_RE, row)
            for s in range(2):
                half = HALF_STEP * rate[s]
                lv.set(cp, N_G0 + s, row, half)
                lv.put(cs, C_C1 + s, row, end[s] + half + lv.get(cp, N_K0 + s, row))
                lv.put(cs, C_D2_BEFORE + s, row, lv.at(cs, C_D2 + s, row))
                lv.put(cs, C_D2 + s, row, shift[s])
                lv.set(cp, N_RF2 + s, row, last[s])
            return end, last

        def middle_nodes(row):
            mid, scaled, rate = lv.coarse_rates(C_C1, row)
            new, _, new_rate = lv.coarse_rates(C_NEW, row)
            shift = [mid[s] - lv.at(cs, C_X1 + s, row) for s in range(2)]
            f1 = lv.moved_rates(shift, scaled, 0, N_RB, row)
            for s in range(2):
                old = lv.at(cs, C_END + s, row)
                lv.set(cp, N_LAST + s, row, old)
                lv.set(cp, N_F1 + s, row, f1[s])
                lv.put(cs, C_D1 + s, row, shift[s])
                lv.put(cs, C_END + s, row, mid[s] + HALF_STEP * rate[s] + lv.get(cp, N_K1 + s, row))
                change = HALF_STEP * new_rate[s] - lv.get(cp, N_G0 + s, row)
                lv.put(cs, C_E1 + s, row, (new[s] - old) + change)

        def end_nodes(row):
            before = [lv.get(cp, N_RF2 + s, row) for s in range(2)]
            _, last = slice_end(row)
            change, laps = lv.laplacians(C_E1, row)
            old, new, j1s = [], [], []
            for s in range(2):
                j0, j1 = integrals(before[s], lv.get(cp, N_F1 + s, row), last[s])
                old.append(lv.get(cp, N_LAST + s, row) + j0)
                new.append(old[s] + change[s])
                j1s.append(j1)
            feed, both = lv.get(lv.cc, 0, row), lv.get(lv.cc, 1, row)
            lin = [lv.scaled(laps[s], 0.25 * (DIFF_U, DIFF_V)[s]) for s in range(2)]
            rate_new = lv.reacted(new[0], new[1], 0.0, 0.0, feed, both)
            rate_old = lv.reacted(old[0], old[1], 0.0, 0.0, feed, both)
            for s in range(2):
                total = new[s] + j1s[s] + HALF_STEP * (rate_new[s] - rate_old[s])
                lv.put(cs, C_NEW + s, row, total + HALF_STEP * lin[s])

        def corrections(starts):
            def body(row):
                for k, first in enumerate(starts):
                    for s in range(2):
                        d = lv.at(cs, first + s, row)
                        ring = [lv.at(cs, first + s, row, -1), lv.at(cs, first + s, row, 1), lv.left(d), lv.right(d)]
                        north, south, west, east = (lv.scaled(x - d, (DIFF_U, DIFF_V)[s]) for x in ring)
                        for p, (a, b) in enumerate(PHASES):
                            lv.set(lv.tl, k * 8 + s * 4 + p, row, (south if a else north) + (east if b else west))

            return body

        def one_slice(n, carry):
            lv.each(middle_nodes)
            lv.each(end_nodes)
            return carry

        origin = jnp.where(own == 0, 0, 2)
        starts = (C_D2_BEFORE, C_D1, C_D2)
        def own_nodes(row):
            for p in range(4):
                for t in range(0, lv.lanes, 128):
                    lane = pl.ds(t, 128)
                    tile = pl.ds(row, 8)
                    if lv.lanes == 128:
                        take = lambda ref, plane: lv.get(ref, plane, row)
                    else:
                        take = lambda ref, plane, lane=lane: ref[plane, tile, lane]
                    feed, both = take(lv.coef, p), take(lv.coef, 4 + p)
                    rates, start = [], None
                    for k, (base, d) in enumerate(zip((origin, 1, 2), starts)):
                        pair = [take(lv.fine, base * 8 + s * 4 + p) + take(cs, d + s) for s in range(2)]
                        lin = [take(lv.lin, base * 8 + s * 4 + p) + take(lv.tl, k * 8 + s * 4 + p) for s in range(2)]
                        rates.append(lv.reacted(pair[0], pair[1], lin[0], lin[1], feed, both))
                        start = pair if k == 0 else start
                    for s in range(2):
                        f0, f1, f2 = (r[s] for r in rates)
                        second = start[s] + (W0[0] * f0 + W0[1] * f1 + W0[2] * f2)
                        lv.put(lv.fresh, s * 4 + p, row, second, lane)
                        lv.put(lv.rest, s * 4 + p, row, second + (W1[0] * f0 + (W1[1] - HALF_STEP) * f1 + W1[2] * f2), lane)

        def last_node(row):
            _, _, rates = lv.fine_rates(3, row)
            for s in range(2):
                ends = [lv.get(lv.rest, s * 4 + p, row) + HALF_STEP * rates[p][s] for p in range(4)]
                fix = lv.at(cs, C_NEW + s, row) - lv.block_mean(ends)
                for p in range(4):
                    lv.set(lv.ends, s * 4 + p, row, ends[p] + fix)

        def sweeps():
            lv.each(first_sweep)
            lv.each(second_sweep)
            lv.each(third_sweep)

        def written_out(count):
            nonlocal origin
            origin = 0 if count == 0 else 2
            self.recent = {}
            sweeps()
            for n in range(1, count + 1):
                one_slice(n, 0)
            lv.each(corrections(starts))
            lv.each(own_nodes)
            if finish:
                lv.each(last_node)

        if start and self.slices:
            for count in range(self.slices):
                pl.when(own == count)(functools.partial(written_out, count))
            return
        if start:
            sweeps()
            lax.fori_loop(1, own + 1, one_slice, 0)
            lv.each(corrections(starts))
            lv.each(own_nodes)
        if finish:
            lv.each(last_node)


def load_planes(level, sources, columns, natural):
    count = level.lanes // 128
    matrix = group_matrix(count, False)
    slot = slots(count)
    for read, first in sources:
        blocks = []
        for k in range(count):
            values = [read(plane, k) for plane in range(4)]
            blocks.append(permuted(jnp.concatenate(values, axis=0), matrix))
        rows = blocks[0].shape[0] // 4
        for b in range(2):
            tiles = exchanged([block[:, 128 * b : 128 * b + 128] for block in blocks], slot)
            for q, tile in enumerate(tiles):
                for plane in range(4):
                    natural[plane, 2 * q + b, pl.ds(first, rows), :] = tile[plane * rows : (plane + 1) * rows]
    chunks = level.chunks
    for q in range(count):
        for p, (a, b) in enumerate(PHASES):
            for t in range(chunks):
                picked = [natural[plane, 2 * q + b, pl.ds(2 * t + a, 8, stride=2 * chunks), :] for plane in range(4)]
                lane, row = pl.ds(128 * q, 128), 8 * t
                for s in range(2):
                    level.fine[s * 4 + p, pl.ds(row, 8), lane] = picked[s]
                level.coef[p, pl.ds(row, 8), lane] = picked[2]
                level.coef[4 + p, pl.ds(row, 8), lane] = picked[2] + picked[3]


def spread(level, natural):
    count, chunks = level.lanes // 128, level.chunks
    for s in range(2):
        for q in range(count):
            for p, (a, b) in enumerate(PHASES):
                for t in range(chunks):
                    value = level.ends[s * 4 + p, pl.ds(8 * t, 8), pl.ds(128 * q, 128)]
                    natural[s, 2 * q + b, pl.ds(2 * t + a, 8, stride=2 * chunks), :] = value


def merged(level, first, rows, natural, matrix):
    count = level.lanes // 128
    slot = slots(count)
    halves = []
    for b in range(2):
        tiles = []
        for q in range(count):
            tiles.append(jnp.concatenate([natural[s, 2 * q + b, pl.ds(first, rows), :] for s in range(2)], axis=0))
        halves.append(exchanged(tiles, slot))
    blocks = [permuted(jnp.concatenate([halves[0][k], halves[1][k]], axis=1), matrix) for k in range(count)]
    return [[block[s * rows : (s + 1) * rows] for block in blocks] for s in range(2)]


def own_first(rows):
    return pl.multiple_of(lax.axis_index("gx") * rows, rows)


def source_list(refs, rows, parts):
    if parts == 2:
        mine = own_first(rows)
        state, feed, kill = refs[4:]
        other = [state.at[0], state.at[1], feed, kill]
        return [(refs[:4], mine), (other, pl.multiple_of(rows - mine, rows))]
    state, feed, kill = refs
    return [([state.at[g, 0], state.at[g, 1], feed.at[g], kill.at[g]], g * rows) for g in range(parts)]


def interior_kernel(parts, rows, columns, halo, depth, width, start, finish, *refs):
    refs = list(refs)
    take = lambda count: [refs.pop(0) for _ in range(count)]
    here = columns // 2 if parts == 2 else columns
    origin = pl.multiple_of(lax.axis_index("gx") * here, here) if parts == 2 else 0
    seam = 4 * depth if parts == 2 else 0
    side = (width - seam) // 2 - halo
    ins = take(7 if parts == 2 else 3) if start else []
    names = [] if finish and start else list(HANDED)
    handed = take(len(names)) if not start else []
    window = take(1)[0] if start else None
    outs = take(2 if parts == 2 else 1) if finish else []
    handed = handed or take(len(names))
    names += [name for name in PLANES if name not in names] if start else ["ends"]
    handed += take(len(names) - len(handed))
    (natural,) = take(1)
    level = Level(dict(zip(names, handed)), parts * rows // 2, here // 2, None)

    def reader(planes):
        return lambda plane, block: planes[plane][:, pl.ds(origin + 256 * block, 256)]

    if start:
        sources = []
        for planes, first in source_list(ins, rows, parts):
            sources.append((reader(planes), first))
            for plane in range(4):
                value = planes[plane][...]
                blank = jnp.zeros((rows, halo), F32)
                cuts = [blank, value[:, :side], value[:, (columns - seam) // 2 : (columns + seam) // 2]]
                cuts += [value[:, columns - side :], blank]
                window[plane, pl.ds(first, rows), :] = jnp.concatenate([cut for cut in cuts if cut.shape[1]], axis=1)
        load_planes(level, sources, here, natural)
    level.run(lax.axis_index("ta"), start, finish)
    if finish:
        spread(level, natural)
        matrix = group_matrix(level.lanes // 128, True)
        mine = own_first(rows)
        firsts = [mine, pl.multiple_of(rows - mine, rows)] if parts == 2 else [mine]
        for target, first in zip(outs, firsts):
            blocks = merged(level, first, rows, natural, matrix)
            for s in range(2):
                for k, block in enumerate(blocks[s]):
                    target[s, :, pl.ds(256 * k, 256)] = block


def few(count):
    return count if count <= 4 else 0


def places(halo, depth, width):
    last = -depth % 128
    return (halo, 0), (width // 2 - depth, last), (width // 2, 0), (width - halo - depth, last)


def border_kernel(parts, rows, halo, depth, width, window, near, far, out, *work):
    lanes = width // 2
    index, size = lax.axis_index("gy"), lax.axis_size("gy")
    swap = lax.rem(index, 2) == 0
    if parts == 2:
        swap = swap == (lax.axis_index("gx") == 0)
    tiles = lanes // 128
    at = lax.broadcasted_iota(jnp.int32, (1, lanes), 1)
    at = tiles * (at % 128) + at // 128
    outside = ((at < halo // 2) & (index == 0)) | ((at >= lanes - halo // 2) & (index == size - 1))
    level = Level(dict(zip(PLANES, work)), parts * rows // 2, lanes, jnp.where(outside, 0.0, 1.0), few(lax.axis_size("ta")))

    strips = []
    for edge, (a, b) in ((0, (far, near)), (size - 1, (near, far))):
        strip = jnp.where(index == edge, 0.0, jnp.where(swap, a[...], b[...]))
        strips.append(strip)

    def reader(first):
        def read(plane, block):
            low, high = (unfolded(strip, first, rows, plane, depth, parts * rows) for strip in strips)
            own = window[plane, pl.ds(first, rows), :]
            cuts = [own[:, : halo - depth], low, own[:, halo : width - halo], high, own[:, width - halo + depth :]]
            whole = jnp.concatenate([cut for cut in cuts if cut.shape[1]], axis=1)
            return whole[:, 256 * block : 256 * block + 256]

        return read

    load_planes(level, [(reader(g * rows), g * rows) for g in range(parts)], width, work[-1])
    level.run(lax.axis_index("ta"))
    spread(level, work[-1])
    if parts == 2 and tiles == 1:
        mine = own_first(rows)
        for k, (start, at) in enumerate(places(halo, depth, width)):
            source = lax.broadcasted_iota(jnp.int32, (8, 128), 1) + (start - at)
            for s in range(2):
                for row in range(0, rows, 8):
                    pair = [work[-1][s, b, pl.ds(pl.multiple_of(mine + row, 8), 8), :] for b in range(2)]
                    even, odd = (jnp.take_along_axis(x, (source >> 1) & 127, axis=1) for x in pair)
                    out[k, s, pl.ds(row, 8), :] = jnp.where((source & 1) == 0, even, odd)
        return
    natural = merged(level, own_first(rows), rows, work[-1], group_matrix(tiles, True))
    for s in range(2):
        for k, block in enumerate(natural[s]):
            out[s, :, pl.ds(256 * k, 256)] = block


def final_kernel(halo, depth, width, inner, border, out):
    total = out.shape[-1]
    out[0] = inner[...]
    for s in range(2):
        for column, source in ((0, halo), (total - depth, width - halo - depth)):
            low = column // 128 * 128
            high = round_up(column + depth, 128)
            old, new = out[0, s, :, pl.ds(low, high - low)], border[s][:, source : source + depth]
            parts_of = [old[:, : column - low], new, old[:, column + depth - low :]]
            out[0, s, :, pl.ds(low, high - low)] = jnp.concatenate([x for x in parts_of if x.shape[1]], axis=1)


def joined_kernel(halo, depth, width, keep, got, border, out, ends, middle, sems):
    total = out.shape[-1]
    half = total // 2
    tile = round_up(depth, 128)
    core = lax.axis_index("gx")
    copies = []
    for k, value in enumerate((keep, got)):
        origin = pl.multiple_of((core if k == 0 else 1 - core) * half + tile, 128)
        inside = pl.ds(tile, half - 2 * tile)
        target = out.at[0, :, :, pl.ds(origin, half - 2 * tile)]
        copies.append(pltpu.make_async_copy(value.at[:, :, inside], target, sems.at[k]))
        copies[-1].start()
    first = core == 0
    low, high = pl.ds(0, tile), pl.ds(half - tile, tile)
    starts = [start for start, _ in places(halo, depth, width)]
    lane = lax.broadcasted_iota(jnp.int32, (1, tile), 1)
    for s in range(2):
        old = [jnp.where(first, a[s, :, at], b[s, :, at]) for a, b in ((keep, got), (got, keep)) for at in (low, high)]
        if border.ndim == 4:
            targets = (ends.at[0, s], middle.at[s, :, pl.ds(0, tile)], middle.at[s, :, pl.ds(tile, tile)], ends.at[1, s])
            for k, (target, (_, at)) in enumerate(zip(targets, places(halo, depth, width))):
                target[...] = jnp.where((lane >= at) & (lane < at + depth), border[k, s], old[k])
            continue
        new = [border[s][:, at : at + depth] for at in starts]
        ends[0, s] = jnp.concatenate([new[0], old[0][:, depth:]], axis=1)
        ends[1, s] = jnp.concatenate([old[3][:, : tile - depth], new[3]], axis=1)
        middle[s] = jnp.concatenate([old[1][:, : tile - depth], new[1], new[2], old[2][:, depth:]], axis=1)
    copies.append(pltpu.make_async_copy(ends.at[0], out.at[0, :, :, pl.ds(0, tile)], sems.at[2]))
    copies.append(pltpu.make_async_copy(ends.at[1], out.at[0, :, :, pl.ds(total - tile, tile)], sems.at[3]))
    copies.append(pltpu.make_async_copy(middle, out.at[0, :, :, pl.ds(half - tile, 2 * tile)], sems.at[4]))
    for copy in copies[2:]:
        copy.start()
    for copy in copies:
        copy.wait()


def folds(rows, columns):
    tiles, spare = rows // 8, max(128 // columns - 4, 0)
    return (-(-4 * tiles // (spare + 4)), spare) if spare else (tiles, 0)


def folded(strip, columns):
    rows = strip.shape[0]
    kept, spare = folds(rows, columns)
    if not spare:
        return strip
    tail = [(row, plane) for row in range(8 * kept, rows, 8) for plane in range(4)]
    tiles = []
    for k in range(kept):
        beside = [strip[row : row + 8, p * columns : (p + 1) * columns] for row, p in tail[k * spare : (k + 1) * spare]]
        blank = jnp.zeros((8, 128 - (4 + len(beside)) * columns), F32)
        cuts = [strip[8 * k : 8 * k + 8], *beside, blank]
        tiles.append(jnp.concatenate([cut for cut in cuts if cut.shape[1]], axis=1))
    return jnp.concatenate(tiles, axis=0)


def unfolded(value, first, rows, plane, columns, total):
    kept, spare = folds(total, columns)
    tiles = []
    for row in range(first, first + rows, 8):
        at, lane = row, plane * columns
        if spare and row >= 8 * kept:
            index = (row // 8 - kept) * 4 + plane
            at, lane = index // spare * 8, (4 + index % spare) * columns
        tiles.append(value[at : at + 8, lane : lane + columns])
    return jnp.concatenate(tiles, axis=0)


def pack_kernel(parts, rows, depth, *refs):
    count = 7 if parts == 2 else 3
    ins, outs = refs[:count], refs[count:]
    even = lax.rem(lax.axis_index("gy"), 2) == 0
    sources = source_list(ins, rows, parts)
    total, tile = ins[-1].shape[-1], round_up(depth, 128)
    if parts == 2 and depth <= 32:
        first = lax.axis_index("gx") == 0
        upper = even == first
        column = pl.multiple_of(jnp.where(upper, total - tile, 0), 128)
        offset = jnp.where(upper, tile - depth, 0)
        lane = lax.broadcasted_iota(jnp.int32, (1, 128), 1)
        strip = jnp.zeros((2 * rows, 128), F32)
        for plane in range(4):
            own, other = (planes[plane][:, pl.ds(column, tile)] for planes, _ in sources)
            value = jnp.concatenate([jnp.where(first, own, other), jnp.where(first, other, own)], axis=0)
            value = pltpu.roll(value, lax.rem(plane * depth + 128 - offset, 128), 1)
            strip = jnp.where((lane >= plane * depth) & (lane < (plane + 1) * depth), value, strip)
        outs[0][...] = folded(strip[:, : 4 * depth], depth)
        return
    strips = []
    for planes, _ in sources:
        low = jnp.concatenate([ref[:, pl.ds(0, tile)][:, :depth] for ref in planes], axis=1)
        high = jnp.concatenate([ref[:, pl.ds(total - tile, tile)][:, tile - depth :] for ref in planes], axis=1)
        strips.append((jnp.where(even, high, low), jnp.where(even, low, high)))
    if parts == 2:
        first = lax.axis_index("gx") == 0
        (own_a, own_b), (other_a, other_b) = strips
        own, other = jnp.where(first, own_a, own_b), jnp.where(first, other_a, other_b)
        whole = [jnp.concatenate([jnp.where(first, own, other), jnp.where(first, other, own)], axis=0)]
    else:
        whole = [jnp.concatenate(each, axis=0) for each in zip(*strips)]
    for out, strip in zip(outs, whole):
        out[...] = folded(strip, depth)


def fetch_kernel(state, feed, kill, *refs):
    planes, sems = refs[:4], refs[4]
    sources = (state.at[0], state.at[1], feed, kill)
    copies = [pltpu.make_async_copy(sources[i], planes[i], sems.at[i]) for i in range(4)]
    for copy in copies:
        copy.start()
    for copy in copies:
        copy.wait()


def both_ways(pairs):
    return [pair for low, high in pairs for pair in ((low, high), (high, low))]


VMEM = pl.BlockSpec(memory_space=pltpu.VMEM)
ANY = pl.BlockSpec(memory_space=pl.ANY)


def arrays(shapes):
    return [jax.ShapeDtypeStruct(shape, F32) for shape in shapes]


def buffers(shapes):
    return [pltpu.VMEM(shape, F32) for shape in shapes]


def size_of(shapes):
    return sum(4 * math.prod(shape) for shape in shapes)


def called(name, kernel, outs, scratch, limit, inputs, specs=VMEM, out_specs=VMEM, flops=0):
    return pl.pallas_call(
        kernel,
        out_shape=outs,
        in_specs=[specs] * len(inputs),
        out_specs=[out_specs] * len(outs),
        scratch_shapes=scratch,
        compiler_params=pltpu.CompilerParams(vmem_limit_bytes=limit),
        cost_estimate=pl.CostEstimate(flops=flops, bytes_accessed=flops // 2, transcendentals=0),
        name=name,
    )(*inputs)


def per_device(initial_state, feed_rate, kill_rate):
    slices, parts, blocks = (lax.axis_size(axis) for axis in ("ta", "gx", "gy"))
    _, rows, columns = initial_state.shape
    depth = 2 * (2 * slices + 2)
    halo = round_up(depth, 32)
    seam = 4 * depth if parts == 2 else 0
    width = round_up(2 * halo + 4 * depth + seam, 256)
    every = parts * rows
    here = columns // 2 if parts == 2 else columns
    given = (initial_state, feed_rate, kill_rate)
    plane_bytes = 4 * every * columns

    low_pairs = both_ways([(i, i + 1) for i in range(0, blocks - 1, 2)])
    high_pairs = both_ways([(i, (i + 1) % blocks) for i in range(1, blocks - blocks % 2, 2)])

    def crossed(value):
        return lax.ppermute(value, "gx", [(0, 1), (1, 0)])

    if parts == 2:
        others = [crossed(value) for value in given]
        limit = 1709 * 2**15
        own = called("fetch", fetch_kernel, arrays([(rows, columns)] * 4), [pltpu.SemaphoreType.DMA((4,))], limit, given, ANY)
        fields = [*own, *others]
    else:
        fields = [lax.all_gather(value, "gx") for value in given]
    pack = functools.partial(pack_kernel, parts, rows, depth)
    kept, spare = folds(every, depth)
    strips = arrays([(8 * kept, 128 if spare else 4 * depth)] * (1 if parts == 2 else 2))
    sent = called("pack", pack, strips, [], 8 * plane_bytes + 2**22, fields)
    if parts == 2:
        pairs = []
        for n in range(slices):
            base = n * 2 * blocks
            inner_pairs = both_ways([(i, i + 1) for i in range(1, blocks - 1, 2)])
            pairs += [(base + source, base + target) for source, target in low_pairs]
            pairs += [(base + blocks + source, base + blocks + target) for source, target in inner_pairs]
            if n ^ 1 < slices:
                met = {0, blocks - 1} - {source for source, _ in inner_pairs}
                pairs += [(base + blocks + i, (n ^ 1) * 2 * blocks + blocks + i) for i in sorted(met)]
        near = lax.ppermute(sent[0], ("ta", "gx", "gy"), pairs)
    else:
        near = lax.ppermute(sent[0], "gy", low_pairs)
        far = lax.ppermute(sent[1], "gy", high_pairs)

    natural = natural_shape(every // 2, here // 2)
    everything = shapes_of(PLANES, every // 2, here // 2) + [natural]
    limit = size_of(everything) + 32 * every * (columns + width) + 2**22
    interior = functools.partial(interior_kernel, parts, rows, columns, halo, depth, width)
    window_shape = (4, every, width)
    result_shape = (2, rows, here)
    if parts == 2:
        first = functools.partial(interior, True, False)
        handed = shapes_of(HANDED, every // 2, here // 2)
        scratch = buffers(shapes_of([name for name in PLANES if name not in HANDED], every // 2, here // 2) + [natural])
        made = called("interior", first, arrays([window_shape] + handed), scratch, limit, fields, flops=2**24)
        near, window, *made = lax.optimization_barrier((near, *made))
        far = crossed(near)
        last = functools.partial(interior, False, True)
        scratch = buffers(shapes_of(["ends"], every // 2, here // 2) + [natural])
        keep, give = called("own", last, arrays([result_shape] * 2), scratch, limit, made, flops=2**34)
        inner = [keep, crossed(give)]
    else:
        whole = functools.partial(interior, True, True)
        shapes = [window_shape, result_shape]
        window, *inner = called("interior", whole, arrays(shapes), buffers(everything), limit, fields, flops=2**24)
    work = shapes_of(PLANES, every // 2, width // 2) + [natural_shape(every // 2, width // 2)]
    limit = size_of(work) + 32 * every * width + 2**23
    shape = (4, 2, rows, 128) if parts == 2 and width == 256 else (2, rows, width)
    border = functools.partial(border_kernel, parts, rows, halo, depth, width)
    (edges,) = called("border", border, arrays([shape]), buffers(work), limit, (window, near, far), flops=2**34)
    result = arrays([(1, 2, rows, columns)])
    if parts == 2:
        tile = round_up(depth, 128)
        scratch = buffers([(2, 2, rows, tile), (2, rows, 2 * tile)]) + [pltpu.SemaphoreType.DMA((5,))]
        final = functools.partial(joined_kernel, halo, depth, width)
        (out,) = called("final", final, result, scratch, 2**23, (*inner, edges), out_specs=ANY)
    else:
        final = functools.partial(final_kernel, halo, depth, width)
        (out,) = called("final", final, result, [], 16 * plane_bytes + 2**22, (*inner, edges))
    return out


def solution(mesh):
    placed = (P(None, "gx", "gy"), P("gx", "gy"), P("gx", "gy"))
    return jax.shard_map(
        per_device, mesh=mesh, in_specs=placed, out_specs=P("ta", None, "gx", "gy"), check_vma=False
    )
```

```python
import functools
import math

import jax
import jax.numpy as jnp
from jax import lax
from jax.experimental import pallas as pl
from jax.experimental.pallas import tpu as pltpu
from jax.sharding import PartitionSpec as P

TURNS = 2

DIFF_U = 0.2
DIFF_V = 0.1
HALF_STEP = 0.5
W0 = (5.0 / 24.0, 1.0 / 3.0, -1.0 / 24.0)
W1 = (-1.0 / 24.0, 1.0 / 3.0, 5.0 / 24.0)
F32 = jnp.float32
BF16 = jnp.bfloat16
PHASES = ((0, 0), (0, 1), (1, 0), (1, 1))


def round_up(value, step):
    return -(-value // step) * step


def thirds(value):
    high = value.astype(BF16)
    rest = value - high.astype(F32)
    middle = rest.astype(BF16)
    low = (rest - middle.astype(F32)).astype(BF16)
    return high, middle, low


def permuted(value, matrix):
    rows = value.shape[0]
    parts = jnp.concatenate(thirds(value), axis=0)
    moved = jnp.dot(parts, matrix, preferred_element_type=F32)
    return (moved[2 * rows :] + moved[rows : 2 * rows]) + moved[:rows]


def group_matrix(tiles, inverse):
    group, bits = 128 // tiles, (tiles - 1).bit_length()
    source = lax.broadcasted_iota(jnp.int32, (256, 256), 0)
    target = lax.broadcasted_iota(jnp.int32, (1, 256), 1)
    if inverse:
        wanted = ((target & 1) << 7) + (((target >> 1) & (tiles - 1)) << (7 - bits)) + (target >> (1 + bits))
    else:
        wanted = ((target & (group - 1)) << (1 + bits)) + (((target & 127) >> (7 - bits)) << 1) + (target >> 7)
    return jnp.where(source == wanted, 1.0, 0.0).astype(BF16)


def exchanged(tiles, slot):
    count = len(tiles)
    if count == 1:
        return tiles
    group = 128 // count
    turned = [pltpu.roll(tile, k * group, 1) if k else tile for k, tile in enumerate(tiles)]
    results = []
    for q in range(count):
        value = turned[(count - q) % count]
        for at in range(1, count):
            value = jnp.where(slot == at, turned[(at - q) % count], value)
        results.append(pltpu.roll(value, (count - q) * group, 1) if q else value)
    return results


def slots(tiles):
    return lax.broadcasted_iota(jnp.int32, (1, 128), 1) >> (7 - (tiles - 1).bit_length())


C_X0, C_X1, C_X2, C_END, C_C1, C_NEW, C_E1, C_D1, C_D2, C_D2_BEFORE = (2 * i for i in range(10))
COARSE_STENCIL = 20
N_LAST, N_K0, N_K1, N_G0, N_RA, N_RB, N_RE, N_F1, N_RF2 = (2 * i for i in range(9))
COARSE_PLAIN = 18


PLANES = {
    "fine": 24,
    "lin": 24,
    "coef": 8,
    "cs": COARSE_STENCIL,
    "cp": COARSE_PLAIN,
    "cc": 2,
    "mom": 8,
    "fresh": 8,
    "rest": 8,
    "tl": 24,
    "ends": 8,
}
HANDED = ("fresh", "rest", "coef", "cs")


def shapes_of(names, rows, lanes):
    return [(PLANES[name], rows, lanes) for name in names]


def natural_shape(rows, lanes):
    return (4, 2 * lanes // 128, 2 * rows, 128)


class Level:
    def __init__(self, refs, rows, lanes, mask, slices=0):
        self.slices = slices if rows <= 32 else 0
        for name, ref in refs.items():
            setattr(self, name, ref)
        self.rows, self.lanes, self.mask = rows, lanes, mask
        self.chunks = rows // 8
        self.recent = {}

    def each(self, body):
        if self.chunks <= 4:
            for i in range(self.chunks):
                body(8 * i)
        else:
            pl.loop(0, self.chunks)(lambda i: body(pl.multiple_of(8 * i, 8)))

    def left(self, value):
        if self.lanes == 128:
            return pltpu.roll(value, 1, 1)
        return jnp.concatenate([pltpu.roll(value[:, -128:], 1, 1), value[:, :-128]], axis=1)

    def right(self, value):
        if self.lanes == 128:
            return pltpu.roll(value, 127, 1)
        return jnp.concatenate([value[:, 128:], pltpu.roll(value[:, :128], 127, 1)], axis=1)

    def scaled(self, value, factor):
        if self.mask is None:
            return factor * value
        return (factor * self.mask) * value

    def known(self, ref, plane, row):
        return self.recent.get((id(ref), plane, row)) if self.slices else None

    def note(self, ref, plane, row, value):
        if self.slices:
            self.recent[id(ref), plane, row] = value

    def at(self, ref, plane, row, shift=0):
        target = row + 8 * shift
        if isinstance(row, int) and 0 <= target < self.rows:
            return self.get(ref, plane, target)
        sublane = lax.broadcasted_iota(jnp.int32, (8, 1), 0)
        if isinstance(row, int):
            value = self.get(ref, plane, target % self.rows)
            return jnp.where(sublane == (0 if shift < 0 else 7), 0.0, pltpu.roll(value, 1 if shift < 0 else 7, 0))
        if shift == 0:
            return ref[plane, pl.ds(row, 8), :]
        inside = (target >= 0) & (target < self.rows)
        value = ref[plane, pl.ds(pl.multiple_of(lax.rem(target + self.rows, self.rows), 8), 8), :]
        wrapped = jnp.where(sublane == (0 if shift < 0 else 7), 0.0, pltpu.roll(value, 1 if shift < 0 else 7, 0))
        return jnp.where(inside, value, wrapped)

    def put(self, ref, plane, row, value, lane=slice(None)):
        ref[plane, pl.ds(row, 8), lane] = value
        if isinstance(row, int) and (lane == slice(None) or self.lanes == 128):
            self.note(ref, plane, row, value)

    def get(self, ref, plane, row):
        value = self.known(ref, plane, row)
        return ref[plane, pl.ds(row, 8), :] if value is None else value

    def set(self, ref, plane, row, value):
        self.put(ref, plane, row, value)

    def fine_rates(self, base, row):
        ref, base = (self.fresh, 0) if base == 3 else (self.fine, base)
        state = [[self.at(ref, base * 8 + s * 4 + p, row) for p in range(4)] for s in range(2)]
        linear, rates = [], []
        for p, (a, b) in enumerate(PHASES):
            laps = []
            for s in range(2):
                across = state[s][2 * a + 1 - b]
                along = state[s][2 * (1 - a) + b]
                moved = self.at(ref, base * 8 + s * 4 + 2 * (1 - a) + b, row, 1 if a else -1)
                side = self.right(across) if b else self.left(across)
                laps.append((((along + moved) + across) - 4.0 * state[s][p]) + side)
            u, v = state[0][p], state[1][p]
            feed = self.get(self.coef, p, row)
            both = self.get(self.coef, 4 + p, row)
            rest_u, rest_v = self.reacted(u, v, feed, 0.0, feed, both)
            scaled_u, scaled_v = self.scaled(laps[0], DIFF_U), self.scaled(laps[1], DIFF_V)
            linear.append((scaled_u + feed, scaled_v))
            rates.append((scaled_u + rest_u, scaled_v + rest_v))
        return state, linear, rates

    def reacted(self, u, v, lin_u, lin_v, feed, both):
        return lin_u - u * (feed + v * v), lin_v + v * (u * v - both)

    def laplacians(self, first, row):
        pair, laps = [], []
        for plane in (first, first + 1):
            value = self.at(self.cs, plane, row)
            rows = self.at(self.cs, plane, row, -1) + self.at(self.cs, plane, row, 1)
            pair.append(value)
            laps.append((rows - 4.0 * value) + (self.left(value) + self.right(value)))
        return pair, laps

    def coarse_rates(self, first, row):
        (u, v), laps = self.laplacians(first, row)
        scaled = [self.scaled(laps[s], 0.25 * (DIFF_U, DIFF_V)[s]) for s in range(2)]
        feed, both = self.get(self.cc, 0, row), self.get(self.cc, 1, row)
        rest_u, rest_v = self.reacted(u, v, feed, 0.0, feed, both)
        return (u, v), scaled, (scaled[0] + rest_u, scaled[1] + rest_v)

    def moved_rates(self, shift, scaled, which, base, row):
        a, b = shift
        m_vv, m_uv, m_u, m_v = (self.get(self.mom, 4 * which + k, row) for k in range(4))
        react = a * (m_vv + b * (2.0 * m_v + b)) + b * (2.0 * m_uv + b * m_u)
        feed, both = self.get(self.cc, 0, row), self.get(self.cc, 1, row)
        rate_u = (self.get(self.cp, base, row) + 2.0 * scaled[0]) - (feed * a + react)
        rate_v = (self.get(self.cp, base + 1, row) + 2.0 * scaled[1]) + (react - both * b)
        return rate_u, rate_v

    def block_mean(self, values):
        return 0.25 * ((values[0] + values[1]) + (values[2] + values[3]))

    def run(self, own, start=True, finish=True):
        lv = self
        cs, cp = self.cs, getattr(self, "cp", None)

        made = {}

        def first_sweep(row):
            for k in range(2):
                lv.set(lv.cc, k, row, lv.block_mean([lv.get(lv.coef, 4 * k + p, row) for p in range(4)]))
            state, linear, rates = lv.fine_rates(0, row)
            if isinstance(row, int):
                made[0, row] = state, rates
            for s in range(2):
                for p in range(4):
                    lv.set(lv.lin, s * 4 + p, row, linear[p][s])
                    lv.put(lv.fine, 8 + s * 4 + p, row, state[s][p] + HALF_STEP * rates[p][s])
                mean = lv.block_mean([r[s] for r in rates])
                start = lv.block_mean(state[s])
                lv.set(cp, N_RA + s, row, mean)
                lv.put(cs, C_X0 + s, row, start)
                lv.put(cs, C_X1 + s, row, start + HALF_STEP * mean)
                lv.put(cs, C_END + s, row, start + mean)
                lv.put(cs, C_D1 + s, row, jnp.zeros_like(mean))
                lv.put(cs, C_D2 + s, row, jnp.zeros_like(mean))

        def moments(which, state, row):
            u, v = state
            lv.set(lv.mom, 4 * which, row, lv.block_mean([v[p] * v[p] for p in range(4)]))
            lv.set(lv.mom, 4 * which + 1, row, lv.block_mean([u[p] * v[p] for p in range(4)]))
            lv.set(lv.mom, 4 * which + 2, row, lv.block_mean(u))
            lv.set(lv.mom, 4 * which + 3, row, lv.block_mean(v))

        def second_sweep(row):
            state, linear, rates = lv.fine_rates(1, row)
            if isinstance(row, int):
                made[1, row] = state, rates
            _, _, g0 = lv.coarse_rates(C_X0, row)
            first, scaled, g1 = lv.coarse_rates(C_X1, row)
            for s in range(2):
                for p in range(4):
                    lv.set(lv.lin, 8 + s * 4 + p, row, linear[p][s])
                    lv.put(lv.fine, 16 + s * 4 + p, row, state[s][p] + HALF_STEP * rates[p][s])
                mean = lv.block_mean([r[s] for r in rates])
                lv.set(cp, N_F1 + s, row, mean)
                lv.set(cp, N_RB + s, row, mean - 2.0 * scaled[s])
                lv.put(cs, C_X2 + s, row, first[s] + HALF_STEP * mean)
                integral = HALF_STEP * lv.get(cp, N_RA + s, row)
                lv.set(cp, N_K0 + s, row, integral - HALF_STEP * g0[s])
                lv.set(cp, N_K1 + s, row, integral - HALF_STEP * g1[s])
            moments(0, state, row)

        def third_sweep(row):
            state, linear, rates = lv.fine_rates(2, row)
            for s in range(2):
                for p in range(4):
                    lv.set(lv.lin, 16 + s * 4 + p, row, linear[p][s])
            moments(1, state, row)
            second, laps = lv.laplacians(C_X2, row)
            for s in range(2):
                mean = lv.block_mean([r[s] for r in rates])
                lv.set(cp, N_RE + s, row, mean - lv.scaled(laps[s], 0.5 * (DIFF_U, DIFF_V)[s]))
            end, last = slice_end(row)
            for s in range(2):
                j0, j1 = integrals(lv.get(cp, N_RA + s, row), lv.get(cp, N_F1 + s, row), last[s])
                lv.put(cs, C_NEW + s, row, lv.at(cs, C_X0 + s, row) + (j0 + j1))

        def integrals(f0, f1, f2):
            middle = W0[1] * f1
            return middle + (W0[0] * f0 + W0[2] * f2), middle + (W1[0] * f0 + W1[2] * f2)

        def slice_end(row):
            end, scaled, rate = lv.coarse_rates(C_END, row)
            shift = [end[s] - lv.at(cs, C_X2 + s, row) for s in range(2)]
            last = lv.moved_rates(shift, scaled, 1, N_RE, row)
            for s in range(2):
                half = HALF_STEP * rate[s]
                lv.set(cp, N_G0 + s, row, half)
                lv.put(cs, C_C1 + s, row, end[s] + half + lv.get(cp, N_K0 + s, row))
                lv.put(cs, C_D2_BEFORE + s, row, lv.at(cs, C_D2 + s, row))
                lv.put(cs, C_D2 + s, row, shift[s])
                lv.set(cp, N_RF2 + s, row, last[s])
            return end, last

        def middle_nodes(row):
            mid, scaled, rate = lv.coarse_rates(C_C1, row)
            new, _, new_rate = lv.coarse_rates(C_NEW, row)
            shift = [mid[s] - lv.at(cs, C_X1 + s, row) for s in range(2)]
            f1 = lv.moved_rates(shift, scaled, 0, N_RB, row)
            for s in range(2):
                old = lv.at(cs, C_END + s, row)
                lv.set(cp, N_LAST + s, row, old)
                lv.set(cp, N_F1 + s, row, f1[s])
                lv.put(cs, C_D1 + s, row, shift[s])
                lv.put(cs, C_END + s, row, mid[s] + HALF_STEP * rate[s] + lv.get(cp, N_K1 + s, row))
                change = HALF_STEP * new_rate[s] - lv.get(cp, N_G0 + s, row)
                lv.put(cs, C_E1 + s, row, (new[s] - old) + change)

        def end_nodes(row):
            before = [lv.get(cp, N_RF2 + s, row) for s in range(2)]
            _, last = slice_end(row)
            change, laps = lv.laplacians(C_E1, row)
            old, new, j1s = [], [], []
            for s in range(2):
                j0, j1 = integrals(before[s], lv.get(cp, N_F1 + s, row), last[s])
                old.append(lv.get(cp, N_LAST + s, row) + j0)
                new.append(old[s] + change[s])
                j1s.append(j1)
            feed, both = lv.get(lv.cc, 0, row), lv.get(lv.cc, 1, row)
            lin = [lv.scaled(laps[s], 0.25 * (DIFF_U, DIFF_V)[s]) for s in range(2)]
            rate_new = lv.reacted(new[0], new[1], 0.0, 0.0, feed, both)
            rate_old = lv.reacted(old[0], old[1], 0.0, 0.0, feed, both)
            for s in range(2):
                total = new[s] + j1s[s] + HALF_STEP * (rate_new[s] - rate_old[s])
                lv.put(cs, C_NEW + s, row, total + HALF_STEP * lin[s])

        def corrections(starts):
            def body(row):
                for k, first in enumerate(starts):
                    if taken and k < 2:
                        continue
                    for s in range(2):
                        d = lv.at(cs, first + s, row)
                        ring = [lv.at(cs, first + s, row, -1), lv.at(cs, first + s, row, 1), lv.left(d), lv.right(d)]
                        north, south, west, east = (lv.scaled(x - d, (DIFF_U, DIFF_V)[s]) for x in ring)
                        for p, (a, b) in enumerate(PHASES):
                            lv.set(lv.tl, k * 8 + s * 4 + p, row, (south if a else north) + (east if b else west))

            return body

        def one_slice(n, carry):
            lv.each(middle_nodes)
            lv.each(end_nodes)
            return carry

        origin = jnp.where(own == 0, 0, 2)
        starts = (C_D2_BEFORE, C_D1, C_D2)
        taken = False
        def own_nodes(row):
            for p in range(4):
                for t in range(0, lv.lanes, 128):
                    lane = pl.ds(t, 128)
                    tile = pl.ds(row, 8)
                    if lv.lanes == 128:
                        take = lambda ref, plane: lv.get(ref, plane, row)
                    else:
                        take = lambda ref, plane, lane=lane: ref[plane, tile, lane]
                    feed, both = take(lv.coef, p), take(lv.coef, 4 + p)
                    rates, start = [], None
                    cases = list(enumerate(zip((origin, 1, 2), starts)))
                    if taken:
                        rates = [made[k, row][1][p] for k in range(2)]
                        start = [made[0, row][0][s][p] for s in range(2)]
                        cases = cases[2:]
                    for k, (base, d) in cases:
                        pair = [take(lv.fine, base * 8 + s * 4 + p) + take(cs, d + s) for s in range(2)]
                        lin = [take(lv.lin, base * 8 + s * 4 + p) + take(lv.tl, k * 8 + s * 4 + p) for s in range(2)]
                        rates.append(lv.reacted(pair[0], pair[1], lin[0], lin[1], feed, both))
                        start = pair if k == 0 else start
                    for s in range(2):
                        f0, f1, f2 = (r[s] for r in rates)
                        second = start[s] + (W0[0] * f0 + W0[1] * f1 + W0[2] * f2)
                        lv.put(lv.fresh, s * 4 + p, row, second, lane)
                        lv.put(lv.rest, s * 4 + p, row, second + (W1[0] * f0 + (W1[1] - HALF_STEP) * f1 + W1[2] * f2), lane)

        def last_node(row):
            _, _, rates = lv.fine_rates(3, row)
            for s in range(2):
                ends = [lv.get(lv.rest, s * 4 + p, row) + HALF_STEP * rates[p][s] for p in range(4)]
                fix = lv.at(cs, C_NEW + s, row) - lv.block_mean(ends)
                for p in range(4):
                    lv.set(lv.ends, s * 4 + p, row, ends[p] + fix)

        def sweeps():
            lv.each(first_sweep)
            lv.each(second_sweep)
            lv.each(third_sweep)

        def written_out(count):
            nonlocal origin, taken
            origin, taken = 0 if count == 0 else 2, count == 0 and lv.lanes == 128
            made.clear()
            self.recent = {}
            sweeps()
            for n in range(1, count + 1):
                one_slice(n, 0)
            lv.each(corrections(starts))
            lv.each(own_nodes)
            if finish:
                lv.each(last_node)

        if start and self.slices:
            for count in range(self.slices):
                pl.when(own == count)(functools.partial(written_out, count))
            return
        if start:
            sweeps()
            lax.fori_loop(1, own + 1, one_slice, 0)
            lv.each(corrections(starts))
            lv.each(own_nodes)
        if finish:
            lv.each(last_node)


def load_planes(level, sources, columns, natural):
    count = level.lanes // 128
    matrix = group_matrix(count, False)
    slot = slots(count)
    for read, first in sources:
        blocks = []
        for k in range(count):
            values = [read(plane, k) for plane in range(4)]
            blocks.append(permuted(jnp.concatenate(values, axis=0), matrix))
        rows = blocks[0].shape[0] // 4
        for b in range(2):
            tiles = exchanged([block[:, 128 * b : 128 * b + 128] for block in blocks], slot)
            for q, tile in enumerate(tiles):
                for plane in range(4):
                    natural[plane, 2 * q + b, pl.ds(first, rows), :] = tile[plane * rows : (plane + 1) * rows]
    chunks = level.chunks
    for q in range(count):
        for p, (a, b) in enumerate(PHASES):
            for t in range(chunks):
                picked = [natural[plane, 2 * q + b, pl.ds(2 * t + a, 8, stride=2 * chunks), :] for plane in range(4)]
                lane, row = pl.ds(128 * q, 128), 8 * t
                for s in range(2):
                    level.fine[s * 4 + p, pl.ds(row, 8), lane] = picked[s]
                level.coef[p, pl.ds(row, 8), lane] = picked[2]
                level.coef[4 + p, pl.ds(row, 8), lane] = picked[2] + picked[3]


def spread(level, natural):
    count, chunks = level.lanes // 128, level.chunks
    for s in range(2):
        for q in range(count):
            for p, (a, b) in enumerate(PHASES):
                for t in range(chunks):
                    value = level.ends[s * 4 + p, pl.ds(8 * t, 8), pl.ds(128 * q, 128)]
                    natural[s, 2 * q + b, pl.ds(2 * t + a, 8, stride=2 * chunks), :] = value


def merged(level, first, rows, natural, matrix):
    count = level.lanes // 128
    slot = slots(count)
    halves = []
    for b in range(2):
        tiles = []
        for q in range(count):
            tiles.append(jnp.concatenate([natural[s, 2 * q + b, pl.ds(first, rows), :] for s in range(2)], axis=0))
        halves.append(exchanged(tiles, slot))
    blocks = [permuted(jnp.concatenate([halves[0][k], halves[1][k]], axis=1), matrix) for k in range(count)]
    return [[block[s * rows : (s + 1) * rows] for block in blocks] for s in range(2)]


def own_first(rows):
    return pl.multiple_of(lax.axis_index("gx") * rows, rows)


def source_list(refs, rows, parts):
    if parts == 2:
        mine = own_first(rows)
        state, feed, kill = refs[4:]
        other = [state.at[0], state.at[1], feed, kill]
        return [(refs[:4], mine), (other, pl.multiple_of(rows - mine, rows))]
    state, feed, kill = refs
    return [([state.at[g, 0], state.at[g, 1], feed.at[g], kill.at[g]], g * rows) for g in range(parts)]


def interior_kernel(parts, rows, columns, halo, depth, width, start, finish, *refs):
    refs = list(refs)
    take = lambda count: [refs.pop(0) for _ in range(count)]
    here = columns // 2 if parts == 2 else columns
    origin = pl.multiple_of(lax.axis_index("gx") * here, here) if parts == 2 else 0
    seam = 4 * depth if parts == 2 else 0
    side = (width - seam) // 2 - halo
    ins = take(7 if parts == 2 else 3) if start else []
    names = [] if finish and start else list(HANDED)
    handed = take(len(names)) if not start else []
    window = take(1)[0] if start else None
    outs = take(2 if parts == 2 else 1) if finish else []
    handed = handed or take(len(names))
    names += [name for name in PLANES if name not in names] if start else ["ends"]
    handed += take(len(names) - len(handed))
    (natural,) = take(1)
    level = Level(dict(zip(names, handed)), parts * rows // 2, here // 2, None)

    def reader(planes):
        return lambda plane, block: planes[plane][:, pl.ds(origin + 256 * block, 256)]

    if start:
        sources = []
        for planes, first in source_list(ins, rows, parts):
            sources.append((reader(planes), first))
            for plane in range(4):
                value = planes[plane][...]
                blank = jnp.zeros((rows, halo), F32)
                cuts = [blank, value[:, :side], value[:, (columns - seam) // 2 : (columns + seam) // 2]]
                cuts += [value[:, columns - side :], blank]
                window[plane, pl.ds(first, rows), :] = jnp.concatenate([cut for cut in cuts if cut.shape[1]], axis=1)
        load_planes(level, sources, here, natural)
    level.run(lax.axis_index("ta"), start, finish)
    if finish:
        spread(level, natural)
        matrix = group_matrix(level.lanes // 128, True)
        mine = own_first(rows)
        firsts = [mine, pl.multiple_of(rows - mine, rows)] if parts == 2 else [mine]
        for target, first in zip(outs, firsts):
            blocks = merged(level, first, rows, natural, matrix)
            for s in range(2):
                for k, block in enumerate(blocks[s]):
                    target[s, :, pl.ds(256 * k, 256)] = block


def few(count):
    return count if count <= 4 else 0


def places(halo, depth, width):
    last = -depth % 128
    return (halo, 0), (width // 2 - depth, last), (width // 2, 0), (width - halo - depth, last)


def border_kernel(parts, rows, halo, depth, width, window, near, far, out, *work):
    lanes = width // 2
    index, size = lax.axis_index("gy"), lax.axis_size("gy")
    swap = lax.rem(index, 2) == 0
    if parts == 2:
        swap = swap == (lax.axis_index("gx") == 0)
    tiles = lanes // 128
    at = lax.broadcasted_iota(jnp.int32, (1, lanes), 1)
    at = tiles * (at % 128) + at // 128
    outside = ((at < halo // 2) & (index == 0)) | ((at >= lanes - halo // 2) & (index == size - 1))
    level = Level(dict(zip(PLANES, work)), parts * rows // 2, lanes, jnp.where(outside, 0.0, 1.0), few(lax.axis_size("ta")))

    strips = []
    for edge, (a, b) in ((0, (far, near)), (size - 1, (near, far))):
        strip = jnp.where(index == edge, 0.0, jnp.where(swap, a[...], b[...]))
        strips.append(strip)

    def reader(first):
        def read(plane, block):
            low, high = (unfolded(strip, first, rows, plane, depth, parts * rows) for strip in strips)
            own = window[plane, pl.ds(first, rows), :]
            cuts = [own[:, : halo - depth], low, own[:, halo : width - halo], high, own[:, width - halo + depth :]]
            whole = jnp.concatenate([cut for cut in cuts if cut.shape[1]], axis=1)
            return whole[:, 256 * block : 256 * block + 256]

        return read

    load_planes(level, [(reader(g * rows), g * rows) for g in range(parts)], width, work[-1])
    level.run(lax.axis_index("ta"))
    spread(level, work[-1])
    if parts == 2 and tiles == 1:
        mine = own_first(rows)
        for k, (start, at) in enumerate(places(halo, depth, width)):
            source = lax.broadcasted_iota(jnp.int32, (8, 128), 1) + (start - at)
            for s in range(2):
                for row in range(0, rows, 8):
                    pair = [work[-1][s, b, pl.ds(pl.multiple_of(mine + row, 8), 8), :] for b in range(2)]
                    even, odd = (jnp.take_along_axis(x, (source >> 1) & 127, axis=1) for x in pair)
                    out[k, s, pl.ds(row, 8), :] = jnp.where((source & 1) == 0, even, odd)
        return
    natural = merged(level, own_first(rows), rows, work[-1], group_matrix(tiles, True))
    for s in range(2):
        for k, block in enumerate(natural[s]):
            out[s, :, pl.ds(256 * k, 256)] = block


def final_kernel(halo, depth, width, inner, border, out):
    total = out.shape[-1]
    out[0] = inner[...]
    for s in range(2):
        for column, source in ((0, halo), (total - depth, width - halo - depth)):
            low = column // 128 * 128
            high = round_up(column + depth, 128)
            old, new = out[0, s, :, pl.ds(low, high - low)], border[s][:, source : source + depth]
            parts_of = [old[:, : column - low], new, old[:, column + depth - low :]]
            out[0, s, :, pl.ds(low, high - low)] = jnp.concatenate([x for x in parts_of if x.shape[1]], axis=1)


def joined_kernel(halo, depth, width, keep, got, border, out, ends, middle, sems):
    total = out.shape[-1]
    half = total // 2
    tile = round_up(depth, 128)
    core = lax.axis_index("gx")
    copies = []
    for k, value in enumerate((keep, got)):
        origin = pl.multiple_of((core if k == 0 else 1 - core) * half + tile, 128)
        inside = pl.ds(tile, half - 2 * tile)
        target = out.at[0, :, :, pl.ds(origin, half - 2 * tile)]
        copies.append(pltpu.make_async_copy(value.at[:, :, inside], target, sems.at[k]))
        copies[-1].start()
    first = core == 0
    low, high = pl.ds(0, tile), pl.ds(half - tile, tile)
    starts = [start for start, _ in places(halo, depth, width)]
    lane = lax.broadcasted_iota(jnp.int32, (1, tile), 1)
    for s in range(2):
        old = [jnp.where(first, a[s, :, at], b[s, :, at]) for a, b in ((keep, got), (got, keep)) for at in (low, high)]
        if border.ndim == 4:
            targets = (ends.at[0, s], middle.at[s, :, pl.ds(0, tile)], middle.at[s, :, pl.ds(tile, tile)], ends.at[1, s])
            for k, (target, (_, at)) in enumerate(zip(targets, places(halo, depth, width))):
                target[...] = jnp.where((lane >= at) & (lane < at + depth), border[k, s], old[k])
            continue
        new = [border[s][:, at : at + depth] for at in starts]
        ends[0, s] = jnp.concatenate([new[0], old[0][:, depth:]], axis=1)
        ends[1, s] = jnp.concatenate([old[3][:, : tile - depth], new[3]], axis=1)
        middle[s] = jnp.concatenate([old[1][:, : tile - depth], new[1], new[2], old[2][:, depth:]], axis=1)
    copies.append(pltpu.make_async_copy(ends.at[0], out.at[0, :, :, pl.ds(0, tile)], sems.at[2]))
    copies.append(pltpu.make_async_copy(ends.at[1], out.at[0, :, :, pl.ds(total - tile, tile)], sems.at[3]))
    copies.append(pltpu.make_async_copy(middle, out.at[0, :, :, pl.ds(half - tile, 2 * tile)], sems.at[4]))
    for copy in copies[2:]:
        copy.start()
    for copy in copies:
        copy.wait()


def folds(rows, columns):
    tiles, spare = rows // 8, max(128 // columns - 4, 0)
    return (-(-4 * tiles // (spare + 4)), spare) if spare else (tiles, 0)


def folded(strip, columns):
    rows = strip.shape[0]
    kept, spare = folds(rows, columns)
    if not spare:
        return strip
    tail = [(row, plane) for row in range(8 * kept, rows, 8) for plane in range(4)]
    tiles = []
    for k in range(kept):
        beside = [strip[row : row + 8, p * columns : (p + 1) * columns] for row, p in tail[k * spare : (k + 1) * spare]]
        blank = jnp.zeros((8, 128 - (4 + len(beside)) * columns), F32)
        cuts = [strip[8 * k : 8 * k + 8], *beside, blank]
        tiles.append(jnp.concatenate([cut for cut in cuts if cut.shape[1]], axis=1))
    return jnp.concatenate(tiles, axis=0)


def unfolded(value, first, rows, plane, columns, total):
    kept, spare = folds(total, columns)
    tiles = []
    for row in range(first, first + rows, 8):
        at, lane = row, plane * columns
        if spare and row >= 8 * kept:
            index = (row // 8 - kept) * 4 + plane
            at, lane = index // spare * 8, (4 + index % spare) * columns
        tiles.append(value[at : at + 8, lane : lane + columns])
    return jnp.concatenate(tiles, axis=0)


def pack_kernel(parts, rows, depth, *refs):
    count = 7 if parts == 2 else 3
    ins, outs = refs[:count], refs[count:]
    even = lax.rem(lax.axis_index("gy"), 2) == 0
    sources = source_list(ins, rows, parts)
    total, tile = ins[-1].shape[-1], round_up(depth, 128)
    if parts == 2 and depth <= 32:
        first = lax.axis_index("gx") == 0
        upper = even == first
        column = pl.multiple_of(jnp.where(upper, total - tile, 0), 128)
        offset = jnp.where(upper, tile - depth, 0)
        lane = lax.broadcasted_iota(jnp.int32, (1, 128), 1)
        strip = jnp.zeros((2 * rows, 128), F32)
        for plane in range(4):
            own, other = (planes[plane][:, pl.ds(column, tile)] for planes, _ in sources)
            value = jnp.concatenate([jnp.where(first, own, other), jnp.where(first, other, own)], axis=0)
            value = pltpu.roll(value, lax.rem(plane * depth + 128 - offset, 128), 1)
            strip = jnp.where((lane >= plane * depth) & (lane < (plane + 1) * depth), value, strip)
        outs[0][...] = folded(strip[:, : 4 * depth], depth)
        return
    strips = []
    for planes, _ in sources:
        low = jnp.concatenate([ref[:, pl.ds(0, tile)][:, :depth] for ref in planes], axis=1)
        high = jnp.concatenate([ref[:, pl.ds(total - tile, tile)][:, tile - depth :] for ref in planes], axis=1)
        strips.append((jnp.where(even, high, low), jnp.where(even, low, high)))
    if parts == 2:
        first = lax.axis_index("gx") == 0
        (own_a, own_b), (other_a, other_b) = strips
        own, other = jnp.where(first, own_a, own_b), jnp.where(first, other_a, other_b)
        whole = [jnp.concatenate([jnp.where(first, own, other), jnp.where(first, other, own)], axis=0)]
    else:
        whole = [jnp.concatenate(each, axis=0) for each in zip(*strips)]
    for out, strip in zip(outs, whole):
        out[...] = folded(strip, depth)


def fetch_kernel(state, feed, kill, *refs):
    planes, sems = refs[:4], refs[4]
    sources = (state.at[0], state.at[1], feed, kill)
    copies = [pltpu.make_async_copy(sources[i], planes[i], sems.at[i]) for i in range(4)]
    for copy in copies:
        copy.start()
    for copy in copies:
        copy.wait()


def both_ways(pairs):
    return [pair for low, high in pairs for pair in ((low, high), (high, low))]


VMEM = pl.BlockSpec(memory_space=pltpu.VMEM)
ANY = pl.BlockSpec(memory_space=pl.ANY)


def arrays(shapes):
    return [jax.ShapeDtypeStruct(shape, F32) for shape in shapes]


def buffers(shapes):
    return [pltpu.VMEM(shape, F32) for shape in shapes]


def size_of(shapes):
    return sum(4 * math.prod(shape) for shape in shapes)


def called(name, kernel, outs, scratch, limit, inputs, specs=VMEM, out_specs=VMEM, flops=0):
    return pl.pallas_call(
        kernel,
        out_shape=outs,
        in_specs=[specs] * len(inputs),
        out_specs=[out_specs] * len(outs),
        scratch_shapes=scratch,
        compiler_params=pltpu.CompilerParams(vmem_limit_bytes=limit),
        cost_estimate=pl.CostEstimate(flops=flops, bytes_accessed=flops // 2, transcendentals=0),
        name=name,
    )(*inputs)


def per_device(initial_state, feed_rate, kill_rate):
    slices, parts, blocks = (lax.axis_size(axis) for axis in ("ta", "gx", "gy"))
    _, rows, columns = initial_state.shape
    depth = 2 * (2 * slices + 2)
    halo = round_up(depth, 32)
    seam = 4 * depth if parts == 2 else 0
    width = round_up(2 * halo + 4 * depth + seam, 256)
    every = parts * rows
    here = columns // 2 if parts == 2 else columns
    given = (initial_state, feed_rate, kill_rate)
    plane_bytes = 4 * every * columns

    low_pairs = both_ways([(i, i + 1) for i in range(0, blocks - 1, 2)])
    high_pairs = both_ways([(i, (i + 1) % blocks) for i in range(1, blocks - blocks % 2, 2)])

    def crossed(value):
        return lax.ppermute(value, "gx", [(0, 1), (1, 0)])

    if parts == 2:
        others = [crossed(value) for value in given]
        limit = 1709 * 2**15
        own = called("fetch", fetch_kernel, arrays([(rows, columns)] * 4), [pltpu.SemaphoreType.DMA((4,))], limit, given, ANY)
        fields = [*own, *others]
    else:
        fields = [lax.all_gather(value, "gx") for value in given]
    pack = functools.partial(pack_kernel, parts, rows, depth)
    kept, spare = folds(every, depth)
    strips = arrays([(8 * kept, 128 if spare else 4 * depth)] * (1 if parts == 2 else 2))
    sent = called("pack", pack, strips, [], 8 * plane_bytes + 2**22, fields)
    if parts == 2:
        pairs = []
        for n in range(slices):
            base = n * 2 * blocks
            inner_pairs = both_ways([(i, i + 1) for i in range(1, blocks - 1, 2)])
            pairs += [(base + source, base + target) for source, target in low_pairs]
            pairs += [(base + blocks + source, base + blocks + target) for source, target in inner_pairs]
            if n ^ 1 < slices:
                met = {0, blocks - 1} - {source for source, _ in inner_pairs}
                pairs += [(base + blocks + i, (n ^ 1) * 2 * blocks + blocks + i) for i in sorted(met)]
        near = lax.ppermute(sent[0], ("ta", "gx", "gy"), pairs)
    else:
        near = lax.ppermute(sent[0], "gy", low_pairs)
        far = lax.ppermute(sent[1], "gy", high_pairs)

    natural = natural_shape(every // 2, here // 2)
    everything = shapes_of(PLANES, every // 2, here // 2) + [natural]
    limit = size_of(everything) + 32 * every * (columns + width) + 2**22
    interior = functools.partial(interior_kernel, parts, rows, columns, halo, depth, width)
    window_shape = (4, every, width)
    result_shape = (2, rows, here)
    if parts == 2:
        first = functools.partial(interior, True, False)
        handed = shapes_of(HANDED, every // 2, here // 2)
        scratch = buffers(shapes_of([name for name in PLANES if name not in HANDED], every // 2, here // 2) + [natural])
        made = called("interior", first, arrays([window_shape] + handed), scratch, limit, fields, flops=2**24)
        near, window, *made = lax.optimization_barrier((near, *made))
        far = crossed(near)
        last = functools.partial(interior, False, True)
        scratch = buffers(shapes_of(["ends"], every // 2, here // 2) + [natural])
        keep, give = called("own", last, arrays([result_shape] * 2), scratch, limit, made, flops=2**34)
        inner = [keep, crossed(give)]
    else:
        whole = functools.partial(interior, True, True)
        shapes = [window_shape, result_shape]
        window, *inner = called("interior", whole, arrays(shapes), buffers(everything), limit, fields, flops=2**24)
    work = shapes_of(PLANES, every // 2, width // 2) + [natural_shape(every // 2, width // 2)]
    limit = size_of(work) + 32 * every * width + 2**23
    shape = (4, 2, rows, 128) if parts == 2 and width == 256 else (2, rows, width)
    border = functools.partial(border_kernel, parts, rows, halo, depth, width)
    (edges,) = called("border", border, arrays([shape]), buffers(work), limit, (window, near, far), flops=2**34)
    result = arrays([(1, 2, rows, columns)])
    if parts == 2:
        tile = round_up(depth, 128)
        scratch = buffers([(2, 2, rows, tile), (2, rows, 2 * tile)]) + [pltpu.SemaphoreType.DMA((5,))]
        final = functools.partial(joined_kernel, halo, depth, width)
        (out,) = called("final", final, result, scratch, 2**23, (*inner, edges), out_specs=ANY)
    else:
        final = functools.partial(final_kernel, halo, depth, width)
        (out,) = called("final", final, result, [], 16 * plane_bytes + 2**22, (*inner, edges))
    return out


def solution(mesh):
    placed = (P(None, "gx", "gy"), P("gx", "gy"), P("gx", "gy"))
    return jax.shard_map(
        per_device, mesh=mesh, in_specs=placed, out_specs=P("ta", None, "gx", "gy"), check_vma=False
    )
```
